32 devices in a mesh: dp: 16 (over z, y, core), mp: 2 (over x).
Axes of the slice: x: 2, y: 2, z: 4, core: 2. Of those that a mesh axis runs over, the one named last changes fastest.
Arguments:
- token_ids: int32 [16384], P('dp'), may hold values from 0 to 31999
- segment_ids: int32 [16, 1024], P('dp'), may hold values from 0 to 3, never falling along the last dimension, each value on 1 to 512 neighbouring positions
- time_index: int32 [16], P('dp'), may hold values from 0 to 15
- noise_vec: bfloat16 [16384, 256], P('dp'), may hold values from -6 to 6
- embed_table: bfloat16 [32000, 256], P('mp'), may hold values from -6 to 6
- w_in: bfloat16 [256, 1024], replicated, may hold values from -0.375 to 0.375
- norm1_gain: bfloat16 [1024], replicated, may hold values from 0.5 to 1.5
- norm1_bias: bfloat16 [1024], replicated, may hold values from -1.5 to 1.5
- w_query: bfloat16 [1024, 1024], P(None, 'mp'), may hold values from -0.1875 to 0.1875
- w_key: bfloat16 [1024, 1024], P(None, 'mp'), may hold values from -0.1875 to 0.1875
- w_value: bfloat16 [1024, 1024], P(None, 'mp'), may hold values from -0.1875 to 0.1875
- w_out: bfloat16 [1024, 1024], P('mp'), may hold values from -1.5 to 1.5
- norm2_gain: bfloat16 [1024], replicated, may hold values from 0.5 to 1.5
- norm2_bias: bfloat16 [1024], replicated, may hold values from -1.5 to 1.5
- w_up: bfloat16 [1024, 4096], P(None, 'mp'), may hold values from -0.1875 to 0.1875
- bias_up: bfloat16 [4096], P('mp'), may hold values from -2.5 to 2.5
- w_down: bfloat16 [4096, 1024], P('mp'), may hold values from -0.09375 to 0.09375
- bias_down: bfloat16 [1024], replicated, may hold values from -1.5 to 1.5
- cotangent: bfloat16 [16384, 1024], P('dp'), may hold values from -6 to 6
Outputs:
- layer_out: bfloat16 [16384, 1024], P('dp')
- noise_grad: float32 [16384, 256], P('dp')
- table_grad: float32 [32000, 256], P(('mp', 'dp'))
- w_in_grad: float32 [256, 1024], P('dp')
- norm1_gain_grad: float32 [1024], P('dp')
- norm1_bias_grad: float32 [1024], P('dp')
- w_query_grad: float32 [1024, 1024], P('dp', 'mp')
- w_key_grad: float32 [1024, 1024], P('dp', 'mp')
- w_value_grad: float32 [1024, 1024], P('dp', 'mp')
- w_out_grad: float32 [1024, 1024], P(('mp', 'dp'))
- norm2_gain_grad: float32 [1024], P('dp')
- norm2_bias_grad: float32 [1024], P('dp')
- w_up_grad: float32 [1024, 4096], P('dp', 'mp')
- bias_up_grad: float32 [4096], P(('mp', 'dp'))
- w_down_grad: float32 [4096, 1024], P(('mp', 'dp'))
- bias_down_grad: float32 [1024], P('dp')
The draws below stay inside these ranges and needn't reach their ends.
Inputs may be any that keep to these rules, and one draw needn't show every extreme that they name: `segment_ids`: along each row of 1024 tokens the numbers never fall, so that each document is one run of positions.
All inputs are finite; a program needn't handle non-finite values.
Results may differ from the reference program's by a relative error of at most 0.015.
Values may be sent and summed in bfloat16 or wider, within the bound.
A program may use at most 192 MiB of HBM per device.

```python
import math
import jax
import jax.numpy as jnp
import numpy as np
from jax import lax

D = 1024
HEADS = 16
HEAD_DIM = 64
FF = 4096
E = 256
V = 32000
LEN = 1024
DOCS = 4
TLEVELS = 16
ROWS = 16
TOKENS = 16384


def place_ends(entries, stream_key, least, high):
    extent = entries.shape
    place = [jax.random.randint(jax.random.fold_in(stream_key, axis), (), 0, extent[axis]) for axis in range(len(extent))]
    entries = entries.at[tuple(place)].set(least)
    longest = extent.index(max(extent))
    place[longest] = (place[longest] + 1) % extent[longest]
    return entries.at[tuple(place)].set(high)


def steps_of(own_key, dims, cuts, smallest, top_value):
    def one(axis_at, blocks):
        draws = jax.random.uniform(jax.random.fold_in(jax.random.fold_in(own_key, 6), axis_at), (blocks,), jnp.float32, smallest / len(cuts), top_value / len(cuts))
        return jnp.repeat(jnp.exp(draws), dims[axis_at] // blocks).reshape((-1,) + (1,) * (len(dims) - axis_at - 1))

    loudness = one(*cuts[0])
    for cut in cuts[1:]:
        loudness = loudness * one(*cut)
    return loudness


def cumulative_ranks(number_of, slope):
    loads = [(1 << 20) // math.isqrt(rank ** slope) + 1 for rank in range(1, number_of + 1)]
    deviation = 1 + sum(loads) // (1 << 30)
    return np.cumsum(np.array([max(1, weight // deviation) for weight in loads]))


def skewed_ids(key, dims, number_of, skew):
    table = cumulative_ranks(number_of, skew)
    pick = jax.random.randint(jax.random.fold_in(key, 1), dims, 0, int(table[number_of - 1]))
    grade = jnp.searchsorted(jnp.asarray(table, jnp.int32), pick, side="right")
    return jax.random.permutation(jax.random.fold_in(key, 2), number_of)[grade].astype(jnp.int32)


def length_profile(count, total, limit, lean):
    weights = [(1 << 20) // math.isqrt(rank ** lean) + 1 for rank in range(2, count + 1)]
    surplus, counts = total - limit - (count - 1), [1] * (count - 1)
    while surplus > 0:
        candidates = [i for i in range(count - 1) if counts[i] < limit]
        mass, left = sum([weights[i] for i in candidates]), surplus
        for i in candidates:
            addition = min(limit - counts[i], max(1, left * weights[i] // mass), surplus)
            counts[i] = counts[i] + addition
            surplus = surplus - addition
    return np.array([limit] + counts)


def ragged(stream_key, count, total, limit, slope):
    if count == 2:
        one = jax.random.randint(stream_key, (), max(1, total - limit), min(limit, total - 1) + 1)
        return jnp.stack([one, total - one])
    tallies = jnp.asarray(length_profile(count, total, limit, slope), jnp.int32)
    pairs = (count - 1) // 2
    donor, receiver = tallies[1:1 + 2 * pairs:2], tallies[2:2 + 2 * pairs:2]
    room = jnp.minimum(donor - 1, limit - receiver)
    passed = jax.random.randint(jax.random.fold_in(stream_key, 1), (pairs,), 0, 1 << 20) % (room + 1)
    tallies = tallies.at[1:1 + 2 * pairs:2].set(donor - passed).at[2:2 + 2 * pairs:2].set(receiver + passed)
    return tallies[jax.random.permutation(jax.random.fold_in(stream_key, 2), count)]


def scatter_about(stream_key, extent, scale, reach, split=(), held_as=jnp.bfloat16):
    loudness = steps_of(stream_key, extent, split, -0.22, 0.18) if split else 1.0
    values = jax.random.normal(stream_key, extent, jnp.float32) * scale * loudness
    return jnp.minimum(jnp.maximum(values, -reach), reach).astype(held_as)


def setup_inputs(seed: int = 0) -> dict:
    seeds = jax.random.split(jax.random.key(seed), 20)
    token_ids = place_ends(skewed_ids(seeds[0], (TOKENS,), V, 2), jax.random.fold_in(seeds[0], 3), 0, V - 1).astype(jnp.int32)
    segment_ids = jax.vmap(lambda own: jnp.searchsorted(jnp.cumsum(ragged(own, DOCS, LEN, LEN // 2, 1)), jnp.arange(LEN), side="right"))(jax.random.split(seeds[1], ROWS)).reshape((ROWS, LEN)).astype(jnp.int32)
    time_index = place_ends(jax.random.randint(seeds[2], (ROWS,), 0, TLEVELS), jax.random.fold_in(seeds[2], 1), 0, TLEVELS - 1).astype(jnp.int32)
    noise_vec = scatter_about(seeds[3], (TOKENS, E), 1.0, 6.0, ((0, 16),))
    embed_table = scatter_about(seeds[4], (V, E), 1.0, 6.0, ((0, 2),))
    w_in = scatter_about(seeds[5], (E, D), E ** -0.5, 0.375)
    norm1_gain = jnp.clip(1.0 + 0.1 * jax.random.normal(seeds[6], (D,), jnp.float32), 0.5, 1.5).astype(jnp.bfloat16)
    norm1_bias = scatter_about(seeds[7], (D,), 0.3, 1.5)
    w_query = scatter_about(seeds[8], (D, D), D ** -0.5, 0.1875, ((1, 2),))
    w_key = scatter_about(seeds[9], (D, D), D ** -0.5, 0.1875, ((1, 2),))
    w_value = scatter_about(seeds[10], (D, D), D ** -0.5, 0.1875, ((1, 2),))
    w_out = scatter_about(seeds[11], (D, D), (D // 64) ** -0.5, 1.5, ((0, 2),))
    norm2_gain = jnp.clip(1.0 + 0.1 * jax.random.normal(seeds[12], (D,), jnp.float32), 0.5, 1.5).astype(jnp.bfloat16)
    norm2_bias = scatter_about(seeds[13], (D,), 0.3, 1.5)
    w_up = scatter_about(seeds[14], (D, FF), D ** -0.5, 0.1875, ((1, 2),))
    bias_up = scatter_about(seeds[15], (FF,), 0.5, 2.5, ((0, 2),))
    w_down = scatter_about(seeds[16], (FF, D), FF ** -0.5, 0.09375, ((0, 2),))
    bias_down = scatter_about(seeds[17], (D,), 0.3, 1.5)
    cotangent = scatter_about(seeds[18], (TOKENS, D), 1.0, 6.0, ((0, 16),))
    return {"token_ids": token_ids, "segment_ids": segment_ids, "time_index": time_index, "noise_vec": noise_vec, "embed_table": embed_table, "w_in": w_in, "norm1_gain": norm1_gain, "norm1_bias": norm1_bias, "w_query": w_query, "w_key": w_key, "w_value": w_value, "w_out": w_out, "norm2_gain": norm2_gain, "norm2_bias": norm2_bias, "w_up": w_up, "bias_up": bias_up, "w_down": w_down, "bias_down": bias_down, "cotangent": cotangent}


@jax.custom_vjp
def low(v):
    return lax.optimization_barrier(v.astype(jnp.bfloat16)).astype(jnp.float32)

@jax.custom_vjp
def low_back(v):
    return v

def low_keep(v):
    return (low(v), None)

def low_pass(kept, grad):
    return (grad,)

def back_keep(v):
    return (v, None)

def back_low(kept, grad):
    return (low(grad),)
low.defvjp(low_keep, low_pass)
low_back.defvjp(back_keep, back_low)
time_low = 0.5
time_high = 10.0
norm_eps = 1e-05
table_eps = 1e-06
masked_score = -1e+30
highest = lax.Precision.HIGHEST

def to_float(value):
    return value.astype(jnp.float32)

def layer_norm(values, gain, bias):
    centred = values - lax.optimization_barrier(jnp.mean(values, axis=-1, keepdims=True))
    spread = lax.optimization_barrier(jnp.mean(centred * centred, axis=-1, keepdims=True))
    return centred * lax.rsqrt(spread + norm_eps) * gain + bias

def attend(pieces):
    query_seq, key_seq, value_seq, seg_seq = pieces
    score_scale = HEAD_DIM ** (-0.5)
    scores = low_back(jnp.einsum('qhd,khd->hqk', query_seq, key_seq, precision=highest) * score_scale)
    allowed = (seg_seq[:, None] == seg_seq[None, :])[None]
    scores = jnp.where(allowed, scores, masked_score)
    weights = jax.nn.softmax(scores, axis=-1)
    return jnp.einsum('hqk,khd->qhd', low(weights), value_seq, precision=highest)

def reference(token_ids, segment_ids, time_index, noise_vec, embed_table, w_in, norm1_gain, norm1_bias, w_query, w_key, w_value, w_out, norm2_gain, norm2_bias, w_up, bias_up, w_down, bias_down, cotangent):
    level_step = jnp.log(time_high / time_low) / (TLEVELS - 1)
    level = jnp.repeat(time_low * jnp.exp(time_index.astype(jnp.float32) * level_step), LEN)[:, None]
    c_in = lax.rsqrt(1.0 + level * level)
    params = jax.tree.map(to_float, (noise_vec, embed_table, w_in, norm1_gain, norm1_bias, w_query, w_key, w_value, w_out, norm2_gain, norm2_bias, w_up, bias_up, w_down, bias_down))

    def forward(noise_in, table_in, proj_in, gain_one, bias_one, query_w, key_w, value_w, out_w, gain_two, bias_two, up_w, up_bias, down_w, down_bias):
        scaled_table = low(table_in * lax.rsqrt(lax.optimization_barrier(jnp.mean(table_in * table_in, axis=1, keepdims=True)) + table_eps))
        embedded = low_back(scaled_table[token_ids])
        inputs = c_in * (embedded + level * noise_in)
        stream = low_back(jnp.dot(low(inputs), proj_in, precision=highest))
        normed_one = low(layer_norm(stream, gain_one, bias_one))

        def heads(weight):
            return low_back(low(jnp.dot(normed_one, weight, precision=highest))).reshape(ROWS, LEN, HEADS, HEAD_DIM)
        mixed = lax.map(jax.checkpoint(attend), (heads(query_w), heads(key_w), heads(value_w), segment_ids))
        mixed_low = low_back(low(mixed.reshape(TOKENS, D)))
        hidden = stream + low_back(jnp.dot(mixed_low, out_w, precision=highest))
        normed_two = low(layer_norm(hidden, gain_two, bias_two))
        upward = low_back(jnp.dot(normed_two, up_w, precision=highest) + up_bias)
        activated = low(jax.nn.gelu(upward))
        return hidden + low_back(jnp.dot(activated, down_w, precision=highest)) + down_bias
    result, pullback = jax.vjp(forward, *params)
    grads = pullback(cotangent.astype(jnp.float32))
    return (result.astype(jnp.bfloat16), grads[0], grads[1], grads[2], grads[3], grads[4], grads[5], grads[6], grads[7], grads[8], grads[9], grads[10], grads[11], grads[12], grads[13], grads[14])
```

```python
import functools

import jax
import jax.numpy as jnp
from jax import lax
from jax.experimental import pallas as pl
from jax.experimental.pallas import tpu as pltpu
from jax.sharding import PartitionSpec as P

HEAD_DIM = 64
TLEVELS = 16
DOCS = 4
MAX_RUN = 512

time_low = 0.5
time_high = 10.0
norm_eps = 1e-05
table_eps = 1e-06
masked_score = -1e30

BF = jnp.bfloat16
F32 = jnp.float32
VMEM_LIMIT = 56 * 1024 * 1024
BLOCK = 256
LANES = 128


def to_bf16(value):
    return value.astype(BF)


def product(left, right):
    return jnp.dot(left, right, preferred_element_type=F32)


def contract_rows(left, right):
    return lax.dot_general(left, right, (((0,), (0,)), ((), ())), preferred_element_type=F32)


def times_back(left, right):
    return lax.dot_general(left, right, (((1,), (1,)), ((), ())), preferred_element_type=F32)


def params(limit=VMEM_LIMIT):
    return pltpu.CompilerParams(vmem_limit_bytes=limit)


def cost(flops, nbytes, trans=0):
    return pl.CostEstimate(flops=int(flops), bytes_accessed=int(nbytes), transcendentals=int(trans))


def full_spec():
    return pl.BlockSpec(memory_space=pltpu.VMEM)


def row_scale(table_rows):
    return lax.rsqrt(jnp.mean(table_rows * table_rows, axis=1, keepdims=True) + table_eps)


def normalize(values, gain, bias):
    centred = values - jnp.mean(values, axis=-1, keepdims=True)
    inverse = lax.rsqrt(jnp.mean(centred * centred, axis=-1, keepdims=True) + norm_eps)
    unit_rows = centred * inverse
    return (unit_rows * gain + bias, unit_rows, inverse)


def norm_back(grad, unit_rows, inverse, gain):
    scaled = grad * gain
    spread = (
        scaled
        - jnp.mean(scaled, axis=-1, keepdims=True)
        - unit_rows * jnp.mean(scaled * unit_rows, axis=-1, keepdims=True)
    )
    return (inverse * spread, jnp.sum(grad * unit_rows, axis=0), jnp.sum(grad, axis=0))


def gather_kernel(parts, ids, table, out, staged, wide, picked, sems):
    rows, width = table.shape
    tokens = picked.shape[0]
    step = rows // parts

    def copy(part):
        span = pl.ds(part * step, step)
        return pltpu.make_async_copy(table.at[span], staged.at[span], sems.at[part])

    for part in range(parts):
        copy(part).start()
    wide[pl.ds(rows, 8), :] = jnp.zeros((8, width), F32)
    for part in range(parts):
        copy(part).wait()
        piece = step // 5

        @pl.loop(0, 5)
        def _(at):
            span = pl.ds(pl.multiple_of(part * step + at * piece, 16), piece)
            wide[span, :] = staged[span, :].astype(F32)

    def one(at, carry):
        row = ids[at]
        inside = jnp.logical_and(row >= 0, row < rows)
        picked[pl.ds(at, 1), :] = wide[pl.ds(jnp.where(inside, row, rows), 1), :]
        return carry

    lax.fori_loop(0, tokens, one, 0, unroll=8)
    found = picked[...]
    out[...] = (found * row_scale(found)).astype(BF)


def gather_rows(local_ids, table):
    rows, width = table.shape
    tokens = local_ids.shape[0]
    parts = 5
    return pl.pallas_call(
        functools.partial(gather_kernel, parts),
        grid_spec=pltpu.PrefetchScalarGridSpec(
            num_scalar_prefetch=1,
            grid=(1,),
            in_specs=[pl.BlockSpec(memory_space=pl.ANY)],
            out_specs=pl.BlockSpec((tokens, width), lambda i, ids: (0, 0)),
            scratch_shapes=[
                pltpu.VMEM((rows, width), BF),
                pltpu.VMEM((rows + 8, width), F32),
                pltpu.VMEM((tokens, width), F32),
                pltpu.SemaphoreType.DMA((parts,)),
            ],
        ),
        out_shape=jax.ShapeDtypeStruct((tokens, width), BF),
        compiler_params=params(),
        cost_estimate=cost(0, rows * width * 2),
        name="embed_rows",
    )(local_ids, table)


def head_lanes(rows, head):
    lane = lax.broadcasted_iota(jnp.int32, (rows, LANES), 1)
    return (lane // HEAD_DIM) == head


def fill_queries(q_ref, fq_ref, joined):
    length = q_ref.shape[0]
    scaled = (q_ref[...].astype(F32) * (HEAD_DIM**-0.5)).astype(BF)
    for head in range(2):
        joined[head, :, :LANES] = jnp.where(head_lanes(length, head), scaled, jnp.zeros_like(scaled))
        joined[head, :, LANES:] = fq_ref[...]


def near(block, count):
    reach = MAX_RUN // BLOCK
    return max(0, block - reach) * BLOCK, min(count, block + reach + 1) * BLOCK


def attn_bwd_kernel(
    q_ref, k_ref, v_ref, g_ref, o_ref, lse_ref, fq_ref, fk_ref, dq_ref, dk_ref, dv_ref,
    qs, ks, kt, gs, delta, probs, slopes,
):
    length = q_ref.shape[0]
    count = length // BLOCK
    fill_queries(q_ref, fq_ref, qs)
    ks[:, :LANES] = k_ref[...]
    ks[:, LANES:] = fk_ref[...]
    kt[...] = k_ref[...].T
    grad = g_ref[...]
    for head in range(2):
        gs[head] = jnp.where(head_lanes(length, head), grad, jnp.zeros_like(grad))
    both = (grad.astype(F32) * o_ref[...].astype(F32)).T
    for head in range(2):
        delta[head : head + 1, :] = jnp.sum(
            both[head * HEAD_DIM : (head + 1) * HEAD_DIM], axis=0, keepdims=True
        )
    for block in range(count):
        here = slice(block * BLOCK, (block + 1) * BLOCK)
        low, high = near(block, count)
        dq = []
        for head in range(2):
            scores = times_back(ks[low:high, :], qs[head, here, :])
            weights = jnp.exp(scores - lse_ref[0, head : head + 1, here])
            weight_grad = times_back(v_ref[low:high, :], gs[head, here, :])
            score_grad = (weights * (weight_grad - delta[head : head + 1, here])).astype(BF)
            probs[head, low:high, here] = weights.astype(BF)
            slopes[head, low:high, here] = score_grad
            dq.append(product(kt[head * HEAD_DIM : (head + 1) * HEAD_DIM, low:high], score_grad))
        dq_ref[here, :] = (jnp.concatenate(dq, axis=0).T * (HEAD_DIM**-0.5)).astype(BF)
    for block in range(count):
        here = slice(block * BLOCK, (block + 1) * BLOCK)
        low, high = near(block, count)
        dk = jnp.zeros((BLOCK, LANES), F32)
        dv = jnp.zeros((BLOCK, LANES), F32)
        for head in range(2):
            dv = dv + product(probs[head, here, low:high], gs[head, low:high, :])
            dk = dk + product(slopes[head, here, low:high], qs[head, low:high, :LANES])
        dk_ref[here, :] = dk.astype(BF)
        dv_ref[here, :] = dv.astype(BF)


def attention_backward(queries, keys, values, grads, mixed, lse, fq, fk):
    seqs, length = fq.shape[0], fq.shape[1]
    pairs = queries.shape[1] // LANES
    column = pl.BlockSpec((length, LANES), lambda s, p: (s, p))
    mask = pl.BlockSpec((None, length, LANES), lambda s, p: (s, 0, 0))
    shape = jax.ShapeDtypeStruct(queries.shape, BF)
    return pl.pallas_call(
        attn_bwd_kernel,
        grid=(seqs, pairs),
        in_specs=[column] * 5
        + [pl.BlockSpec((1, 2, length), lambda s, p: (p, 0, s)), mask, mask],
        out_specs=[column] * 3,
        scratch_shapes=[
            pltpu.VMEM((2, length, 2 * LANES), BF),
            pltpu.VMEM((length, 2 * LANES), BF),
            pltpu.VMEM((LANES, length), BF),
            pltpu.VMEM((2, length, LANES), BF),
            pltpu.VMEM((2, length), F32),
            pltpu.VMEM((2, length, length), BF),
            pltpu.VMEM((2, length, length), BF),
        ],
        out_shape=[shape] * 3,
        compiler_params=params(),
        cost_estimate=cost(pairs * 8e9, 4e6 * pairs, pairs * 1e6),
        name="attention_backward",
    )(queries, keys, values, grads, mixed, lse, fq, fk)


def attention_masks(segment_ids):
    seqs, length = segment_ids.shape
    lane = lax.broadcasted_iota(jnp.int32, (1, 1, LANES), 2)
    same = segment_ids[:, :, None] == lane
    fk = jnp.where(same, 1.0, 0.0).astype(BF)
    fq = jnp.where(jnp.logical_or(same, lane >= DOCS), 0.0, masked_score).astype(BF)
    return fq, fk


gelu_slope = 0.7978845608028654
gelu_cubic = 0.044715


MESH = pl.DeviceIdType.MESH


class Place:
    def __init__(self):
        self.dp = lax.axis_index("dp")
        self.side = lax.axis_index("mp")
        self.outers = lax.axis_size("dp") // 4
        self.outer = self.dp // 4
        self.mid = (self.dp // 2) % 2
        self.core = self.dp % 2

    def other_core(self):
        return (self.dp + 1 - 2 * self.core, self.side)

    def other_mid(self):
        return (self.dp + 2 - 4 * self.mid, self.side)

    def other_side(self):
        return (self.dp, 1 - self.side)

    def at_outer(self, outer):
        return (outer * 4 + self.mid * 2 + self.core, self.side)

    def turn(self, step):
        return lax.rem(self.outer + 1 + step, self.outers)


def greet(place, with_side):
    barrier = pltpu.get_barrier_semaphore()
    peers = [place.other_core(), place.other_mid()]
    if with_side:
        peers.append(place.other_side())
    for peer in peers:
        pl.semaphore_signal(barrier, inc=1, device_id=peer, device_id_type=MESH)
    for step in range(place.outers - 1):
        pl.semaphore_signal(
            barrier, inc=1, device_id=place.at_outer(place.turn(step)), device_id_type=MESH
        )
    pl.semaphore_wait(barrier, len(peers) + place.outers - 1)


def remote(src, dst, send, recv, device):
    return pltpu.make_async_remote_copy(
        src_ref=src, dst_ref=dst, send_sem=send, recv_sem=recv, device_id=device, device_id_type=MESH
    )


def add_into(dst, left, right):
    dst[...] = (left[...].astype(F32) + right[...].astype(F32)).astype(dst.dtype)


class Scatter:
    def __init__(self, place, sources, one, two, three, sems):
        self.place, self.sources = place, sources
        self.one, self.two, self.three = one, two, three
        self.sems = sems
        self.items = range(len(sources))

    def core_copy(self, step, item):
        p = self.place
        turn = p.turn(step)
        return remote(
            self.sources[item].at[turn, :, 1 - p.core],
            self.one[item].at[turn],
            self.sems[0].at[step, item],
            self.sems[1].at[step, item],
            p.other_core(),
        )

    def mid_copy(self, step, item):
        p = self.place
        turn = p.turn(step)
        return remote(
            self.one[item].at[turn, 1 - p.mid],
            self.two[item].at[turn],
            self.sems[2].at[step, item],
            self.sems[3].at[step, item],
            p.other_mid(),
        )

    def outer_copy(self, step, item):
        p = self.place
        turn = p.turn(step)
        return remote(
            self.two[item].at[turn],
            self.three[item].at[p.outer],
            self.sems[4].at[step, item],
            self.sems[5].at[p.outer, item],
            p.at_outer(turn),
        )

    def arrival(self, step, item):
        p = self.place
        turn = p.turn(step)
        return remote(
            self.two[item].at[turn],
            self.three[item].at[turn],
            self.sems[4].at[step, item],
            self.sems[5].at[turn, item],
            p.at_outer(turn),
        )

    def start_core(self, step):
        for item in self.items:
            self.core_copy(step, item).start()

    def core_to_mid(self, step):
        p = self.place
        turn = p.turn(step)
        for item in self.items:
            self.core_copy(step, item).wait_recv()
            one = self.one[item]
            for mid in range(2):
                add_into(one.at[turn, mid], one.at[turn, mid], self.sources[item].at[turn, mid, p.core])
            self.mid_copy(step, item).start()

    def mid_to_outer(self, step, last):
        p = self.place
        turn = p.turn(step)
        for item in self.items:
            self.mid_copy(step, item).wait_recv()
            two = self.two[item]
            add_into(two.at[turn], two.at[turn], self.one[item].at[turn, p.mid])
            if not last:
                self.outer_copy(step, item).start()

    def finish(self, outs):
        p = self.place
        for item in self.items:
            total = self.two[item][p.outer].astype(F32)
            for step in range(p.outers - 1):
                self.arrival(step, item).wait_recv()
                total = total + self.three[item][p.turn(step)].astype(F32)
            outs[item][...] = total

    def drain(self):
        def one(step, carry):
            for item in self.items:
                self.core_copy(step, item).wait_send()
                self.mid_copy(step, item).wait_send()
            return carry

        lax.fori_loop(0, self.place.outers, one, 0)
        for step in range(self.place.outers - 1):
            for item in self.items:
                self.outer_copy(step, item).wait_send()


def scatter_shapes(sources):
    one = [pltpu.VMEM((s.shape[0], 2) + s.shape[3:], s.dtype) for s in sources]
    two = [pltpu.VMEM((s.shape[0],) + s.shape[3:], s.dtype) for s in sources]
    three = [pltpu.VMEM((s.shape[0],) + s.shape[3:], s.dtype) for s in sources]
    sems = [pltpu.SemaphoreType.DMA((sources[0].shape[0], len(sources))) for _ in range(6)]
    return one + two + three + sems


def owner_blocks(value, dp_size):
    rows, columns = value.shape
    if (rows // dp_size) % 16:
        rows, columns = rows * columns // LANES, LANES
        value = value.reshape(rows, columns)
    return value.reshape(dp_size // 4, 2, 2, rows // dp_size, columns)


class IdGather:
    def __init__(self, place, every, sems):
        self.place, self.every, self.sems = place, every, sems

    def copy(self, stage, step, theirs=0):
        p = self.place
        turn = lax.rem(p.outer + step, p.outers)
        if stage == 0:
            at = turn if theirs else p.outer
            part, peer, mark = self.every.at[at, p.mid, p.core], p.at_outer(turn), at
        elif stage == 1:
            mid = 1 - p.mid if theirs else p.mid
            part, peer, mark = self.every.at[turn, mid, p.core], p.other_mid(), step
        else:
            core = 1 - p.core if theirs else p.core
            part, peer, mark = self.every.at[turn, :, core], p.other_core(), step
        return remote(part, part, self.sems[2 * stage].at[step], self.sems[2 * stage + 1].at[mark], peer)


class Swap:
    def __init__(self, place, src, dst, send, recv):
        self.place, self.src, self.dst, self.send, self.recv = place, src, dst, send, recv

    def copy(self, at, src_rows, dst_rows):
        return remote(
            self.src.at[src_rows], self.dst.at[dst_rows], self.send.at[at], self.recv.at[at], self.place.other_side()
        )


def rows_from(start, size):
    return pl.ds(pl.multiple_of(start, size), size)


def feed_forward_kernel(
    ids, x, cot, wu, bu, wd, hidden, gain, wo, mixed, bd,
    every, layer, hg, hgrad, norm_sums, mg, wo_part, dwd_out, dwu_out, alone_out,
    act_t, ug, xt, xg, rg, dbu, dbd, src_d, src_u, src_a, *rest,
):
    scatter_refs, rest = rest[:15], rest[15:]
    id_sems, (send_x, recv_x, send_h, recv_h, send_d, recv_d, send_l, recv_l) = rest[:6], rest[6:]
    tokens, width = x.shape
    features = wu.shape[1]
    half = tokens // 2
    chunk, part, piece = 256, 512, 128
    place = Place()
    outers = place.outers
    work = Scatter(
        place, [src_d, src_u, src_a], scatter_refs[0:3], scatter_refs[3:6], scatter_refs[6:9], scatter_refs[9:]
    )
    known = IdGather(place, every, id_sems)
    every[place.outer, place.mid, place.core] = ids[...]
    mine_at, other_at = place.side * half, (1 - place.side) * half
    grads = Swap(place, xg, rg, send_x, recv_x)
    shares = Swap(place, hg, hg, send_h, recv_h)
    downs = Swap(place, xg, rg, send_d, recv_d)
    layers = Swap(place, layer, layer, send_l, recv_l)
    dbu[...] = jnp.zeros_like(dbu)
    dbd[...] = jnp.zeros_like(dbd)
    src_a[...] = jnp.zeros_like(src_a)
    norm_sums[...] = jnp.zeros_like(norm_sums)
    greet(place, True)

    def loop(low, high, stage):
        lax.fori_loop(low, high, lambda step, carry: (stage(step), carry)[1], 0)

    def ids_mid(step):
        known.copy(0, step, 1).wait_recv()
        known.copy(1, step).start()

    def ids_core(step):
        known.copy(1, step, 1).wait_recv()
        known.copy(2, step).start()

    loop(1, outers, lambda step: known.copy(0, step).start())
    known.copy(1, 0).start()

    def forward(start):
        rows = rows_from(start, chunk)
        xc = x[rows, :]
        gc = cot[rows, :]
        xt[:, rows] = xc.T
        dbd[...] += jnp.sum(gc.astype(F32), axis=0, keepdims=True)
        total = jnp.zeros((chunk, width), F32)
        for at in range(features // part):
            cols = slice(at * part, (at + 1) * part)
            up = product(xc, wu[:, cols]) + bu[:, cols]
            square = up * up
            gate = 0.5 + 0.5 * jnp.tanh(up * (gelu_slope + (gelu_slope * gelu_cubic) * square))
            value = up * gate
            act_t[cols, rows] = value.astype(BF).T
            slope = gate + value * (1.0 - gate) * (
                2.0 * gelu_slope + (6.0 * gelu_slope * gelu_cubic) * square
            )
            low = (times_back(gc, wd[cols, :]) * slope).astype(BF)
            ug[rows, cols] = low
            dbu[:, cols] += jnp.sum(low.astype(F32), axis=0, keepdims=True)
            total = total + times_back(low, wu[:, cols])
        xg[rows, :] = total.astype(BF)

    def sent(at):
        return grads.copy(at, rows_from(other_at + at * chunk, chunk), rows_from(at * chunk, chunk))

    def theirs(at):
        forward(other_at + at * chunk)
        sent(at).start()

    loop(0, half // chunk, theirs)
    loop(0, half // chunk, lambda at: forward(mine_at + at * chunk))
    loop(1, outers, ids_mid)
    dp_size = 4 * outers
    up_lanes, down_lanes = features // dp_size, width // dp_size
    for at in range(dp_size):
        spot = (at // 4, (at // 2) % 2, at % 2)
        src_a[spot + (slice(0, 1), slice(0, up_lanes))] = dbu[:, at * up_lanes : (at + 1) * up_lanes]
        src_a[spot + (slice(1, 2), slice(0, down_lanes))] = dbd[:, at * down_lanes : (at + 1) * down_lanes]

    down_rows, up_rows = features // outers // 2, width // outers

    def weight_grads(step):
        turn = place.turn(step)
        for mid in range(2):
            rows = rows_from(turn * (2 * down_rows) + mid * down_rows, down_rows)
            src_d[turn, mid] = product(act_t[rows, :], cot[...]).astype(BF).reshape(2, down_rows // 2, width)
        rows = rows_from(turn * up_rows, up_rows)
        for at in range(features // part):
            cols = slice(at * part, (at + 1) * part)
            src_u[turn, :, :, :, cols] = (
                product(xt[rows, :], ug[:, cols]).astype(BF).reshape(2, 2, up_rows // 4, part)
            )
        work.start_core(step)

    def norm_grads(at):
        @pl.when(at % (chunk // piece) == 0)
        def _():
            sent(at // (chunk // piece)).wait_recv()

        here = rows_from(at * piece, piece)
        rows = rows_from(mine_at + at * piece, piece)
        grad = xg[rows, :].astype(F32) + rg[here, :].astype(F32)
        _, unit, inverse = normalize(hidden[here, :], 1.0, 0.0)
        back, gain_sum, bias_sum = norm_back(grad, unit, inverse, gain[...])
        norm_sums[0:1, :] += gain_sum[None, :]
        norm_sums[1:2, :] += bias_sum[None, :]
        total = cot[rows, :].astype(F32) + back
        hgrad[here, :] = total
        hg[rows, :] = total.astype(BF)
        shares.copy(at, rows, rows).start()

    weight_grads(0)
    weight_grads(1)
    work.core_to_mid(0)
    loop(0, half // piece, norm_grads)

    def more(step):
        weight_grads(step)
        work.core_to_mid(step - 1)

    loop(2, outers, more)
    work.core_to_mid(outers - 1)
    loop(0, outers, ids_core)

    def downward(at):
        rows = rows_from(at * chunk, chunk)
        xg[rows, :] = contract_rows(act_t[:, rows], wd[...]).astype(BF)

    work.mid_to_outer(0, False)
    loop(0, half // chunk, lambda at: sent(at).wait_send())
    loop(0, tokens // chunk, downward)
    loop(1, outers - 1, lambda step: work.mid_to_outer(step, False))

    def share_from(at):
        rows = rows_from(other_at + at * piece, piece)
        return shares.copy(at, rows, rows)

    loop(0, half // piece, lambda at: share_from(at).wait_recv())

    def down_sent(at):
        return downs.copy(at, rows_from(other_at + at * piece, piece), rows_from(at * piece, piece))

    loop(0, half // piece, lambda at: down_sent(at).start())

    def mixed_grads(at):
        rows = rows_from(at * chunk, chunk)
        mg[rows, :] = times_back(hg[rows, :], wo[...]).astype(BF)

    loop(0, tokens // chunk, mixed_grads)
    wo_part[...] = contract_rows(mixed[...], hg[...]).astype(BF)

    def layer_copy(at, start):
        rows = rows_from(start + at * piece, piece)
        return layers.copy(at, rows, rows)

    def layer_rows(at):
        down_sent(at).wait_recv()
        here = rows_from(at * piece, piece)
        rows = rows_from(mine_at + at * piece, piece)
        layer[rows, :] = (
            hidden[here, :] + (xg[rows, :].astype(F32) + rg[here, :].astype(F32)) + bd[...]
        ).astype(BF)
        layer_copy(at, mine_at).start()

    loop(0, half // piece, layer_rows)
    work.mid_to_outer(outers - 1, True)
    work.finish([dwd_out, dwu_out, alone_out])
    work.drain()
    loop(0, outers, lambda step: known.copy(2, step, 1).wait_recv())
    loop(1, outers, lambda step: known.copy(0, step).wait_send())
    loop(0, outers, lambda step: known.copy(1, step).wait_send())
    loop(0, outers, lambda step: known.copy(2, step).wait_send())

    def swaps_done(at):
        rows = rows_from(mine_at + at * piece, piece)
        shares.copy(at, rows, rows).wait_send()
        down_sent(at).wait_send()
        layer_copy(at, other_at).wait_recv()
        layer_copy(at, mine_at).wait_send()

    loop(0, half // piece, swaps_done)


def feed_forward(ids, x, cot, wu, bu, wd, hidden, gain, wo, mixed, bd, dp_size, collective_id):
    tokens, width = x.shape
    features = wu.shape[1]
    half = tokens // 2
    outers = dp_size // 4
    shape = jax.ShapeDtypeStruct
    items = [
        shape((outers, 2, 2, features // dp_size, width), BF),
        shape((outers, 2, 2, width // dp_size, features), BF),
        shape((outers, 2, 2, 8, LANES), F32),
    ]
    return pl.pallas_call(
        feed_forward_kernel,
        in_specs=[full_spec()] * 11,
        out_specs=[full_spec()] * 10,
        out_shape=[
            shape((outers, 2, 2) + ids.shape, ids.dtype),
            shape((tokens, width), BF),
            shape((tokens, width), BF),
            shape((half, width), F32),
            shape((2, width), F32),
            shape((tokens, wo.shape[0]), BF),
            shape(wo.shape, BF),
        ]
        + [shape(item.shape[3:], F32) for item in items],
        scratch_shapes=[
            pltpu.VMEM((features, tokens), BF),
            pltpu.VMEM((tokens, features), BF),
            pltpu.VMEM((width, tokens), BF),
            pltpu.VMEM((tokens, width), BF),
            pltpu.VMEM((half, width), BF),
            pltpu.VMEM((1, features), F32),
            pltpu.VMEM((1, width), F32),
        ]
        + [pltpu.VMEM(item.shape, item.dtype) for item in items]
        + scatter_shapes(items)
        + [pltpu.SemaphoreType.DMA((outers,)) for _ in range(6)]
        + [pltpu.SemaphoreType.DMA((half // 256,)) for _ in range(2)]
        + [pltpu.SemaphoreType.DMA((half // 128,)) for _ in range(6)],
        compiler_params=pltpu.CompilerParams(
            vmem_limit_bytes=61 * 1024 * 1024, collective_id=collective_id, has_side_effects=True
        ),
        name="feed_forward",
    )(ids, x, cot, wu, bu, wd, hidden, gain, wo, mixed, bd)


def front_kernel(
    rows_ref, noise, scale_c, level, w_in, gain1, bias1, wq, wk, wv, fq_ref, fk_ref, wo, gain2, bias2,
    q_out, k_out, v_out, n1t_out, stream_out, inputs_out, mixed, lse, hidden_out, x2,
    q, k, v, n1t, stream_own, stream, theirs, wo_other, others, qs, ks, vt,
    send_r, recv_r, send_m, recv_m, local,
):
    tokens, width = stream.shape
    half = tokens // 2
    chunk = 256
    pairs = q.shape[1] // LANES
    place = Place()
    mine_at = place.side * half
    barrier = pltpu.get_barrier_semaphore()
    pl.semaphore_signal(barrier, inc=1, device_id=place.other_side(), device_id_type=MESH)
    pl.semaphore_wait(barrier, 1)

    def loop(low, high, stage):
        lax.fori_loop(low, high, lambda step, carry: (stage(step), carry)[1], 0)

    def row_copy(at):
        span = rows_from(at * chunk, chunk)
        return remote(rows_ref.at[span], theirs.at[span], send_r.at[at], recv_r.at[at], place.other_side())

    count = tokens // chunk
    weights = remote(wo, wo_other, send_r.at[count], recv_r.at[count], place.other_side())
    loop(0, count, lambda at: row_copy(at).start())
    weights.start()

    def start_of(at):
        row_copy(at).wait_recv()
        span = rows_from(at * chunk, chunk)
        embedded = rows_ref[span, :].astype(F32) + theirs[span, :].astype(F32)
        low = (scale_c[span, :] * (embedded + level[span, :] * noise[span, :].astype(F32))).astype(BF)
        inputs_out[span, :] = low
        flow = product(low, w_in[...])
        stream[span, :] = flow
        normed, _, _ = normalize(flow, gain1[...], bias1[...])
        normed = normed.astype(BF)
        n1t[:, span] = normed.T
        q[span, :] = product(normed, wq[...]).astype(BF)
        k[span, :] = product(normed, wk[...]).astype(BF)
        v[span, :] = product(normed, wv[...]).astype(BF)

    loop(0, count, start_of)

    def keep(at):
        span = rows_from(at * chunk, chunk)
        stream_own[span, :] = stream[rows_from(mine_at + at * chunk, chunk), :]

    loop(0, half // chunk, keep)
    kept = [
        pltpu.make_async_copy(src, dst, local.at[at])
        for at, (src, dst) in enumerate(
            ((q, q_out), (k, k_out), (v, v_out), (n1t, n1t_out), (stream_own, stream_out))
        )
    ]
    for copy in kept:
        copy.start()

    blocks = tokens // BLOCK
    scale = HEAD_DIM**-0.5

    def pair_copy(at):
        lanes = pl.ds(pl.multiple_of(at * LANES, LANES), LANES)
        return remote(mixed.at[:, lanes], others.at[:, lanes], send_m.at[at], recv_m.at[at], place.other_side())

    def one_pair(at):
        lanes = pl.ds(pl.multiple_of(at * LANES, LANES), LANES)
        scaled = (q[:, lanes].astype(F32) * scale).astype(BF)
        for head in range(2):
            qs[head, :, :LANES] = jnp.where(head_lanes(tokens, head), scaled, jnp.zeros_like(scaled))
            qs[head, :, LANES:] = fq_ref[...]
        ks[:, :LANES] = k[:, lanes]
        ks[:, LANES:] = fk_ref[...]
        vt[...] = v[:, lanes].T
        for block in range(blocks):
            here = slice(block * BLOCK, (block + 1) * BLOCK)
            low, high = near(block, blocks)
            found = []
            for head in range(2):
                scores = times_back(ks[low:high, :], qs[head, here, :])
                peak = jnp.max(scores, axis=0, keepdims=True)
                probs = jnp.exp(scores - peak)
                total = jnp.sum(probs, axis=0, keepdims=True)
                values = vt[head * HEAD_DIM : (head + 1) * HEAD_DIM, low:high]
                found.append(product(values, probs.astype(BF)) / total)
                lse[at, head : head + 1, here] = peak + jnp.log(total)
            mixed[here, lanes] = jnp.concatenate(found, axis=0).T.astype(BF)
        pair_copy(at).start()

    loop(0, pairs, one_pair)

    def ours(at):
        span = rows_from(at * chunk, chunk)
        stream[span, :] += product(mixed[span, :], wo[...])

    loop(0, count, ours)
    weights.wait_recv()
    loop(0, pairs, lambda at: pair_copy(at).wait_recv())

    def finish(at):
        span = rows_from(at * chunk, chunk)
        hidden = stream[span, :] + product(others[span, :], wo_other[...])
        stream[span, :] = hidden
        normed, _, _ = normalize(hidden, gain2[...], bias2[...])
        x2[span, :] = normed.astype(BF)

    loop(0, count, finish)
    hidden_out[...] = stream[rows_from(mine_at, half), :]
    loop(0, count, lambda at: row_copy(at).wait_send())
    weights.wait_send()
    loop(0, pairs, lambda at: pair_copy(at).wait_send())
    for copy in kept:
        copy.wait()


def front(rows, noise, scale_c, level, w_in, gain1, bias1, wq, wk, wv, fq, fk, wo, gain2, bias2, collective_id):
    tokens, embed = rows.shape
    width, columns = wq.shape
    half = tokens // 2
    pairs = columns // LANES
    count = tokens // 256
    shape = jax.ShapeDtypeStruct
    head = shape((tokens, columns), BF)
    scratch = pltpu.VMEM
    return pl.pallas_call(
        front_kernel,
        in_specs=[full_spec()] * 15,
        out_specs=[pl.BlockSpec(memory_space=pl.ANY)] * 5 + [full_spec()] * 5,
        out_shape=[
            head,
            head,
            head,
            shape((width, tokens), BF),
            shape((half, width), F32),
            shape((tokens, embed), BF),
            head,
            shape((pairs, 2, tokens), F32),
            shape((half, width), F32),
            shape((tokens, width), BF),
        ],
        scratch_shapes=[
            scratch(head.shape, BF),
            scratch(head.shape, BF),
            scratch(head.shape, BF),
            scratch((width, tokens), BF),
            scratch((half, width), F32),
            scratch((tokens, width), F32),
            scratch(rows.shape, BF),
            scratch(wo.shape, BF),
            scratch(head.shape, BF),
            scratch((2, tokens, 2 * LANES), BF),
            scratch((tokens, 2 * LANES), BF),
            scratch((LANES, tokens), BF),
        ]
        + [pltpu.SemaphoreType.DMA((count + 1,)) for _ in range(2)]
        + [pltpu.SemaphoreType.DMA((pairs,)) for _ in range(2)]
        + [pltpu.SemaphoreType.DMA((5,))],
        compiler_params=pltpu.CompilerParams(
            vmem_limit_bytes=VMEM_LIMIT, collective_id=collective_id, has_side_effects=True
        ),
        name="front",
    )(rows, noise, scale_c, level, w_in, gain1, bias1, wq, wk, wv, fq, fk, wo, gain2, bias2)


class Gather:
    def __init__(self, place, every, sems):
        self.place, self.every, self.sems = place, every, sems

    def turn(self, step):
        return lax.rem(self.place.outer + step, self.place.outers)

    def copy(self, stage, piece, step, theirs=0):
        p = self.place
        turn = self.turn(step)
        mark = step
        if stage == 0:
            at = turn if theirs else p.outer
            part = self.every.at[at, p.mid, p.core, p.side, piece]
            peer, mark = p.at_outer(turn), at
        elif stage == 3:
            core = 1 - p.core if theirs else p.core
            part, peer = self.every.at[turn, :, core, :, piece], p.other_core()
        elif (stage == 1) == (piece == 0):
            side = 1 - p.side if theirs else p.side
            mid = p.mid if piece == 0 else slice(None)
            part, peer = self.every.at[turn, mid, p.core, side, piece], p.other_side()
        else:
            mid = 1 - p.mid if theirs else p.mid
            side = p.side if piece == 1 else slice(None)
            part, peer = self.every.at[turn, mid, p.core, side, piece], p.other_mid()
        sems = self.sems[2 * stage : 2 * stage + 2]
        return remote(part, part, sems[0].at[piece, step], sems[1].at[piece, mark], peer)


def tail_kernel(
    vocab_part,
    large,
    dq, dk, dv, n1t, wq, wk, wv, stream, hgrad, gain, w_in, inputs, scale_c, scale_n, ids, mine, src_o, sums_two,
    qkv_out, wo_out, w_in_out, sides_out, noise, table,
    every, part, rpart, nsend, nrecv, stage_in, stage_out, total, sums, src_q, src_w, src_s, side_w, side_s, *rest,
):
    early_refs, rest = rest[:12], rest[12:]
    late_refs, rest = rest[:12], rest[12:]
    gather_sems, rest = rest[:8], rest[8:]
    send_x, recv_x, send_n, recv_n, send_s, recv_s, local = rest
    width, tokens = n1t.shape
    columns = wq.shape[1]
    half = tokens // 2
    chunk, piece = 256, 128
    place = Place()
    outers = place.outers
    early = Scatter(place, [src_q, src_o], early_refs[0:2], early_refs[2:4], early_refs[4:6], early_refs[6:])
    late = Scatter(place, [src_w, src_s], late_refs[0:2], late_refs[2:4], late_refs[4:6], late_refs[6:])
    gather = Gather(place, every, gather_sems)
    mine_at, other_at = place.side * half, (1 - place.side) * half
    grads = Swap(place, part, rpart, send_x, recv_x)
    noises = Swap(place, nsend, nrecv, send_n, recv_n)
    sums[...] = jnp.zeros_like(sums)
    src_s[...] = jnp.zeros_like(src_s)
    total[...] = jnp.zeros_like(total)

    sums[2:4, :] = sums_two[...]
    greet(place, True)

    def loop(low, high, stage):
        lax.fori_loop(low, high, lambda step, carry: (stage(step), carry)[1], 0)

    def back_product(start):
        rows = rows_from(start, chunk)
        part[rows, :] = (
            times_back(dq[rows, :], wq[...])
            + times_back(dk[rows, :], wk[...])
            + times_back(dv[rows, :], wv[...])
        ).astype(BF)

    def sent(at):
        return grads.copy(at, rows_from(other_at + at * chunk, chunk), rows_from(at * chunk, chunk))

    def theirs(at):
        back_product(other_at + at * chunk)
        sent(at).start()

    loop(0, half // chunk, theirs)

    group = width // outers

    def weight_grads(step):
        turn = place.turn(step)
        rows = rows_from(turn * group, group)
        for at, grad in enumerate((dq, dk, dv)):
            src_q[turn, :, :, :, at * columns : (at + 1) * columns] = (
                product(n1t[rows, :], grad[...]).astype(BF).reshape(2, 2, group // 4, columns)
            )
        early.start_core(step)

    weight_grads(0)

    def more(step):
        weight_grads(step)
        early.core_to_mid(step - 1)

    loop(1, outers, more)
    loop(0, half // chunk, lambda at: back_product(mine_at + at * chunk))
    early.core_to_mid(outers - 1)

    def norm_grads(which):
        sent(which).wait_recv()

        def one(at):
            here = rows_from(which * chunk + at * piece, piece)
            rows = rows_from(mine_at + which * chunk + at * piece, piece)
            grad = part[rows, :].astype(F32) + rpart[here, :].astype(F32)
            _, unit, inverse = normalize(stream[here, :], 1.0, 0.0)
            back, gain_sum, bias_sum = norm_back(grad, unit, inverse, gain[...])
            sums[0:1, :] += gain_sum[None, :]
            sums[1:2, :] += bias_sum[None, :]
            low = (hgrad[here, :] + back).astype(BF)
            rpart[here, :] = low
            back_in = times_back(low, w_in[...])
            noised = scale_n[here, :] * back_in
            noise[rows, :] = noised
            nsend[here, :] = noised.astype(BF)
            store[rows_from(at * piece, piece), :] = (scale_c[here, :] * back_in).astype(BF)

        spot = every.at[place.outer, place.mid, place.core, place.side, which]
        store = stage_out if large else spot
        loop(0, chunk // piece, one)
        if large:
            moved = pltpu.make_async_copy(stage_out, spot, local.at[0])
            moved.start()
            moved.wait()
        loop(1, outers, lambda step: gather.copy(0, which, step).start())
        gather.copy(1, which, 0).start()

    norm_grads(0)
    norm_grads(1)
    noises.copy(0, pl.ds(0, half), pl.ds(0, half)).start()
    work = contract_rows(inputs[...], rpart[...])
    dp_size = 4 * outers
    rows_w = w_in.shape[0] // dp_size
    lanes = width // dp_size
    for at in range(dp_size):
        spot = (at // 4, (at // 2) % 2, at % 2)
        src_w[spot] = work[at * rows_w : (at + 1) * rows_w, :]
        src_s[spot + (slice(None), slice(0, lanes))] = sums[:, at * lanes : (at + 1) * lanes]
    loop(0, outers, late.start_core)
    loop(0, outers - 1, lambda step: early.mid_to_outer(step, False))
    early.mid_to_outer(outers - 1, True)

    def forward(stage, step):
        for which in range(2):
            gather.copy(stage - 1, which, step, 1).wait_recv()
            gather.copy(stage, which, step).start()

    owned = table.shape[0]
    wanted = lax.broadcasted_iota(jnp.int32, (total.shape[0], 1), 0)
    first = place.side * vocab_part + place.dp * owned

    def collect(step):
        turn = gather.turn(step)
        for which in range(2):
            gather.copy(3, which, step, 1).wait_recv()
            found = jnp.zeros(total.shape, F32)
            pieces = every.at[turn, :, :, :, which]
            if large:
                moved = pltpu.make_async_copy(pieces, stage_in, local.at[0])
                moved.start()
                moved.wait()
                pieces = stage_in
            for spot in range(8):
                mid, core, side = spot // 4, (spot // 2) % 2, spot % 2
                line = 4 * side + 2 * which
                picked = jnp.concatenate(
                    [
                        ((ids[turn, mid, core, line + at : line + at + 1, :] - first) == wanted).astype(BF)
                        for at in range(2)
                    ],
                    axis=1,
                )
                found = found + product(picked, pieces[mid, core, side])
            total[...] += found

    def beat(step):
        @pl.when(step < outers)
        def _():
            forward(1, step)

        @pl.when(jnp.logical_and(step >= 1, step < outers + 1))
        def _():
            forward(2, step - 1)

        @pl.when(jnp.logical_and(step >= 2, step < outers + 2))
        def _():
            forward(3, step - 2)

        @pl.when(step >= 3)
        def _():
            collect(step - 3)

    beat(1)
    loop(0, outers, late.core_to_mid)
    beat(2)
    loop(0, outers - 1, lambda step: late.mid_to_outer(step, False))
    late.mid_to_outer(outers - 1, True)
    early.finish([qkv_out, wo_out])
    loop(3, outers + 2, beat)
    late.finish([w_in_out, sides_out])
    sided = []
    for at, (out, buffer) in enumerate(((w_in_out, side_w), (sides_out, side_s))):
        buffer[0] = out[...]
        sided.append(remote(buffer.at[0], buffer.at[1], send_s.at[at], recv_s.at[at], place.other_side()))
        sided[at].start()
    beat(outers + 2)
    noises.copy(0, pl.ds(0, half), pl.ds(0, half)).wait()
    noise[rows_from(other_at, half), :] = nrecv[...].astype(F32)
    mine_rows = mine[...].astype(F32)
    scale = row_scale(mine_rows)
    grad = total[...][:owned]
    table[...] = scale * grad - mine_rows * (scale * scale * scale) * jnp.mean(
        grad * mine_rows, axis=1, keepdims=True
    )
    for at, (out, buffer) in enumerate(((w_in_out, side_w), (sides_out, side_s))):
        sided[at].wait()
        out[...] = out[...] + buffer[1]
    early.drain()
    late.drain()
    loop(0, half // chunk, lambda at: sent(at).wait_send())

    def done(step):
        for which in range(2):
            for stage in range(1, 4):
                gather.copy(stage, which, step).wait_send()

    loop(0, outers, done)

    def done_outer(step):
        for which in range(2):
            gather.copy(0, which, step).wait_send()

    loop(1, outers, done_outer)


def tail(vocab_part, dp_size, collective_id, *operands):
    (_, _, _, n1t, wq, _, _, _, _, _, w_in, _, _, _, _, mine, src_o, _) = operands
    width, tokens = n1t.shape
    columns = wq.shape[1]
    half = tokens // 2
    outers = dp_size // 4
    embed = w_in.shape[0]
    owned = mine.shape[0]
    padded = -(-owned // LANES) * LANES
    large = outers > 4
    every_shape = (outers, 2, 2, 2, 2, half // 2, embed)

    def blocks_of(rows, cols, dtype):
        return jax.ShapeDtypeStruct((outers, 2, 2, rows, cols), dtype)

    src_q = blocks_of(width // dp_size, 3 * columns, BF)
    src_w = blocks_of(embed // dp_size, width, F32)
    src_s = blocks_of(8, LANES, F32)

    def owned_shape(value):
        return jax.ShapeDtypeStruct(value.shape[3:], F32)

    def scratch(shape, dtype):
        return pltpu.VMEM(shape, dtype)

    return pl.pallas_call(
        functools.partial(tail_kernel, vocab_part, large),
        in_specs=[full_spec()] * len(operands),
        out_specs=[full_spec()] * 6 + ([pl.BlockSpec(memory_space=pl.ANY)] if large else []),
        out_shape=[
            owned_shape(src_q),
            owned_shape(src_o),
            owned_shape(src_w),
            owned_shape(src_s),
            jax.ShapeDtypeStruct((tokens, embed), F32),
            jax.ShapeDtypeStruct((owned, embed), F32),
        ]
        + ([jax.ShapeDtypeStruct(every_shape, BF)] if large else []),
        scratch_shapes=([] if large else [scratch(every_shape, BF)])
        + [
            scratch((tokens, width), BF),
            scratch((half, width), BF),
            scratch((half, embed), BF),
            scratch((half, embed), BF),
            scratch((2, 2, 2, half // 2, embed) if large else (16, LANES), BF),
            scratch((half // 2, embed) if large else (16, LANES), BF),
            scratch((padded, embed), F32),
            scratch((8, width), F32),
            scratch(src_q.shape, BF),
            scratch(src_w.shape, F32),
            scratch(src_s.shape, F32),
            scratch((2,) + src_w.shape[3:], F32),
            scratch((2,) + src_s.shape[3:], F32),
        ]
        + scatter_shapes([src_q, src_o])
        + scatter_shapes([src_w, src_s])
        + [pltpu.SemaphoreType.DMA((2, outers)) for _ in range(8)]
        + [pltpu.SemaphoreType.DMA((2,)) for _ in range(2)]
        + [pltpu.SemaphoreType.DMA((1,)) for _ in range(2)]
        + [pltpu.SemaphoreType.DMA((2,)) for _ in range(3)],
        compiler_params=pltpu.CompilerParams(
            vmem_limit_bytes=VMEM_LIMIT, collective_id=collective_id, has_side_effects=True
        ),
        name="tail",
    )(*operands)


def on_device(
    token_ids,
    segment_ids,
    time_index,
    noise_vec,
    embed_table,
    w_in,
    norm1_gain,
    norm1_bias,
    w_query,
    w_key,
    w_value,
    w_out,
    norm2_gain,
    norm2_bias,
    w_up,
    bias_up,
    w_down,
    bias_down,
    cotangent,
):
    seq_count, length = segment_ids.shape
    tokens = seq_count * length
    half = tokens // 2
    vocab_part = embed_table.shape[0]
    dp_size = lax.axis_size("dp")
    dp_index = lax.axis_index("dp")
    side = lax.axis_index("mp")
    mine_at = side * half

    def own(value):
        return lax.dynamic_slice_in_dim(value, mine_at, half, 0)

    gain_one = norm1_gain.astype(F32)[None, :]
    gain_two = norm2_gain.astype(F32)[None, :]
    fq, fk = attention_masks(segment_ids)
    level_step = jnp.log(time_high / time_low) / (TLEVELS - 1)
    level = jnp.repeat(time_low * jnp.exp(time_index.astype(F32) * level_step), length)[:, None]
    c_in = lax.rsqrt(1.0 + level * level)
    rows = gather_rows(token_ids - side * vocab_part, embed_table)
    (
        queries, key_rows, value_rows, normed_one_t, stream_half, inputs_low, mixed_low, log_total, hidden_half, normed_two,
    ) = front(
        rows, noise_vec, c_in, level, w_in, gain_one, norm1_bias.astype(F32)[None, :], w_query, w_key, w_value,
        fq[0], fk[0], w_out, gain_two, norm2_bias.astype(F32)[None, :], 3,
    )
    (
        every_id, layer_out, _, hidden_grad, norm_two_sums, mixed_grad, w_out_part, w_down_grad, w_up_grad, alone_grad,
    ) = feed_forward(
        token_ids.reshape(-1, LANES), normed_two, cotangent, w_up, bias_up.astype(F32)[None, :], w_down,
        hidden_half, gain_two, w_out, mixed_low, bias_down.astype(F32)[None, :], dp_size, 1,
    )
    query_grad, key_grad, value_grad = attention_backward(
        queries, key_rows, value_rows, mixed_grad, mixed_low, log_total, fq, fk
    )
    owned = vocab_part // dp_size
    mine = lax.dynamic_slice_in_dim(embed_table, dp_index * owned, owned, 0)
    half_c, half_level = own(c_in), own(level)
    qkv_grad, w_out_grad, w_in_grad, sides_grad, noise_grad, table_grad, *_ = tail(
        vocab_part, dp_size, 2, query_grad, key_grad, value_grad, normed_one_t, w_query, w_key, w_value,
        stream_half, hidden_grad, gain_one, w_in, own(inputs_low), half_c, half_c * half_level, every_id, mine,
        owner_blocks(w_out_part, dp_size), norm_two_sums,
    )
    width = gain_one.shape[1] // dp_size
    columns = w_query.shape[1]
    return (
        layer_out,
        noise_grad,
        table_grad,
        w_in_grad,
        sides_grad[0, :width],
        sides_grad[1, :width],
        qkv_grad[:, :columns],
        qkv_grad[:, columns : 2 * columns],
        qkv_grad[:, 2 * columns :],
        w_out_grad.reshape(-1, w_out.shape[1]),
        sides_grad[2, :width],
        sides_grad[3, :width],
        w_up_grad,
        alone_grad[0, : bias_up.shape[0] // dp_size],
        w_down_grad,
        alone_grad[1, :width],
    )


def solution(mesh):
    placed = (
        P("dp"),
        P("dp", None),
        P("dp"),
        P("dp", None),
        P("mp", None),
        P(),
        P(),
        P(),
        P(None, "mp"),
        P(None, "mp"),
        P(None, "mp"),
        P("mp", None),
        P(),
        P(),
        P(None, "mp"),
        P("mp"),
        P("mp", None),
        P(),
        P("dp", None),
    )
    return jax.shard_map(
        on_device,
        mesh=mesh,
        in_specs=placed,
        out_specs=(
            P("dp", None),
            P("dp", None),
            P(("mp", "dp"), None),
            P("dp", None),
            P("dp"),
            P("dp"),
            P("dp", "mp"),
            P("dp", "mp"),
            P("dp", "mp"),
            P(("mp", "dp"), None),
            P("dp"),
            P("dp"),
            P("dp", "mp"),
            P(("mp", "dp")),
            P(("mp", "dp"), None),
            P("dp"),
        ),
        check_vma=False,
    )
```

```python
import functools

import jax
import jax.numpy as jnp
from jax import lax
from jax.experimental import pallas as pl
from jax.experimental.pallas import tpu as pltpu
from jax.sharding import PartitionSpec as P

HEAD_DIM = 64
TLEVELS = 16
DOCS = 4
MAX_RUN = 512

time_low = 0.5
time_high = 10.0
norm_eps = 1e-05
table_eps = 1e-06
masked_score = -1e30

BF = jnp.bfloat16
F32 = jnp.float32
VMEM_LIMIT = 56 * 1024 * 1024
BLOCK = 256
STRIP = 64
LANES = 128


def to_bf16(value):
    return value.astype(BF)


def product(left, right):
    return jnp.dot(left, right, preferred_element_type=F32)


def contract_rows(left, right):
    return lax.dot_general(left, right, (((0,), (0,)), ((), ())), preferred_element_type=F32)


def times_back(left, right):
    return lax.dot_general(left, right, (((1,), (1,)), ((), ())), preferred_element_type=F32)


def params(limit=VMEM_LIMIT):
    return pltpu.CompilerParams(vmem_limit_bytes=limit)


def cost(flops, nbytes, trans=0):
    return pl.CostEstimate(flops=int(flops), bytes_accessed=int(nbytes), transcendentals=int(trans))


def full_spec():
    return pl.BlockSpec(memory_space=pltpu.VMEM)


def row_scale(table_rows):
    return lax.rsqrt(jnp.mean(table_rows * table_rows, axis=1, keepdims=True) + table_eps)


def normalize(values, gain, bias):
    centred = values - jnp.mean(values, axis=-1, keepdims=True)
    inverse = lax.rsqrt(jnp.mean(centred * centred, axis=-1, keepdims=True) + norm_eps)
    unit_rows = centred * inverse
    return (unit_rows * gain + bias, unit_rows, inverse)


def norm_back(grad, unit_rows, inverse, gain):
    scaled = grad * gain
    spread = (
        scaled
        - jnp.mean(scaled, axis=-1, keepdims=True)
        - unit_rows * jnp.mean(scaled * unit_rows, axis=-1, keepdims=True)
    )
    return (inverse * spread, jnp.sum(grad * unit_rows, axis=0), jnp.sum(grad, axis=0))


def gather_kernel(parts, ids, table, out, staged, wide, picked, sems):
    rows, width = table.shape
    tokens = picked.shape[0]
    step = rows // parts

    def copy(part):
        span = pl.ds(part * step, step)
        return pltpu.make_async_copy(table.at[span], staged.at[span], sems.at[part])

    for part in range(parts):
        copy(part).start()
    wide[pl.ds(rows, 8), :] = jnp.zeros((8, width), F32)
    for part in range(parts):
        copy(part).wait()
        piece = step // 5

        @pl.loop(0, 5)
        def _(at):
            span = pl.ds(pl.multiple_of(part * step + at * piece, 16), piece)
            wide[span, :] = staged[span, :].astype(F32)

    def one(at, carry):
        picked[pl.ds(at, 1), :] = wide[pl.ds(ids[at], 1), :]
        return carry

    lax.fori_loop(0, tokens, one, 0, unroll=8)
    found = picked[...]
    out[...] = (found * row_scale(found)).astype(BF)


def gather_rows(local_ids, table):
    rows, width = table.shape
    local_ids = jnp.where(jnp.logical_and(local_ids >= 0, local_ids < rows), local_ids, rows)
    tokens = local_ids.shape[0]
    parts = 5
    return pl.pallas_call(
        functools.partial(gather_kernel, parts),
        grid_spec=pltpu.PrefetchScalarGridSpec(
            num_scalar_prefetch=1,
            grid=(1,),
            in_specs=[pl.BlockSpec(memory_space=pl.ANY)],
            out_specs=pl.BlockSpec((tokens, width), lambda i, ids: (0, 0)),
            scratch_shapes=[
                pltpu.VMEM((rows, width), BF),
                pltpu.VMEM((rows + 8, width), F32),
                pltpu.VMEM((tokens, width), F32),
                pltpu.SemaphoreType.DMA((parts,)),
            ],
        ),
        out_shape=jax.ShapeDtypeStruct((tokens, width), BF),
        compiler_params=params(),
        cost_estimate=cost(0, rows * width * 2),
        name="embed_rows",
    )(local_ids, table)


def head_lanes(rows, head):
    lane = lax.broadcasted_iota(jnp.int32, (rows, LANES), 1)
    return (lane // HEAD_DIM) == head


def near(block, count):
    reach = MAX_RUN // BLOCK
    return max(0, block - reach) * BLOCK, min(count, block + reach + 1) * BLOCK


def attention_masks(segment_ids):
    lane = lax.broadcasted_iota(jnp.int32, (1, LANES), 1)
    same = segment_ids[:, None] == lane
    fk = jnp.where(same, 1.0, 0.0).astype(BF)
    fq = jnp.where(jnp.logical_or(same, lane >= DOCS), 0.0, masked_score).astype(BF)
    return fq, fk


gelu_slope = 0.7978845608028654
gelu_cubic = 0.044715


MESH = pl.DeviceIdType.MESH


class Place:
    def __init__(self):
        self.dp = lax.axis_index("dp")
        self.side = lax.axis_index("mp")
        self.outers = lax.axis_size("dp") // 4
        self.outer = self.dp // 4
        self.mid = (self.dp // 2) % 2
        self.core = self.dp % 2

    def other_core(self):
        return (self.dp + 1 - 2 * self.core, self.side)

    def other_mid(self):
        return (self.dp + 2 - 4 * self.mid, self.side)

    def other_side(self):
        return (self.dp, 1 - self.side)

    def at_outer(self, outer):
        return (outer * 4 + self.mid * 2 + self.core, self.side)

    def turn(self, step):
        return lax.rem(self.outer + 1 + step, self.outers)


def greet(place, with_side):
    barrier = pltpu.get_barrier_semaphore()
    peers = [place.other_core(), place.other_mid()]
    if with_side:
        peers.append(place.other_side())
    for peer in peers:
        pl.semaphore_signal(barrier, inc=1, device_id=peer, device_id_type=MESH)
    for step in range(place.outers - 1):
        pl.semaphore_signal(
            barrier, inc=1, device_id=place.at_outer(place.turn(step)), device_id_type=MESH
        )
    pl.semaphore_wait(barrier, len(peers) + place.outers - 1)


def remote(src, dst, send, recv, device):
    return pltpu.make_async_remote_copy(
        src_ref=src, dst_ref=dst, send_sem=send, recv_sem=recv, device_id=device, device_id_type=MESH
    )


def add_into(dst, left, right):
    dst[...] = (left[...].astype(F32) + right[...].astype(F32)).astype(dst.dtype)


class Scatter:
    def __init__(self, place, sources, one, two, three, sems):
        self.place, self.sources = place, sources
        self.one, self.two, self.three = one, two, three
        self.sems = sems
        self.items = range(len(sources))

    def core_copy(self, step, item):
        p = self.place
        turn = p.turn(step)
        return remote(
            self.sources[item].at[turn, :, 1 - p.core],
            self.one[item].at[turn],
            self.sems[0].at[step, item],
            self.sems[1].at[step, item],
            p.other_core(),
        )

    def mid_copy(self, step, item):
        p = self.place
        turn = p.turn(step)
        return remote(
            self.one[item].at[turn, 1 - p.mid],
            self.two[item].at[turn],
            self.sems[2].at[step, item],
            self.sems[3].at[step, item],
            p.other_mid(),
        )

    def outer_copy(self, step, item):
        p = self.place
        turn = p.turn(step)
        return remote(
            self.two[item].at[turn],
            self.three[item].at[p.outer],
            self.sems[4].at[step, item],
            self.sems[5].at[p.outer, item],
            p.at_outer(turn),
        )

    def arrival(self, step, item):
        p = self.place
        turn = p.turn(step)
        return remote(
            self.two[item].at[turn],
            self.three[item].at[turn],
            self.sems[4].at[step, item],
            self.sems[5].at[turn, item],
            p.at_outer(turn),
        )

    def start_core(self, step):
        for item in self.items:
            self.core_copy(step, item).start()

    def core_to_mid(self, step):
        p = self.place
        turn = p.turn(step)
        for item in self.items:
            self.core_copy(step, item).wait_recv()
            one = self.one[item]
            for mid in range(2):
                add_into(one.at[turn, mid], one.at[turn, mid], self.sources[item].at[turn, mid, p.core])
            self.mid_copy(step, item).start()

    def mid_to_outer(self, step, last):
        p = self.place
        turn = p.turn(step)
        for item in self.items:
            self.mid_copy(step, item).wait_recv()
            two = self.two[item]
            add_into(two.at[turn], two.at[turn], self.one[item].at[turn, p.mid])
            if not last:
                self.outer_copy(step, item).start()

    def finish(self, outs):
        p = self.place
        for item in self.items:
            total = self.two[item][p.outer].astype(F32)
            for step in range(p.outers - 1):
                self.arrival(step, item).wait_recv()
                total = total + self.three[item][p.turn(step)].astype(F32)
            outs[item][...] = total

    def drain(self):
        def one(step, carry):
            for item in self.items:
                self.core_copy(step, item).wait_send()
                self.mid_copy(step, item).wait_send()
            return carry

        lax.fori_loop(0, self.place.outers, one, 0)
        for step in range(self.place.outers - 1):
            for item in self.items:
                self.outer_copy(step, item).wait_send()


def scatter_shapes(sources):
    one = [pltpu.VMEM((s.shape[0], 2) + s.shape[3:], s.dtype) for s in sources]
    two = [pltpu.VMEM((s.shape[0],) + s.shape[3:], s.dtype) for s in sources]
    three = [pltpu.VMEM((s.shape[0],) + s.shape[3:], s.dtype) for s in sources]
    sems = [pltpu.SemaphoreType.DMA((sources[0].shape[0], len(sources))) for _ in range(6)]
    return one + two + three + sems


def owner_blocks(value, dp_size):
    rows, columns = value.shape
    if (rows // dp_size) % 16:
        rows, columns = rows * columns // LANES, LANES
        value = value.reshape(rows, columns)
    return value.reshape(dp_size // 4, 2, 2, rows // dp_size, columns)


class IdGather:
    def __init__(self, place, every, sems):
        self.place, self.every, self.sems = place, every, sems

    def copy(self, stage, step, theirs=0):
        p = self.place
        turn = lax.rem(p.outer + step, p.outers)
        if stage == 0:
            at = turn if theirs else p.outer
            part, peer, mark = self.every.at[at, p.mid, p.core], p.at_outer(turn), at
        elif stage == 1:
            mid = 1 - p.mid if theirs else p.mid
            part, peer, mark = self.every.at[turn, mid, p.core], p.other_mid(), step
        else:
            core = 1 - p.core if theirs else p.core
            part, peer, mark = self.every.at[turn, :, core], p.other_core(), step
        return remote(part, part, self.sems[2 * stage].at[step], self.sems[2 * stage + 1].at[mark], peer)


class Swap:
    def __init__(self, place, src, dst, send, recv):
        self.place, self.src, self.dst, self.send, self.recv = place, src, dst, send, recv

    def copy(self, at, src_rows, dst_rows):
        return remote(
            self.src.at[src_rows], self.dst.at[dst_rows], self.send.at[at], self.recv.at[at], self.place.other_side()
        )


def rows_from(start, size):
    return pl.ds(pl.multiple_of(start, size), size)


def feed_forward_kernel(
    ids, x_in, cot, wu_in, bu, wd_in, hidden, vectors, wo, mixed, q_in, k_in, v_in, lse, fq_ref, fk_ref,
    every, layer, hgrad, norm_sums, wo_part, dwd_out, dwu_out, alone_out, dq_out, dk_out, dv_out,
    act_t, ug, xt, xg, rg, hg, wu, wd, dbu, dbd, qs, ks, kt, gs, delta, scores, slopes, src_d, src_u, src_a, *rest,
):
    scatter_refs, rest = rest[:15], rest[15:]
    id_sems, (send_x, recv_x, send_h, recv_h, send_d, recv_d, send_l, recv_l, local) = rest[:6], rest[6:]
    tokens, width = x_in.shape
    features = wu.shape[1]
    columns = wo.shape[0]
    x = layer
    gain, bd = vectors[2:3, :], vectors[4:5, :]
    half = tokens // 2
    chunk, part, piece = 256, 512, 128
    place = Place()
    outers = place.outers
    work = Scatter(
        place, [src_d, src_u, src_a], scatter_refs[0:3], scatter_refs[3:6], scatter_refs[6:9], scatter_refs[9:]
    )
    known = IdGather(place, every, id_sems)
    every[place.outer, place.mid, place.core] = ids[...]
    mine_at, other_at = place.side * half, (1 - place.side) * half
    grads = Swap(place, xg, rg, send_x, recv_x)
    shares = Swap(place, hg, hg, send_h, recv_h)
    downs = Swap(place, xg, rg, send_d, recv_d)
    layers = Swap(place, layer, layer, send_l, recv_l)
    dbu[...] = jnp.zeros_like(dbu)
    dbd[...] = jnp.zeros_like(dbd)
    src_a[...] = jnp.zeros_like(src_a)
    norm_sums[...] = jnp.zeros_like(norm_sums)
    loads = [
        pltpu.make_async_copy(src, dst, local.at[at])
        for at, (src, dst) in enumerate(((x_in, x), (wu_in, wu), (wd_in, wd)))
    ]
    for copy in loads:
        copy.start()
    greet(place, True)
    for copy in loads:
        copy.wait()

    def loop(low, high, stage):
        lax.fori_loop(low, high, lambda step, carry: (stage(step), carry)[1], 0)

    def ids_mid(step):
        known.copy(0, step, 1).wait_recv()
        known.copy(1, step).start()

    def ids_core(step):
        known.copy(1, step, 1).wait_recv()
        known.copy(2, step).start()

    loop(1, outers, lambda step: known.copy(0, step).start())
    known.copy(1, 0).start()

    def forward(start):
        rows = rows_from(start, chunk)
        xc = x[rows, :]
        gc = cot[rows, :]
        xt[:, rows] = xc.T
        dbd[...] += jnp.sum(gc.astype(F32), axis=0, keepdims=True)
        total = jnp.zeros((chunk, width), F32)
        for at in range(features // part):
            cols = slice(at * part, (at + 1) * part)
            up = product(xc, wu[:, cols]) + bu[:, cols]
            square = up * up
            gate = 0.5 + 0.5 * jnp.tanh(up * (gelu_slope + (gelu_slope * gelu_cubic) * square))
            value = up * gate
            act_t[cols, rows] = value.astype(BF).T
            slope = gate + value * (1.0 - gate) * (
                2.0 * gelu_slope + (6.0 * gelu_slope * gelu_cubic) * square
            )
            low = (times_back(gc, wd[cols, :]) * slope).astype(BF)
            ug[rows, cols] = low
            dbu[:, cols] += jnp.sum(low.astype(F32), axis=0, keepdims=True)
            total = total + times_back(low, wu[:, cols])
        xg[rows, :] = total.astype(BF)

    def sent(at):
        return grads.copy(at, rows_from(other_at + at * chunk, chunk), rows_from(at * chunk, chunk))

    def theirs(at):
        forward(other_at + at * chunk)
        sent(at).start()

    loop(0, half // chunk, theirs)
    loop(0, half // chunk, lambda at: forward(mine_at + at * chunk))
    heads_in = [
        pltpu.make_async_copy(src, wu.at[:, at * columns : (at + 1) * columns], local.at[at])
        for at, src in enumerate((q_in, k_in, v_in))
    ]
    for copy in heads_in:
        copy.start()
    loop(1, outers, ids_mid)
    dp_size = 4 * outers
    up_lanes, down_lanes = features // dp_size, width // dp_size
    for at in range(dp_size):
        spot = (at // 4, (at // 2) % 2, at % 2)
        src_a[spot + (slice(0, 1), slice(0, up_lanes))] = dbu[:, at * up_lanes : (at + 1) * up_lanes]
        src_a[spot + (slice(1, 2), slice(0, down_lanes))] = dbd[:, at * down_lanes : (at + 1) * down_lanes]

    down_rows, up_rows = features // outers // 2, width // outers

    def weight_grads(step):
        turn = place.turn(step)
        for mid in range(2):
            rows = rows_from(turn * (2 * down_rows) + mid * down_rows, down_rows)
            src_d[turn, mid] = product(act_t[rows, :], cot[...]).astype(BF).reshape(2, down_rows // 2, width)
        rows = rows_from(turn * up_rows, up_rows)
        for at in range(features // part):
            cols = slice(at * part, (at + 1) * part)
            src_u[turn, :, :, :, cols] = (
                product(xt[rows, :], ug[:, cols]).astype(BF).reshape(2, 2, up_rows // 4, part)
            )
        work.start_core(step)

    def norm_grads(at):
        @pl.when(at % (chunk // piece) == 0)
        def _():
            sent(at // (chunk // piece)).wait_recv()

        here = rows_from(at * piece, piece)
        rows = rows_from(mine_at + at * piece, piece)
        grad = xg[rows, :].astype(F32) + rg[here, :].astype(F32)
        _, unit, inverse = normalize(hidden[here, :], 1.0, 0.0)
        back, gain_sum, bias_sum = norm_back(grad, unit, inverse, gain)
        norm_sums[0:1, :] += gain_sum[None, :]
        norm_sums[1:2, :] += bias_sum[None, :]
        total = cot[rows, :].astype(F32) + back
        hgrad[here, :] = total
        hg[rows, :] = total.astype(BF)
        shares.copy(at, rows, rows).start()

    weight_grads(0)
    weight_grads(1)
    work.core_to_mid(0)
    loop(0, half // piece, norm_grads)

    def more(step):
        weight_grads(step)
        work.core_to_mid(step - 1)

    loop(2, outers, more)
    work.core_to_mid(outers - 1)
    loop(0, outers, ids_core)

    def downward(at):
        rows = rows_from(at * chunk, chunk)
        xg[rows, :] = contract_rows(act_t[:, rows], wd[...]).astype(BF)

    work.mid_to_outer(0, False)
    loop(0, half // chunk, lambda at: sent(at).wait_send())
    loop(0, tokens // chunk, downward)
    loop(1, outers - 2, lambda step: work.mid_to_outer(step, False))

    def share_from(at):
        rows = rows_from(other_at + at * piece, piece)
        return shares.copy(at, rows, rows)

    loop(0, half // piece, lambda at: share_from(at).wait_recv())

    def down_sent(at):
        return downs.copy(at, rows_from(other_at + at * piece, piece), rows_from(at * piece, piece))

    loop(0, half // piece, lambda at: down_sent(at).start())
    for copy in heads_in:
        copy.wait()

    def mixed_grads(at):
        rows = rows_from(at * chunk, chunk)
        wu[rows, 3 * columns :] = times_back(hg[rows, :], wo[...]).astype(BF)

    loop(0, tokens // chunk, mixed_grads)

    def layer_copy(at, start):
        rows = rows_from(start + at * piece, piece)
        return layers.copy(at, rows, rows)

    def layer_rows(at):
        down_sent(at).wait_recv()
        here = rows_from(at * piece, piece)
        rows = rows_from(mine_at + at * piece, piece)
        layer[rows, :] = (
            hidden[here, :] + (xg[rows, :].astype(F32) + rg[here, :].astype(F32)) + bd
        ).astype(BF)
        layer_copy(at, mine_at).start()

    blocks = tokens // BLOCK
    scale = HEAD_DIM**-0.5

    def one_pair(at):
        def lanes_of(which):
            return pl.ds(pl.multiple_of(which * columns + at * LANES, LANES), LANES)

        keys, grad = wu[:, lanes_of(1)], wu[:, lanes_of(3)]
        scaled = (wu[:, lanes_of(0)].astype(F32) * scale).astype(BF)
        for head in range(2):
            mine = head_lanes(tokens, head)
            qs[head, :, :LANES] = jnp.where(mine, scaled, jnp.zeros_like(scaled))
            qs[head, :, LANES:] = fq_ref[...]
            gs[head] = jnp.where(mine, grad, jnp.zeros_like(grad))
        ks[:, :LANES] = keys
        ks[:, LANES:] = fk_ref[...]
        kt[...] = keys.T
        both = (grad.astype(F32) * mixed[:, lanes_of(0)].astype(F32)).T
        for head in range(2):
            delta[head : head + 1, :] = jnp.sum(
                both[head * HEAD_DIM : (head + 1) * HEAD_DIM], axis=0, keepdims=True
            )
        for block in range(blocks):
            here = slice(block * BLOCK, (block + 1) * BLOCK)
            low, high = near(block, blocks)
            dq = []
            for head in range(2):
                scores[head, low:high, :] = times_back(ks[low:high, :], qs[head, here, :])
                slopes[head, low:high, :] = times_back(wu[low:high, lanes_of(2)], gs[head, here, :])
            for head in range(2):
                offset, shift = lse[at, head : head + 1, here], delta[head : head + 1, here]
                columns_here = slice(head * tokens + block * BLOCK, head * tokens + (block + 1) * BLOCK)
                for at_key in range(low, high, STRIP):
                    strip = slice(at_key, at_key + STRIP)
                    prob = jnp.exp(scores[head, strip, :] - offset)
                    act_t[head * tokens + at_key : head * tokens + at_key + STRIP, here] = prob.astype(BF)
                    ug[strip, columns_here] = (prob * (slopes[head, strip, :] - shift)).astype(BF)
                dq.append(product(kt[head * HEAD_DIM : (head + 1) * HEAD_DIM, low:high], ug[low:high, columns_here]))
            wd[here, lanes_of(0)] = (jnp.concatenate(dq, axis=0).T * scale).astype(BF)
        for block in range(blocks):
            here = slice(block * BLOCK, (block + 1) * BLOCK)
            low, high = near(block, blocks)
            dk = jnp.zeros((BLOCK, LANES), F32)
            dv = jnp.zeros((BLOCK, LANES), F32)
            for head in range(2):
                dv = dv + product(act_t[head * tokens + block * BLOCK : head * tokens + (block + 1) * BLOCK, low:high], gs[head, low:high, :])
                dk = dk + product(ug[here, head * tokens + low : head * tokens + high], qs[head, low:high, :LANES])
            wd[here, lanes_of(1)] = dk.astype(BF)
            wd[tokens + block * BLOCK : tokens + (block + 1) * BLOCK, lanes_of(0)] = dv.astype(BF)

        @pl.when(at == 0)
        def _():
            work.mid_to_outer(outers - 2, False)

        @pl.when(at == 2)
        def _():
            work.mid_to_outer(outers - 1, True)
            loop(0, half // piece, layer_rows)

    loop(0, columns // LANES, one_pair)
    grads_out = [
        pltpu.make_async_copy(src, dst, local.at[at])
        for at, (src, dst) in enumerate(
            (
                (wd.at[:tokens, :columns], dq_out),
                (wd.at[:tokens, columns : 2 * columns], dk_out),
                (wd.at[tokens : 2 * tokens, :columns], dv_out),
            )
        )
    ]
    for copy in grads_out:
        copy.start()
    wo_part[...] = contract_rows(mixed[...], hg[...]).astype(BF)
    work.finish([dwd_out, dwu_out, alone_out])
    for copy in grads_out:
        copy.wait()
    work.drain()
    loop(0, outers, lambda step: known.copy(2, step, 1).wait_recv())
    loop(1, outers, lambda step: known.copy(0, step).wait_send())
    loop(0, outers, lambda step: known.copy(1, step).wait_send())
    loop(0, outers, lambda step: known.copy(2, step).wait_send())

    def swaps_done(at):
        rows = rows_from(mine_at + at * piece, piece)
        shares.copy(at, rows, rows).wait_send()
        down_sent(at).wait_send()
        layer_copy(at, other_at).wait_recv()
        layer_copy(at, mine_at).wait_send()

    loop(0, half // piece, swaps_done)


def feed_forward(dp_size, collective_id, *operands):
    ids, x, _, wu, _, wd, _, _, wo, _, queries, *_ = operands
    tokens, width = x.shape
    features = wu.shape[1]
    half = tokens // 2
    outers = dp_size // 4
    shape = jax.ShapeDtypeStruct
    items = [
        shape((outers, 2, 2, features // dp_size, width), BF),
        shape((outers, 2, 2, width // dp_size, features), BF),
        shape((outers, 2, 2, 8, LANES), F32),
    ]
    anywhere = pl.BlockSpec(memory_space=pl.ANY)
    return pl.pallas_call(
        feed_forward_kernel,
        in_specs=[anywhere if at in (1, 3, 5, 10, 11, 12) else full_spec() for at in range(len(operands))],
        out_specs=[full_spec()] * 8 + [anywhere] * 3,
        out_shape=[
            shape((outers, 2, 2) + ids.shape, ids.dtype),
            shape((tokens, width), BF),
            shape((half, width), F32),
            shape((2, width), F32),
            shape(wo.shape, BF),
        ]
        + [shape(item.shape[3:], F32) for item in items]
        + [shape(queries.shape, BF)] * 3,
        scratch_shapes=[
            pltpu.VMEM((features, tokens), BF),
            pltpu.VMEM((tokens, features), BF),
            pltpu.VMEM((width, tokens), BF),
            pltpu.VMEM((tokens, width), BF),
            pltpu.VMEM((half, width), BF),
            pltpu.VMEM((tokens, width), BF),
            pltpu.VMEM(wu.shape, BF),
            pltpu.VMEM(wd.shape, BF),
            pltpu.VMEM((1, features), F32),
            pltpu.VMEM((1, width), F32),
            pltpu.VMEM((2, tokens, 2 * LANES), BF),
            pltpu.VMEM((tokens, 2 * LANES), BF),
            pltpu.VMEM((LANES, tokens), BF),
            pltpu.VMEM((2, tokens, LANES), BF),
            pltpu.VMEM((2, tokens), F32),
            pltpu.VMEM((2, tokens, BLOCK), F32),
            pltpu.VMEM((2, tokens, BLOCK), F32),
        ]
        + [pltpu.VMEM(item.shape, item.dtype) for item in items]
        + scatter_shapes(items)
        + [pltpu.SemaphoreType.DMA((outers,)) for _ in range(6)]
        + [pltpu.SemaphoreType.DMA((half // 256,)) for _ in range(2)]
        + [pltpu.SemaphoreType.DMA((half // 128,)) for _ in range(6)]
        + [pltpu.SemaphoreType.DMA((3,))],
        compiler_params=pltpu.CompilerParams(
            vmem_limit_bytes=62 * 1024 * 1024, collective_id=collective_id, has_side_effects=True
        ),
        name="feed_forward",
    )(*operands)


def front_kernel(
    rows_ref, noise, scales, w_in, vectors, wq, wk, wv, fq_ref, fk_ref, wo,
    q_out, k_out, v_out, n1t_out, stream_out, inputs_out, mixed, lse, hidden_out, x2,
    q, k, v, n1t, stream_own, stream, theirs, wo_other, others, qs, ks, vt, scores, probs,
    send_r, recv_r, send_m, recv_m, local,
):
    tokens, width = stream.shape
    half = tokens // 2
    chunk = 256
    pairs = q.shape[1] // LANES
    place = Place()
    mine_at = place.side * half
    barrier = pltpu.get_barrier_semaphore()
    pl.semaphore_signal(barrier, inc=1, device_id=place.other_side(), device_id_type=MESH)
    pl.semaphore_wait(barrier, 1)

    def loop(low, high, stage):
        lax.fori_loop(low, high, lambda step, carry: (stage(step), carry)[1], 0)

    def row_copy(at):
        span = rows_from(at * chunk, chunk)
        return remote(rows_ref.at[span], theirs.at[span], send_r.at[at], recv_r.at[at], place.other_side())

    count = tokens // chunk
    weights = remote(wo, wo_other, send_r.at[count], recv_r.at[count], place.other_side())
    loop(0, count, lambda at: row_copy(at).start())
    weights.start()

    def start_of(at):
        row_copy(at).wait_recv()
        span = rows_from(at * chunk, chunk)
        embedded = rows_ref[span, :].astype(F32) + theirs[span, :].astype(F32)
        low = (scales[0:1, 0:1] * (embedded + scales[1:2, 0:1] * noise[span, :].astype(F32))).astype(BF)
        inputs_out[span, :] = low
        flow = product(low, w_in[...])
        stream[span, :] = flow
        normed, _, _ = normalize(flow, vectors[0:1, :], vectors[1:2, :])
        normed = normed.astype(BF)
        n1t[:, span] = normed.T
        q[span, :] = product(normed, wq[...]).astype(BF)
        k[span, :] = product(normed, wk[...]).astype(BF)
        v[span, :] = product(normed, wv[...]).astype(BF)

    loop(0, count, start_of)

    def keep(at):
        span = rows_from(at * chunk, chunk)
        stream_own[span, :] = stream[rows_from(mine_at + at * chunk, chunk), :]

    loop(0, half // chunk, keep)
    kept = [
        pltpu.make_async_copy(src, dst, local.at[at])
        for at, (src, dst) in enumerate(
            ((q, q_out), (k, k_out), (v, v_out), (n1t, n1t_out), (stream_own, stream_out))
        )
    ]
    for copy in kept:
        copy.start()

    blocks = tokens // BLOCK
    scale = HEAD_DIM**-0.5

    def pair_copy(at):
        lanes = pl.ds(pl.multiple_of(at * LANES, LANES), LANES)
        return remote(mixed.at[:, lanes], others.at[:, lanes], send_m.at[at], recv_m.at[at], place.other_side())

    def one_pair(at):
        lanes = pl.ds(pl.multiple_of(at * LANES, LANES), LANES)
        scaled = (q[:, lanes].astype(F32) * scale).astype(BF)
        for head in range(2):
            qs[head, :, :LANES] = jnp.where(head_lanes(tokens, head), scaled, jnp.zeros_like(scaled))
            qs[head, :, LANES:] = fq_ref[...]
        ks[:, :LANES] = k[:, lanes]
        ks[:, LANES:] = fk_ref[...]
        vt[...] = v[:, lanes].T
        for block in range(blocks):
            here = slice(block * BLOCK, (block + 1) * BLOCK)
            low, high = near(block, blocks)
            found = []
            for head in range(2):
                scores[head, low:high, :] = times_back(ks[low:high, :], qs[head, here, :])
            for head in range(2):
                peak = jnp.full((8, BLOCK), masked_score, F32)
                for at_key in range(low, high, STRIP):
                    strip = scores[head, at_key : at_key + STRIP, :].reshape(STRIP // 8, 8, BLOCK)
                    peak = jnp.maximum(peak, jnp.max(strip, axis=0))
                peak = jnp.max(peak, axis=0, keepdims=True)
                total = jnp.zeros((8, BLOCK), F32)
                for at_key in range(low, high, STRIP):
                    strip = jnp.exp(scores[head, at_key : at_key + STRIP, :] - peak)
                    total = total + jnp.sum(strip.reshape(STRIP // 8, 8, BLOCK), axis=0)
                    probs[head, at_key : at_key + STRIP, :] = strip.astype(BF)
                total = jnp.sum(total, axis=0, keepdims=True)
                values = vt[head * HEAD_DIM : (head + 1) * HEAD_DIM, low:high]
                found.append(product(values, probs[head, low:high, :]) / total)
                lse[at, head : head + 1, here] = peak + jnp.log(total)
            mixed[here, lanes] = jnp.concatenate(found, axis=0).T.astype(BF)
        pair_copy(at).start()

    loop(0, pairs, one_pair)

    def ours(at):
        span = rows_from(at * chunk, chunk)
        stream[span, :] += product(mixed[span, :], wo[...])

    loop(0, count, ours)
    weights.wait_recv()
    loop(0, pairs, lambda at: pair_copy(at).wait_recv())

    def finish(at):
        span = rows_from(at * chunk, chunk)
        hidden = stream[span, :] + product(others[span, :], wo_other[...])
        stream[span, :] = hidden
        normed, _, _ = normalize(hidden, vectors[2:3, :], vectors[3:4, :])
        x2[span, :] = normed.astype(BF)

    loop(0, count, finish)
    hidden_out[...] = stream[rows_from(mine_at, half), :]
    loop(0, count, lambda at: row_copy(at).wait_send())
    weights.wait_send()
    loop(0, pairs, lambda at: pair_copy(at).wait_send())
    for copy in kept:
        copy.wait()


def front(rows, noise, scales, w_in, vectors, wq, wk, wv, fq, fk, wo, collective_id):
    tokens, embed = rows.shape
    width, columns = wq.shape
    half = tokens // 2
    pairs = columns // LANES
    count = tokens // 256
    shape = jax.ShapeDtypeStruct
    head = shape((tokens, columns), BF)
    scratch = pltpu.VMEM
    return pl.pallas_call(
        front_kernel,
        in_specs=[full_spec()] * 11,
        out_specs=[pl.BlockSpec(memory_space=pl.ANY)] * 5 + [full_spec()] * 5,
        out_shape=[
            head,
            head,
            head,
            shape((width, tokens), BF),
            shape((half, width), F32),
            shape((tokens, embed), BF),
            head,
            shape((pairs, 2, tokens), F32),
            shape((half, width), F32),
            shape((tokens, width), BF),
        ],
        scratch_shapes=[
            scratch(head.shape, BF),
            scratch(head.shape, BF),
            scratch(head.shape, BF),
            scratch((width, tokens), BF),
            scratch((half, width), F32),
            scratch((tokens, width), F32),
            scratch(rows.shape, BF),
            scratch(wo.shape, BF),
            scratch(head.shape, BF),
            scratch((2, tokens, 2 * LANES), BF),
            scratch((tokens, 2 * LANES), BF),
            scratch((LANES, tokens), BF),
            scratch((2, tokens, BLOCK), F32),
            scratch((2, tokens, BLOCK), BF),
        ]
        + [pltpu.SemaphoreType.DMA((count + 1,)) for _ in range(2)]
        + [pltpu.SemaphoreType.DMA((pairs,)) for _ in range(2)]
        + [pltpu.SemaphoreType.DMA((5,))],
        compiler_params=pltpu.CompilerParams(
            vmem_limit_bytes=VMEM_LIMIT, collective_id=collective_id, has_side_effects=True
        ),
        name="front",
    )(rows, noise, scales, w_in, vectors, wq, wk, wv, fq, fk, wo)


class Gather:
    def __init__(self, place, every, sems):
        self.place, self.every, self.sems = place, every, sems

    def turn(self, step):
        return lax.rem(self.place.outer + step, self.place.outers)

    def copy(self, stage, piece, step, theirs=0):
        p = self.place
        turn = self.turn(step)
        mark = step
        if stage == 0:
            at = turn if theirs else p.outer
            part = self.every.at[at, p.mid, p.core, p.side, piece]
            peer, mark = p.at_outer(turn), at
        elif stage == 3:
            core = 1 - p.core if theirs else p.core
            part, peer = self.every.at[turn, :, core, :, piece], p.other_core()
        elif (stage == 1) == (piece % 2 == 0):
            side = 1 - p.side if theirs else p.side
            mid = slice(None) if piece % 2 else p.mid
            part, peer = self.every.at[turn, mid, p.core, side, piece], p.other_side()
        else:
            mid = 1 - p.mid if theirs else p.mid
            side = p.side if piece % 2 else slice(None)
            part, peer = self.every.at[turn, mid, p.core, side, piece], p.other_mid()
        sems = self.sems[2 * stage : 2 * stage + 2]
        return remote(part, part, sems[0].at[piece, step], sems[1].at[piece, mark], peer)


def tail_kernel(
    vocab_part,
    large,
    dq, dk, dv, n1t_in, wq, wk, wv, stream_in, hgrad_in, vectors, w_in, inputs, scales, ids, mine, src_o, sums_two,
    qkv_out, wo_out, w_in_out, sides_out, noise, table,
    every, n1t, stream, hgrad, part, rpart, nsend, nrecv, stage_in, stage_out, picked, total, sums,
    src_q, src_w, src_s, side_w, side_s, *rest,
):
    early_refs, rest = rest[:12], rest[12:]
    late_refs, rest = rest[:12], rest[12:]
    gather_sems, rest = rest[:8], rest[8:]
    send_x, recv_x, send_n, recv_n, send_s, recv_s, local = rest
    width, tokens = n1t.shape
    columns = wq.shape[1]
    half = tokens // 2
    chunk, piece = 256, half // 4
    place = Place()
    outers = place.outers
    early = Scatter(place, [src_q, src_o], early_refs[0:2], early_refs[2:4], early_refs[4:6], early_refs[6:])
    late = Scatter(place, [src_w, src_s], late_refs[0:2], late_refs[2:4], late_refs[4:6], late_refs[6:])
    gather = Gather(place, every, gather_sems)
    mine_at, other_at = place.side * half, (1 - place.side) * half
    grads = Swap(place, part, rpart, send_x, recv_x)
    noises = Swap(place, nsend, nrecv, send_n, recv_n)
    loads = [
        pltpu.make_async_copy(src, dst, local.at[at])
        for at, (src, dst) in enumerate(((n1t_in, n1t), (stream_in, stream), (hgrad_in, hgrad)))
    ]
    for copy in loads:
        copy.start()
    sums[...] = jnp.zeros_like(sums)
    src_s[...] = jnp.zeros_like(src_s)
    total[...] = jnp.zeros_like(total)
    sums[2:4, :] = sums_two[...]
    greet(place, True)

    def loop(low, high, stage):
        lax.fori_loop(low, high, lambda step, carry: (stage(step), carry)[1], 0)

    def back_product(start):
        rows = rows_from(start, chunk)
        part[rows, :] = (
            times_back(dq[rows, :], wq[...])
            + times_back(dk[rows, :], wk[...])
            + times_back(dv[rows, :], wv[...])
        ).astype(BF)

    def sent(at):
        return grads.copy(at, rows_from(other_at + at * piece, piece), rows_from(at * piece, piece))

    def theirs(at):
        back_product(other_at + at * chunk)
        for step in range(chunk // piece):
            sent(at * (chunk // piece) + step).start()

    loop(0, half // chunk, theirs)
    for copy in loads:
        copy.wait()
    group = width // outers

    def weight_grads(step):
        turn = place.turn(step)
        rows = rows_from(turn * group, group)
        for at, grad in enumerate((dq, dk, dv)):
            src_q[turn, :, :, :, at * columns : (at + 1) * columns] = (
                product(n1t[rows, :], grad[...]).astype(BF).reshape(2, 2, group // 4, columns)
            )
        early.start_core(step)

    weight_grads(0)

    def more(step):
        weight_grads(step)
        early.core_to_mid(step - 1)

    loop(1, outers, more)
    loop(0, half // chunk, lambda at: back_product(mine_at + at * chunk))
    early.core_to_mid(outers - 1)

    def noise_copy(which):
        rows = pl.ds(which * piece, piece)
        return noises.copy(which, rows, rows)

    def norm_grads(which):
        sent(which).wait_recv()
        here = slice(which * piece, (which + 1) * piece)
        rows = rows_from(mine_at + which * piece, piece)
        grad = part[rows, :].astype(F32) + rpart[here, :].astype(F32)
        _, unit, inverse = normalize(stream[here, :], 1.0, 0.0)
        back, gain_sum, bias_sum = norm_back(grad, unit, inverse, vectors[0:1, :])
        low = (hgrad[here, :] + back).astype(BF)
        back_in = times_back(low, w_in[...])
        spot = every.at[place.outer, place.mid, place.core, place.side, which]
        found = (scales[0:1, 0:1] * back_in).astype(BF)
        if large:
            stage_out[...] = found
            moved = pltpu.make_async_copy(stage_out, spot, local.at[0])
            moved.start()
            moved.wait()
        else:
            spot[...] = found
        loop(1, outers, lambda step: gather.copy(0, which, step).start())
        gather.copy(1, which, 0).start()
        sums[0:1, :] += gain_sum[None, :]
        sums[1:2, :] += bias_sum[None, :]
        rpart[here, :] = low
        noised = (scales[0:1, 0:1] * scales[1:2, 0:1]) * back_in
        noise[rows, :] = noised
        nsend[here, :] = noised.astype(BF)

    dp_size = 4 * outers

    def start_late():
        for which in range(4):
            noise_copy(which).start()
        rows_w = w_in.shape[0] // dp_size
        lanes = width // dp_size
        work = contract_rows(inputs[...], rpart[...])
        for at in range(dp_size):
            spot = (at // 4, (at // 2) % 2, at % 2)
            src_w[spot] = work[at * rows_w : (at + 1) * rows_w, :]
            src_s[spot + (slice(None), slice(0, lanes))] = sums[:, at * lanes : (at + 1) * lanes]
        loop(0, outers, late.start_core)

    def forward(stage, which, step):
        gather.copy(stage - 1, which, step, 1).wait_recv()
        gather.copy(stage, which, step).start()

    owned = table.shape[0]
    wanted = lax.broadcasted_iota(jnp.int32, (total.shape[0], 1), 0)
    first = place.side * vocab_part + place.dp * owned

    def collect(pair, step):
        turn = gather.turn(step)
        for which in (2 * pair, 2 * pair + 1):
            gather.copy(3, which, step, 1).wait_recv()
        pieces = every.at[turn, :, :, :, 2 * pair : 2 * pair + 2]
        if large:
            moved = pltpu.make_async_copy(pieces, stage_in, local.at[0])
            moved.start()
            moved.wait()
            pieces = stage_in
        for spot in range(8):
            mid, core, side = spot // 4, (spot // 2) % 2, spot % 2
            for at in range(2):
                line = 4 * side + 2 * pair + at
                lanes = slice((2 * spot + at) * LANES, (2 * spot + at + 1) * LANES)
                picked[:, lanes] = ((ids[turn, mid, core, line : line + 1, :] - first) == wanted).astype(BF)
        total[...] += product(picked[...], pieces[...].reshape(16 * piece, -1))

    sided = []
    for slot in range(8):
        if slot < 4:
            norm_grads(slot)
            last = slot == 3
            loop(
                slot * outers // 4,
                (slot + 1) * outers // 4 - last,
                lambda step: early.mid_to_outer(step, False),
            )
            if last:
                early.mid_to_outer(outers - 1, True)
                start_late()
        if 1 <= slot < 5:
            loop(1, outers, lambda step: forward(1, slot - 1, step))
            forward(2, slot - 1, 0)
        if 2 <= slot < 6:
            loop(1, outers, lambda step: forward(2, slot - 2, step))
            forward(3, slot - 2, 0)
        if 3 <= slot < 7:
            loop(1, outers, lambda step: forward(3, slot - 3, step))
        if slot == 4:
            loop(0, outers, late.core_to_mid)
        if slot == 5:
            loop(0, outers, lambda step: collect(0, step))
            loop(0, outers - 1, lambda step: late.mid_to_outer(step, False))
            late.mid_to_outer(outers - 1, True)
            early.finish([qkv_out, wo_out])
        if slot == 6:
            late.finish([w_in_out, sides_out])
            for at, (out, buffer) in enumerate(((w_in_out, side_w), (sides_out, side_s))):
                buffer[0] = out[...]
                sided.append(remote(buffer.at[0], buffer.at[1], send_s.at[at], recv_s.at[at], place.other_side()))
                sided[at].start()
        if slot == 7:
            loop(0, outers, lambda step: collect(1, step))
    for which in range(4):
        noise_copy(which).wait()
    noise[rows_from(other_at, half), :] = nrecv[...].astype(F32)
    mine_rows = mine[...].astype(F32)
    scale = row_scale(mine_rows)
    grad = total[...][:owned]
    table[...] = scale * grad - mine_rows * (scale * scale * scale) * jnp.mean(
        grad * mine_rows, axis=1, keepdims=True
    )
    for at, (out, buffer) in enumerate(((w_in_out, side_w), (sides_out, side_s))):
        sided[at].wait()
        out[...] = out[...] + buffer[1]
    early.drain()
    late.drain()
    loop(0, half // piece, lambda at: sent(at).wait_send())

    def done(step):
        for which in range(4):
            for stage in range(1, 4):
                gather.copy(stage, which, step).wait_send()

    loop(0, outers, done)

    def done_outer(step):
        for which in range(4):
            gather.copy(0, which, step).wait_send()

    loop(1, outers, done_outer)


def tail(vocab_part, dp_size, collective_id, *operands):
    (_, _, _, n1t, wq, _, _, stream, _, _, w_in, _, _, _, mine, src_o, _) = operands
    width, tokens = n1t.shape
    columns = wq.shape[1]
    half = tokens // 2
    piece = half // 4
    outers = dp_size // 4
    embed = w_in.shape[0]
    owned = mine.shape[0]
    padded = -(-owned // LANES) * LANES
    large = outers > 4
    every_shape = (outers, 2, 2, 2, 4, piece, embed)
    anywhere = pl.BlockSpec(memory_space=pl.ANY)

    def blocks_of(rows, cols, dtype):
        return jax.ShapeDtypeStruct((outers, 2, 2, rows, cols), dtype)

    src_q = blocks_of(width // dp_size, 3 * columns, BF)
    src_w = blocks_of(embed // dp_size, width, F32)
    src_s = blocks_of(8, LANES, F32)

    def owned_shape(value):
        return jax.ShapeDtypeStruct(value.shape[3:], F32)

    def scratch(shape, dtype):
        return pltpu.VMEM(shape, dtype)

    return pl.pallas_call(
        functools.partial(tail_kernel, vocab_part, large),
        in_specs=[anywhere if at in (3, 7, 8) else full_spec() for at in range(len(operands))],
        out_specs=[full_spec()] * 6 + ([anywhere] if large else []),
        out_shape=[
            owned_shape(src_q),
            owned_shape(src_o),
            owned_shape(src_w),
            owned_shape(src_s),
            jax.ShapeDtypeStruct((tokens, embed), F32),
            jax.ShapeDtypeStruct((owned, embed), F32),
        ]
        + ([jax.ShapeDtypeStruct(every_shape, BF)] if large else []),
        scratch_shapes=([] if large else [scratch(every_shape, BF)])
        + [
            scratch(n1t.shape, BF),
            scratch(stream.shape, F32),
            scratch(stream.shape, F32),
            scratch((tokens, width), BF),
            scratch((half, width), BF),
            scratch((half, embed), BF),
            scratch((half, embed), BF),
            scratch((2, 2, 2, 2, piece, embed) if large else (16, LANES), BF),
            scratch((piece, embed) if large else (16, LANES), BF),
            scratch((padded, 16 * piece), BF),
            scratch((padded, embed), F32),
            scratch((8, width), F32),
            scratch(src_q.shape, BF),
            scratch(src_w.shape, F32),
            scratch(src_s.shape, F32),
            scratch((2,) + src_w.shape[3:], F32),
            scratch((2,) + src_s.shape[3:], F32),
        ]
        + scatter_shapes([src_q, src_o])
        + scatter_shapes([src_w, src_s])
        + [pltpu.SemaphoreType.DMA((4, outers)) for _ in range(8)]
        + [pltpu.SemaphoreType.DMA((4,)) for _ in range(4)]
        + [pltpu.SemaphoreType.DMA((2,)) for _ in range(2)]
        + [pltpu.SemaphoreType.DMA((3,))],
        compiler_params=pltpu.CompilerParams(
            vmem_limit_bytes=VMEM_LIMIT, collective_id=collective_id, has_side_effects=True
        ),
        name="tail",
    )(*operands)


def results_kernel(columns, layer, noise, table, w_in, qkv, wo, wu, wd, sides, alone, *refs):
    outs, sems = refs[:16], refs[16]
    sources = (
        layer, noise, table, w_in, qkv.at[:, :columns], qkv.at[:, columns : 2 * columns], qkv.at[:, 2 * columns :], wo, wu, wd,
    )
    copies = [pltpu.make_async_copy(src, dst, sems.at[at]) for at, (src, dst) in enumerate(zip(sources, outs[:10]))]
    for copy in copies:
        copy.start()
    for at in range(4):
        outs[10 + at][...] = sides[at, : outs[10 + at].shape[0]]
    for at in range(2):
        outs[14 + at][...] = alone[at, : outs[14 + at].shape[0]]
    for copy in copies:
        copy.wait()


def results(layer, noise, table, w_in, qkv, wo, wu, wd, sides, alone, small, bias_up_size):
    columns = qkv.shape[1] // 3
    shape = jax.ShapeDtypeStruct
    head = shape((qkv.shape[0], columns), F32)
    large = [layer, noise, table, w_in, head, head, head, wo, wu, wd]
    anywhere = pl.BlockSpec(memory_space=pl.ANY)
    return pl.pallas_call(
        functools.partial(results_kernel, columns),
        in_specs=[full_spec()] * 10,
        out_specs=[anywhere] * 10 + [full_spec()] * 6,
        out_shape=[shape(value.shape, value.dtype) for value in large]
        + [shape((small,), F32)] * 4
        + [shape((bias_up_size,), F32), shape((small,), F32)],
        scratch_shapes=[pltpu.SemaphoreType.DMA((10,))],
        name="results",
    )(layer, noise, table, w_in, qkv, wo, wu, wd, sides, alone)


def on_device(
    token_ids,
    segment_ids,
    time_index,
    noise_vec,
    embed_table,
    w_in,
    norm1_gain,
    norm1_bias,
    w_query,
    w_key,
    w_value,
    w_out,
    norm2_gain,
    norm2_bias,
    w_up,
    bias_up,
    w_down,
    bias_down,
    cotangent,
):
    seq_count, length = segment_ids.shape
    tokens = seq_count * length
    half = tokens // 2
    vocab_part = embed_table.shape[0]
    dp_size = lax.axis_size("dp")
    dp_index = lax.axis_index("dp")
    side = lax.axis_index("mp")
    mine_at = side * half

    def own(value):
        return lax.dynamic_slice_in_dim(value, mine_at, half, 0)

    vectors = jnp.stack([norm1_gain, norm1_bias, norm2_gain, norm2_bias, bias_down]).astype(F32)
    fq, fk = lax.optimization_barrier(attention_masks(segment_ids[0]))
    level_step = jnp.log(time_high / time_low) / (TLEVELS - 1)
    level = time_low * jnp.exp(time_index.astype(F32) * level_step)
    scales = jnp.stack([lax.rsqrt(1.0 + level * level), level])
    rows = gather_rows(token_ids - side * vocab_part, embed_table)
    (
        queries, key_rows, value_rows, normed_one_t, stream_half, inputs_low, mixed_low, log_total, hidden_half, normed_two,
    ) = front(
        rows, noise_vec, scales, w_in, vectors, w_query, w_key, w_value, fq, fk, w_out, 3,
    )
    (
        every_id, layer_out, hidden_grad, norm_two_sums, w_out_part, w_down_grad, w_up_grad, alone_grad,
        query_grad, key_grad, value_grad,
    ) = feed_forward(
        dp_size, 1, token_ids.reshape(-1, LANES), normed_two, cotangent, w_up, bias_up.astype(F32)[None, :], w_down,
        hidden_half, vectors, w_out, mixed_low, queries, key_rows, value_rows, log_total, fq, fk,
    )
    owned = vocab_part // dp_size
    mine = lax.dynamic_slice_in_dim(embed_table, dp_index * owned, owned, 0)
    qkv_grad, w_out_grad, w_in_grad, sides_grad, noise_grad, table_grad, *_ = tail(
        vocab_part, dp_size, 2, query_grad, key_grad, value_grad, normed_one_t, w_query, w_key, w_value,
        stream_half, hidden_grad, vectors, w_in, own(inputs_low), scales, every_id, mine,
        owner_blocks(w_out_part, dp_size), norm_two_sums,
    )
    width = bias_down.shape[0] // dp_size
    (
        layer, noise, table, w_in_sum, query_sum, key_sum, value_sum, w_out_sum, w_up_sum, w_down_sum,
        gain_one_sum, bias_one_sum, gain_two_sum, bias_two_sum, bias_up_sum, bias_down_sum,
    ) = results(
        layer_out, noise_grad, table_grad, w_in_grad, qkv_grad, w_out_grad.reshape(-1, w_out.shape[1]), w_up_grad, w_down_grad,
        sides_grad, alone_grad, width, bias_up.shape[0] // dp_size,
    )
    return (
        layer, noise, table, w_in_sum, gain_one_sum, bias_one_sum, query_sum, key_sum, value_sum, w_out_sum,
        gain_two_sum, bias_two_sum, w_up_sum, bias_up_sum, w_down_sum, bias_down_sum,
    )


def solution(mesh):
    placed = (
        P("dp"),
        P("dp", None),
        P("dp"),
        P("dp", None),
        P("mp", None),
        P(),
        P(),
        P(),
        P(None, "mp"),
        P(None, "mp"),
        P(None, "mp"),
        P("mp", None),
        P(),
        P(),
        P(None, "mp"),
        P("mp"),
        P("mp", None),
        P(),
        P("dp", None),
    )
    return jax.shard_map(
        on_device,
        mesh=mesh,
        in_specs=placed,
        out_specs=(
            P("dp", None),
            P("dp", None),
            P(("mp", "dp"), None),
            P("dp", None),
            P("dp"),
            P("dp"),
            P("dp", "mp"),
            P("dp", "mp"),
            P("dp", "mp"),
            P(("mp", "dp"), None),
            P("dp"),
            P("dp"),
            P("dp", "mp"),
            P(("mp", "dp")),
            P(("mp", "dp"), None),
            P("dp"),
        ),
        check_vma=False,
    )
```

```python
import functools

import jax
import jax.numpy as jnp
from jax import lax
from jax.experimental import pallas as pl
from jax.experimental.pallas import tpu as pltpu
from jax.sharding import PartitionSpec as P

HEAD_DIM = 64
TLEVELS = 16
DOCS = 4
MAX_RUN = 512

time_low = 0.5
time_high = 10.0
norm_eps = 1e-05
table_eps = 1e-06
masked_score = -1e30

BF = jnp.bfloat16
F32 = jnp.float32
VMEM_LIMIT = 56 * 1024 * 1024
BLOCK = 256
STRIP = 64
LANES = 128


def to_bf16(value):
    return value.astype(BF)


def product(left, right):
    return jnp.dot(left, right, preferred_element_type=F32)


def contract_rows(left, right):
    return lax.dot_general(left, right, (((0,), (0,)), ((), ())), preferred_element_type=F32)


def times_back(left, right):
    return lax.dot_general(left, right, (((1,), (1,)), ((), ())), preferred_element_type=F32)


def params(limit=VMEM_LIMIT):
    return pltpu.CompilerParams(vmem_limit_bytes=limit)


def cost(flops, nbytes, trans=0):
    return pl.CostEstimate(flops=int(flops), bytes_accessed=int(nbytes), transcendentals=int(trans))


def full_spec():
    return pl.BlockSpec(memory_space=pltpu.VMEM)


def row_scale(table_rows):
    return lax.rsqrt(jnp.mean(table_rows * table_rows, axis=1, keepdims=True) + table_eps)


def normalize(values, gain, bias):
    centred = values - jnp.mean(values, axis=-1, keepdims=True)
    inverse = lax.rsqrt(jnp.mean(centred * centred, axis=-1, keepdims=True) + norm_eps)
    unit_rows = centred * inverse
    return (unit_rows * gain + bias, unit_rows, inverse)


def norm_back(grad, unit_rows, inverse, gain):
    scaled = grad * gain
    spread = (
        scaled
        - jnp.mean(scaled, axis=-1, keepdims=True)
        - unit_rows * jnp.mean(scaled * unit_rows, axis=-1, keepdims=True)
    )
    return (inverse * spread, jnp.sum(grad * unit_rows, axis=0), jnp.sum(grad, axis=0))


def gather_kernel(parts, ids, table, out, staged, wide, picked, sems):
    rows, width = table.shape
    tokens = picked.shape[0]
    step = rows // parts

    def copy(part):
        span = pl.ds(part * step, step)
        return pltpu.make_async_copy(table.at[span], staged.at[span], sems.at[part])

    for part in range(parts):
        copy(part).start()
    wide[pl.ds(rows, 8), :] = jnp.zeros((8, width), F32)
    for part in range(parts):
        copy(part).wait()
        piece = step // 5

        @pl.loop(0, 5)
        def _(at):
            span = pl.ds(pl.multiple_of(part * step + at * piece, 16), piece)
            wide[span, :] = staged[span, :].astype(F32)

    def one(at, carry):
        picked[pl.ds(at, 1), :] = wide[pl.ds(ids[at], 1), :]
        return carry

    lax.fori_loop(0, tokens, one, 0, unroll=8)
    found = picked[...]
    out[...] = (found * row_scale(found)).astype(BF)


def gather_rows(local_ids, table):
    rows, width = table.shape
    local_ids = jnp.where(jnp.logical_and(local_ids >= 0, local_ids < rows), local_ids, rows)
    tokens = local_ids.shape[0]
    parts = 5
    return pl.pallas_call(
        functools.partial(gather_kernel, parts),
        grid_spec=pltpu.PrefetchScalarGridSpec(
            num_scalar_prefetch=1,
            grid=(1,),
            in_specs=[pl.BlockSpec(memory_space=pl.ANY)],
            out_specs=pl.BlockSpec((tokens, width), lambda i, ids: (0, 0)),
            scratch_shapes=[
                pltpu.VMEM((rows, width), BF),
                pltpu.VMEM((rows + 8, width), F32),
                pltpu.VMEM((tokens, width), F32),
                pltpu.SemaphoreType.DMA((parts,)),
            ],
        ),
        out_shape=jax.ShapeDtypeStruct((tokens, width), BF),
        compiler_params=params(),
        cost_estimate=cost(0, rows * width * 2),
        name="embed_rows",
    )(local_ids, table)


def head_lanes(rows, head):
    lane = lax.broadcasted_iota(jnp.int32, (rows, LANES), 1)
    return (lane // HEAD_DIM) == head


def near(block, count):
    reach = MAX_RUN // BLOCK
    return max(0, block - reach) * BLOCK, min(count, block + reach + 1) * BLOCK


def attention_masks(segment_ids):
    lane = lax.broadcasted_iota(jnp.int32, (1, LANES), 1)
    same = segment_ids[:, None] == lane
    fk = jnp.where(same, 1.0, 0.0).astype(BF)
    fq = jnp.where(jnp.logical_or(same, lane >= DOCS), 0.0, masked_score).astype(BF)
    return fq, fk


gelu_slope = 0.7978845608028654
gelu_cubic = 0.044715


MESH = pl.DeviceIdType.MESH


class Place:
    def __init__(self):
        self.dp = lax.axis_index("dp")
        self.side = lax.axis_index("mp")
        self.outers = lax.axis_size("dp") // 4
        self.outer = self.dp // 4
        self.mid = (self.dp // 2) % 2
        self.core = self.dp % 2

    def other_core(self):
        return (self.dp + 1 - 2 * self.core, self.side)

    def other_mid(self):
        return (self.dp + 2 - 4 * self.mid, self.side)

    def other_side(self):
        return (self.dp, 1 - self.side)

    def at_outer(self, outer):
        return (outer * 4 + self.mid * 2 + self.core, self.side)

    def turn(self, step):
        return lax.rem(self.outer + 1 + step, self.outers)


def greet(place, with_side):
    barrier = pltpu.get_barrier_semaphore()
    peers = [place.other_core(), place.other_mid()]
    if with_side:
        peers.append(place.other_side())
    for peer in peers:
        pl.semaphore_signal(barrier, inc=1, device_id=peer, device_id_type=MESH)
    for step in range(place.outers - 1):
        pl.semaphore_signal(
            barrier, inc=1, device_id=place.at_outer(place.turn(step)), device_id_type=MESH
        )
    pl.semaphore_wait(barrier, len(peers) + place.outers - 1)


def remote(src, dst, send, recv, device):
    return pltpu.make_async_remote_copy(
        src_ref=src, dst_ref=dst, send_sem=send, recv_sem=recv, device_id=device, device_id_type=MESH
    )


def add_into(dst, left, right):
    dst[...] = (left[...].astype(F32) + right[...].astype(F32)).astype(dst.dtype)


class Scatter:
    def __init__(self, place, sources, one, two, three, sems):
        self.place, self.sources = place, sources
        self.one, self.two, self.three = one, two, three
        self.sems = sems
        self.items = range(len(sources))

    def core_copy(self, step, item):
        p = self.place
        turn = p.turn(step)
        return remote(
            self.sources[item].at[turn, :, 1 - p.core],
            self.one[item].at[turn],
            self.sems[0].at[step, item],
            self.sems[1].at[step, item],
            p.other_core(),
        )

    def mid_copy(self, step, item):
        p = self.place
        turn = p.turn(step)
        return remote(
            self.one[item].at[turn, 1 - p.mid],
            self.two[item].at[turn],
            self.sems[2].at[step, item],
            self.sems[3].at[step, item],
            p.other_mid(),
        )

    def outer_copy(self, step, item):
        p = self.place
        turn = p.turn(step)
        return remote(
            self.two[item].at[turn],
            self.three[item].at[p.outer],
            self.sems[4].at[step, item],
            self.sems[5].at[p.outer, item],
            p.at_outer(turn),
        )

    def arrival(self, step, item):
        p = self.place
        turn = p.turn(step)
        return remote(
            self.two[item].at[turn],
            self.three[item].at[turn],
            self.sems[4].at[step, item],
            self.sems[5].at[turn, item],
            p.at_outer(turn),
        )

    def start_core(self, step):
        for item in self.items:
            self.core_copy(step, item).start()

    def core_to_mid(self, step):
        p = self.place
        turn = p.turn(step)
        for item in self.items:
            self.core_copy(step, item).wait_recv()
            one = self.one[item]
            for mid in range(2):
                add_into(one.at[turn, mid], one.at[turn, mid], self.sources[item].at[turn, mid, p.core])
            self.mid_copy(step, item).start()

    def mid_to_outer(self, step, last):
        p = self.place
        turn = p.turn(step)
        for item in self.items:
            self.mid_copy(step, item).wait_recv()
            two = self.two[item]
            add_into(two.at[turn], two.at[turn], self.one[item].at[turn, p.mid])
            if not last:
                self.outer_copy(step, item).start()

    def finish(self, outs):
        p = self.place
        for item in self.items:
            total = self.two[item][p.outer].astype(F32)
            for step in range(p.outers - 1):
                self.arrival(step, item).wait_recv()
                total = total + self.three[item][p.turn(step)].astype(F32)
            outs[item][...] = total

    def drain(self):
        def one(step, carry):
            for item in self.items:
                self.core_copy(step, item).wait_send()
                self.mid_copy(step, item).wait_send()
            return carry

        lax.fori_loop(0, self.place.outers, one, 0)
        for step in range(self.place.outers - 1):
            for item in self.items:
                self.outer_copy(step, item).wait_send()


def scatter_shapes(sources):
    one = [pltpu.VMEM((s.shape[0], 2) + s.shape[3:], s.dtype) for s in sources]
    two = [pltpu.VMEM((s.shape[0],) + s.shape[3:], s.dtype) for s in sources]
    three = [pltpu.VMEM((s.shape[0],) + s.shape[3:], s.dtype) for s in sources]
    sems = [pltpu.SemaphoreType.DMA((sources[0].shape[0], len(sources))) for _ in range(6)]
    return one + two + three + sems


class IdGather:
    def __init__(self, place, every, sems):
        self.place, self.every, self.sems = place, every, sems

    def copy(self, stage, step, theirs=0):
        p = self.place
        turn = lax.rem(p.outer + step, p.outers)
        if stage == 0:
            at = turn if theirs else p.outer
            part, peer, mark = self.every.at[at, p.mid, p.core], p.at_outer(turn), at
        elif stage == 1:
            mid = 1 - p.mid if theirs else p.mid
            part, peer, mark = self.every.at[turn, mid, p.core], p.other_mid(), step
        else:
            core = 1 - p.core if theirs else p.core
            part, peer, mark = self.every.at[turn, :, core], p.other_core(), step
        return remote(part, part, self.sems[2 * stage].at[step], self.sems[2 * stage + 1].at[mark], peer)


class Swap:
    def __init__(self, place, src, dst, send, recv):
        self.place, self.src, self.dst, self.send, self.recv = place, src, dst, send, recv

    def copy(self, at, src_rows, dst_rows):
        return remote(
            self.src.at[src_rows], self.dst.at[dst_rows], self.send.at[at], self.recv.at[at], self.place.other_side()
        )


def rows_from(start, size):
    return pl.ds(pl.multiple_of(start, size), size)


def feed_forward_kernel(
    ids, x_in, cot, wu_in, bu, wd_in, hidden, vectors, wo_in, mixed, q_in, k_in, v_in, lse, fq_ref, fk_ref, others,
    wo_other_in, every, layer, hg, norm_sums, wo_out, dwd_out, dwu_out, alone_out, dq_out, dk_out, dv_out,
    act_t, ug, xt, xg, rg, mgs, mgr, wu, wd, dbu, dbd, qs, ks, kt, gs, delta, scores, slopes,
    wo_sum, wo_recv, src_d, src_u, src_a, src_o, *rest,
):
    scatter_refs, rest = rest[:15], rest[15:]
    out_refs, rest = rest[:9], rest[9:]
    id_sems, (send_x, recv_x, send_h, recv_h, send_d, recv_d, send_l, recv_l, local) = rest[:6], rest[6:]
    tokens, width = x_in.shape
    features = wu.shape[1]
    columns = wo_in.shape[0]
    x = layer
    wo, wo_other = layer.at[:columns], layer.at[columns : 2 * columns]
    gain, bd = vectors[2:3, :], vectors[4:5, :]
    half = tokens // 2
    chunk, part, piece = 256, 512, 128
    place = Place()
    outers = place.outers
    work = Scatter(
        place, [src_d, src_u, src_a], scatter_refs[0:3], scatter_refs[3:6], scatter_refs[6:9], scatter_refs[9:]
    )
    after = Scatter(place, [src_o], out_refs[0:1], out_refs[1:2], out_refs[2:3], out_refs[3:])
    known = IdGather(place, every, id_sems)
    every[place.outer, place.mid, place.core] = ids[...]
    mine_at, other_at = place.side * half, (1 - place.side) * half
    grads = Swap(place, xg, rg, send_x, recv_x)
    mixes = Swap(place, mgs, mgr, send_h, recv_h)
    downs = Swap(place, xg, rg, send_d, recv_d)
    layers = Swap(place, layer, layer, send_l, recv_l)
    dbu[...] = jnp.zeros_like(dbu)
    dbd[...] = jnp.zeros_like(dbd)
    src_a[...] = jnp.zeros_like(src_a)
    norm_sums[...] = jnp.zeros_like(norm_sums)
    loads = [
        pltpu.make_async_copy(src, dst, local.at[at])
        for at, (src, dst) in enumerate(((x_in, x), (wu_in, wu), (wd_in, wd)))
    ]
    for copy in loads:
        copy.start()
    greet(place, True)
    for copy in loads:
        copy.wait()

    def loop(low, high, stage):
        lax.fori_loop(low, high, lambda step, carry: (stage(step), carry)[1], 0)

    def ids_mid(step):
        known.copy(0, step, 1).wait_recv()
        known.copy(1, step).start()

    def ids_core(step):
        known.copy(1, step, 1).wait_recv()
        known.copy(2, step).start()

    loop(1, outers, lambda step: known.copy(0, step).start())
    known.copy(1, 0).start()

    def forward(start):
        rows = rows_from(start, chunk)
        xc = x[rows, :]
        gc = cot[rows, :]
        xt[:, rows] = xc.T
        dbd[...] += jnp.sum(gc.astype(F32), axis=0, keepdims=True)
        total = jnp.zeros((chunk, width), F32)
        for at in range(features // part):
            cols = slice(at * part, (at + 1) * part)
            up = product(xc, wu[:, cols]) + bu[:, cols]
            square = up * up
            gate = 0.5 + 0.5 * jnp.tanh(up * (gelu_slope + (gelu_slope * gelu_cubic) * square))
            value = up * gate
            act_t[cols, rows] = value.astype(BF).T
            slope = gate + value * (1.0 - gate) * (
                2.0 * gelu_slope + (6.0 * gelu_slope * gelu_cubic) * square
            )
            low = (times_back(gc, wd[cols, :]) * slope).astype(BF)
            ug[rows, cols] = low
            dbu[:, cols] += jnp.sum(low.astype(F32), axis=0, keepdims=True)
            total = total + times_back(low, wu[:, cols])
        xg[rows, :] = total.astype(BF)

    def sent(at):
        return grads.copy(at, rows_from(other_at + at * chunk, chunk), rows_from(at * chunk, chunk))

    def theirs(at):
        forward(other_at + at * chunk)
        sent(at).start()

    loop(0, half // chunk, theirs)
    loop(0, half // chunk, lambda at: forward(mine_at + at * chunk))
    heads_in = [
        pltpu.make_async_copy(src, wu.at[:, at * columns : (at + 1) * columns], local.at[at])
        for at, src in enumerate((q_in, k_in, v_in))
    ] + [
        pltpu.make_async_copy(src, dst, local.at[3 + at])
        for at, (src, dst) in enumerate(((wo_in, wo), (wo_other_in, wo_other)))
    ]
    for copy in heads_in:
        copy.start()
    loop(1, outers, ids_mid)
    dp_size = 4 * outers
    up_lanes, down_lanes = features // dp_size, width // dp_size
    for at in range(dp_size):
        spot = (at // 4, (at // 2) % 2, at % 2)
        src_a[spot + (slice(0, 1), slice(0, up_lanes))] = dbu[:, at * up_lanes : (at + 1) * up_lanes]
        src_a[spot + (slice(1, 2), slice(0, down_lanes))] = dbd[:, at * down_lanes : (at + 1) * down_lanes]

    down_rows, up_rows = features // outers // 2, width // outers

    def weight_grads(step):
        turn = place.turn(step)
        for mid in range(2):
            rows = rows_from(turn * (2 * down_rows) + mid * down_rows, down_rows)
            src_d[turn, mid] = product(act_t[rows, :], cot[...]).astype(BF).reshape(2, down_rows // 2, width)
        rows = rows_from(turn * up_rows, up_rows)
        for at in range(features // part):
            cols = slice(at * part, (at + 1) * part)
            src_u[turn, :, :, :, cols] = (
                product(xt[rows, :], ug[:, cols]).astype(BF).reshape(2, 2, up_rows // 4, part)
            )
        work.start_core(step)

    def norm_grads(at):
        @pl.when(at % (chunk // piece) == 0)
        def _():
            sent(at // (chunk // piece)).wait_recv()

        here = rows_from(at * piece, piece)
        rows = rows_from(mine_at + at * piece, piece)
        grad = xg[rows, :].astype(F32) + rg[here, :].astype(F32)
        _, unit, inverse = normalize(hidden[here, :], 1.0, 0.0)
        back, gain_sum, bias_sum = norm_back(grad, unit, inverse, gain)
        norm_sums[0:1, :] += gain_sum[None, :]
        norm_sums[1:2, :] += bias_sum[None, :]
        total = cot[rows, :].astype(F32) + back
        hg[here, :] = total.astype(BF)

    def mix_copy(at):
        here = rows_from(at * chunk, chunk)
        return mixes.copy(at, here, here)

    def mixed_grads(at):
        here = rows_from(at * chunk, chunk)
        mgs[here, :] = times_back(hg[here, :], wo_other[...]).astype(BF)
        mix_copy(at).start()
        wu[rows_from(mine_at + at * chunk, chunk), 3 * columns :] = times_back(hg[here, :], wo[...]).astype(BF)

    weight_grads(0)
    weight_grads(1)
    work.core_to_mid(0)
    loop(0, half // piece, norm_grads)
    for copy in heads_in:
        copy.wait()
    loop(0, half // chunk, mixed_grads)
    rows_o = columns // dp_size
    for at in range(outers):
        cols = slice(at * 4 * rows_o, (at + 1) * 4 * rows_o)
        src_o[at] = jnp.concatenate(
            [
                contract_rows(mixed[rows_from(mine_at, half), cols], hg[...]).reshape(2, 2, rows_o, width),
                contract_rows(others[:, cols], hg[...]).reshape(2, 2, rows_o, width),
            ],
            axis=2,
        ).astype(BF)
    loop(0, outers, after.start_core)

    def more(step):
        weight_grads(step)
        work.core_to_mid(step - 1)

    loop(2, outers, more)
    work.core_to_mid(outers - 1)
    loop(0, half // chunk, lambda at: sent(at).wait_send())

    def downward(start):
        rows = rows_from(start, chunk)
        xg[rows, :] = contract_rows(act_t[:, rows], wd[...]).astype(BF)

    def down_sent(at):
        return downs.copy(at, rows_from(other_at + at * piece, piece), rows_from(at * piece, piece))

    def down_theirs(at):
        downward(other_at + at * chunk)
        mix_copy(at).wait_recv()

    loop(0, half // chunk, down_theirs)
    loop(0, half // piece, lambda at: down_sent(at).start())
    wu[rows_from(other_at, half), 3 * columns :] = mgr[...]
    loop(0, half // chunk, lambda at: downward(mine_at + at * chunk))
    loop(0, outers, ids_core)
    loop(0, outers, after.core_to_mid)
    loop(0, outers - 3, lambda step: work.mid_to_outer(step, False))

    def layer_copy(at, start):
        rows = rows_from(start + at * piece, piece)
        return layers.copy(at, rows, rows)

    def layer_rows(at):
        down_sent(at).wait_recv()
        here = rows_from(at * piece, piece)
        rows = rows_from(mine_at + at * piece, piece)
        layer[rows, :] = (
            hidden[here, :] + (xg[rows, :].astype(F32) + rg[here, :].astype(F32)) + bd
        ).astype(BF)
        layer_copy(at, mine_at).start()

    blocks = tokens // BLOCK
    scale = HEAD_DIM**-0.5

    def one_pair(at):
        def lanes_of(which):
            return pl.ds(pl.multiple_of(which * columns + at * LANES, LANES), LANES)

        keys, grad = wu[:, lanes_of(1)], wu[:, lanes_of(3)]
        scaled = (wu[:, lanes_of(0)].astype(F32) * scale).astype(BF)
        for head in range(2):
            mine = head_lanes(tokens, head)
            qs[head, :, :LANES] = jnp.where(mine, scaled, jnp.zeros_like(scaled))
            qs[head, :, LANES:] = fq_ref[...]
            gs[head] = jnp.where(mine, grad, jnp.zeros_like(grad))
        ks[:, :LANES] = keys
        ks[:, LANES:] = fk_ref[...]
        kt[...] = keys.T
        both = (grad.astype(F32) * mixed[:, lanes_of(0)].astype(F32)).T
        for head in range(2):
            delta[head : head + 1, :] = jnp.sum(
                both[head * HEAD_DIM : (head + 1) * HEAD_DIM], axis=0, keepdims=True
            )
        for block in range(blocks):
            here = slice(block * BLOCK, (block + 1) * BLOCK)
            low, high = near(block, blocks)
            dq = []
            for head in range(2):
                scores[low:high, :] = times_back(ks[low:high, :], qs[head, here, :])
                slopes[low:high, :] = times_back(wu[low:high, lanes_of(2)], gs[head, here, :])
                offset, shift = lse[at, head : head + 1, here], delta[head : head + 1, here]
                columns_here = slice(head * tokens + block * BLOCK, head * tokens + (block + 1) * BLOCK)
                for at_key in range(low, high, STRIP):
                    strip = slice(at_key, at_key + STRIP)
                    prob = jnp.exp(scores[strip, :] - offset)
                    act_t[head * tokens + at_key : head * tokens + at_key + STRIP, here] = prob.astype(BF)
                    ug[strip, columns_here] = (prob * (slopes[strip, :] - shift)).astype(BF)
                dq.append(product(kt[head * HEAD_DIM : (head + 1) * HEAD_DIM, low:high], ug[low:high, columns_here]))
            wd[here, lanes_of(0)] = (jnp.concatenate(dq, axis=0).T * scale).astype(BF)
        for block in range(blocks):
            here = slice(block * BLOCK, (block + 1) * BLOCK)
            low, high = near(block, blocks)
            dk = jnp.zeros((BLOCK, LANES), F32)
            dv = jnp.zeros((BLOCK, LANES), F32)
            for head in range(2):
                dv = dv + product(act_t[head * tokens + block * BLOCK : head * tokens + (block + 1) * BLOCK, low:high], gs[head, low:high, :])
                dk = dk + product(ug[here, head * tokens + low : head * tokens + high], qs[head, low:high, :LANES])
            wd[here, lanes_of(1)] = dk.astype(BF)
            wd[tokens + block * BLOCK : tokens + (block + 1) * BLOCK, lanes_of(0)] = dv.astype(BF)

        @pl.when(at < 2)
        def _():
            work.mid_to_outer(outers - 3 + at, False)

        @pl.when(at == 2)
        def _():
            work.mid_to_outer(outers - 1, True)
            loop(0, half // piece, layer_rows)

        @pl.when(at == 3)
        def _():
            loop(0, outers - 1, lambda step: after.mid_to_outer(step, False))
            after.mid_to_outer(outers - 1, True)

    loop(0, columns // LANES, one_pair)
    grads_out = [
        pltpu.make_async_copy(src, dst, local.at[at])
        for at, (src, dst) in enumerate(
            (
                (wd.at[:tokens, :columns], dq_out),
                (wd.at[:tokens, columns : 2 * columns], dk_out),
                (wd.at[tokens : 2 * tokens, :columns], dv_out),
            )
        )
    ]
    for copy in grads_out:
        copy.start()
    after.finish([wo_sum])
    wo_swap = remote(
        wo_sum.at[pl.ds(rows_o, rows_o)], wo_recv, send_h.at[half // chunk], recv_h.at[half // chunk], place.other_side()
    )
    wo_swap.start()
    work.finish([dwd_out, dwu_out, alone_out])
    for copy in grads_out:
        copy.wait()
    wo_swap.wait()
    wo_out[...] = wo_sum[:rows_o, :] + wo_recv[...]
    work.drain()
    after.drain()
    loop(0, outers, lambda step: known.copy(2, step, 1).wait_recv())
    loop(1, outers, lambda step: known.copy(0, step).wait_send())
    loop(0, outers, lambda step: known.copy(1, step).wait_send())
    loop(0, outers, lambda step: known.copy(2, step).wait_send())

    def swaps_done(at):
        rows = rows_from(mine_at + at * piece, piece)
        down_sent(at).wait_send()
        layer_copy(at, other_at).wait_recv()
        layer_copy(at, mine_at).wait_send()

    loop(0, half // piece, swaps_done)
    loop(0, half // chunk, lambda at: mix_copy(at).wait_send())


def feed_forward(dp_size, collective_id, *operands):
    ids, x, _, wu, _, wd, _, _, wo, _, queries, *_ = operands
    tokens, width = x.shape
    columns = wo.shape[0]
    features = wu.shape[1]
    half = tokens // 2
    outers = dp_size // 4
    shape = jax.ShapeDtypeStruct
    items = [
        shape((outers, 2, 2, features // dp_size, width), BF),
        shape((outers, 2, 2, width // dp_size, features), BF),
        shape((outers, 2, 2, 8, LANES), F32),
    ]
    item_o = shape((outers, 2, 2, 2 * columns // dp_size, width), BF)
    anywhere = pl.BlockSpec(memory_space=pl.ANY)
    return pl.pallas_call(
        feed_forward_kernel,
        in_specs=[anywhere if at in (1, 3, 5, 8, 10, 11, 12, 17) else full_spec() for at in range(len(operands))],
        out_specs=[full_spec()] * 8 + [anywhere] * 3,
        out_shape=[
            shape((outers, 2, 2) + ids.shape, ids.dtype),
            shape((tokens, width), BF),
            shape((half, width), BF),
            shape((2, width), F32),
            shape((wo.shape[0] // dp_size, width), F32),
        ]
        + [shape(item.shape[3:], F32) for item in items]
        + [shape(queries.shape, BF)] * 3,
        scratch_shapes=[
            pltpu.VMEM((features, tokens), BF),
            pltpu.VMEM((tokens, features), BF),
            pltpu.VMEM((width, tokens), BF),
            pltpu.VMEM((tokens, width), BF),
            pltpu.VMEM((half, width), BF),
            pltpu.VMEM((half, columns), BF),
            pltpu.VMEM((half, columns), BF),
            pltpu.VMEM(wu.shape, BF),
            pltpu.VMEM(wd.shape, BF),
            pltpu.VMEM((1, features), F32),
            pltpu.VMEM((1, width), F32),
            pltpu.VMEM((2, tokens, 2 * LANES), BF),
            pltpu.VMEM((tokens, 2 * LANES), BF),
            pltpu.VMEM((LANES, tokens), BF),
            pltpu.VMEM((2, tokens, LANES), BF),
            pltpu.VMEM((2, tokens), F32),
            pltpu.VMEM((tokens, BLOCK), F32),
            pltpu.VMEM((tokens, BLOCK), F32),
            pltpu.VMEM(item_o.shape[3:], F32),
            pltpu.VMEM((columns // dp_size, width), F32),
        ]
        + [pltpu.VMEM(item.shape, item.dtype) for item in items + [item_o]]
        + scatter_shapes(items)
        + scatter_shapes([item_o])
        + [pltpu.SemaphoreType.DMA((outers,)) for _ in range(6)]
        + [pltpu.SemaphoreType.DMA((half // 256,)) for _ in range(2)]
        + [pltpu.SemaphoreType.DMA((half // 128,)) for _ in range(6)]
        + [pltpu.SemaphoreType.DMA((5,))],
        compiler_params=pltpu.CompilerParams(
            vmem_limit_bytes=60 * 1024 * 1024, collective_id=collective_id, has_side_effects=True
        ),
        name="feed_forward",
    )(*operands)


def front_kernel(
    rows_ref, noise, scales, w_in, vectors, wq, wk, wv, fq_ref, fk_ref, wo,
    q_out, k_out, v_out, n1t_out, stream_out, others_out, wo_out, inputs_out, mixed, lse, hidden_out, x2,
    q, k, v, n1t, stream_own, stream, theirs, wo_other, others, qs, ks, vt, scores, probs,
    send_r, recv_r, send_m, recv_m, local,
):
    tokens, width = stream.shape
    half = tokens // 2
    chunk = 256
    pairs = q.shape[1] // LANES
    place = Place()
    mine_at = place.side * half
    barrier = pltpu.get_barrier_semaphore()
    for peer in (place.other_side(), place.other_core()):
        pl.semaphore_signal(barrier, inc=1, device_id=peer, device_id_type=MESH)
    pl.semaphore_wait(barrier, 2)

    def loop(low, high, stage):
        lax.fori_loop(low, high, lambda step, carry: (stage(step), carry)[1], 0)

    def row_copy(at):
        span = rows_from(at * chunk, chunk)
        return remote(rows_ref.at[span], theirs.at[span], send_r.at[at], recv_r.at[at], place.other_side())

    count = tokens // chunk
    part = wo.shape[0] // 2

    def weights(step):
        rows = rows_from(place.core * part, part)
        src = wo_other if step else wo
        peer = place.other_core() if step else place.other_side()
        return remote(src.at[rows], wo_other.at[rows], send_r.at[count + step], recv_r.at[count + step], peer)

    loop(0, count, lambda at: row_copy(at).start())
    weights(0).start()

    def start_of(at):
        row_copy(at).wait_recv()
        span = rows_from(at * chunk, chunk)
        embedded = rows_ref[span, :].astype(F32) + theirs[span, :].astype(F32)
        low = (scales[0:1, 0:1] * (embedded + scales[1:2, 0:1] * noise[span, :].astype(F32))).astype(BF)
        inputs_out[span, :] = low
        flow = product(low, w_in[...])
        stream[span, :] = flow
        normed, _, _ = normalize(flow, vectors[0:1, :], vectors[1:2, :])
        normed = normed.astype(BF)
        n1t[:, span] = normed.T
        q[span, :] = product(normed, wq[...]).astype(BF)
        k[span, :] = product(normed, wk[...]).astype(BF)
        v[span, :] = product(normed, wv[...]).astype(BF)

    loop(0, count, start_of)

    def keep(at):
        span = rows_from(at * chunk, chunk)
        stream_own[span, :] = stream[rows_from(mine_at + at * chunk, chunk), :]

    loop(0, half // chunk, keep)
    kept = [
        pltpu.make_async_copy(src, dst, local.at[at])
        for at, (src, dst) in enumerate(
            ((q, q_out), (k, k_out), (v, v_out), (n1t, n1t_out), (stream_own, stream_out))
        )
    ]
    for copy in kept:
        copy.start()

    blocks = tokens // BLOCK
    scale = HEAD_DIM**-0.5

    def pair_copy(at):
        lanes = pl.ds(pl.multiple_of(at * LANES, LANES), LANES)
        return remote(mixed.at[:, lanes], others.at[:, lanes], send_m.at[at], recv_m.at[at], place.other_side())

    def one_pair(at):
        lanes = pl.ds(pl.multiple_of(at * LANES, LANES), LANES)
        scaled = (q[:, lanes].astype(F32) * scale).astype(BF)
        for head in range(2):
            qs[head, :, :LANES] = jnp.where(head_lanes(tokens, head), scaled, jnp.zeros_like(scaled))
            qs[head, :, LANES:] = fq_ref[...]
        ks[:, :LANES] = k[:, lanes]
        ks[:, LANES:] = fk_ref[...]
        vt[...] = v[:, lanes].T
        for block in range(blocks):
            here = slice(block * BLOCK, (block + 1) * BLOCK)
            low, high = near(block, blocks)
            found = []
            for head in range(2):
                scores[head, low:high, :] = times_back(ks[low:high, :], qs[head, here, :])
            for head in range(2):
                peak = jnp.full((8, BLOCK), masked_score, F32)
                for at_key in range(low, high, STRIP):
                    strip = scores[head, at_key : at_key + STRIP, :].reshape(STRIP // 8, 8, BLOCK)
                    peak = jnp.maximum(peak, jnp.max(strip, axis=0))
                peak = jnp.max(peak, axis=0, keepdims=True)
                total = jnp.zeros((8, BLOCK), F32)
                for at_key in range(low, high, STRIP):
                    strip = jnp.exp(scores[head, at_key : at_key + STRIP, :] - peak)
                    total = total + jnp.sum(strip.reshape(STRIP // 8, 8, BLOCK), axis=0)
                    probs[head, at_key : at_key + STRIP, :] = strip.astype(BF)
                total = jnp.sum(total, axis=0, keepdims=True)
                values = vt[head * HEAD_DIM : (head + 1) * HEAD_DIM, low:high]
                found.append(product(values, probs[head, low:high, :]) / total)
                lse[at, head : head + 1, here] = peak + jnp.log(total)
            mixed[here, lanes] = jnp.concatenate(found, axis=0).T.astype(BF)
        pair_copy(at).start()

        @pl.when(at == 1)
        def _():
            weights(0).wait_recv()
            weights(1).start()

    loop(0, pairs, one_pair)

    def ours(at):
        span = rows_from(at * chunk, chunk)
        stream[span, :] += product(mixed[span, :], wo[...])

    loop(0, count, ours)
    weights(1).wait_recv()
    loop(0, pairs, lambda at: pair_copy(at).wait_recv())
    kept += [
        pltpu.make_async_copy(src, dst, local.at[5 + at])
        for at, (src, dst) in enumerate(((others.at[rows_from(mine_at, half)], others_out), (wo_other, wo_out)))
    ]
    for copy in kept[5:]:
        copy.start()

    def finish(at):
        span = rows_from(at * chunk, chunk)
        hidden = stream[span, :] + product(others[span, :], wo_other[...])
        stream[span, :] = hidden
        normed, _, _ = normalize(hidden, vectors[2:3, :], vectors[3:4, :])
        x2[span, :] = normed.astype(BF)

    loop(0, count, finish)
    hidden_out[...] = stream[rows_from(mine_at, half), :]
    loop(0, count, lambda at: row_copy(at).wait_send())
    weights(0).wait_send()
    weights(1).wait_send()
    loop(0, pairs, lambda at: pair_copy(at).wait_send())
    for copy in kept:
        copy.wait()


def front(rows, noise, scales, w_in, vectors, wq, wk, wv, fq, fk, wo, collective_id):
    tokens, embed = rows.shape
    width, columns = wq.shape
    half = tokens // 2
    pairs = columns // LANES
    count = tokens // 256
    shape = jax.ShapeDtypeStruct
    head = shape((tokens, columns), BF)
    scratch = pltpu.VMEM
    return pl.pallas_call(
        front_kernel,
        in_specs=[full_spec()] * 11,
        out_specs=[pl.BlockSpec(memory_space=pl.ANY)] * 7 + [full_spec()] * 5,
        out_shape=[
            head,
            head,
            head,
            shape((width, tokens), BF),
            shape((half, width), F32),
            shape((half, columns), BF),
            shape(wo.shape, BF),
            shape((tokens, embed), BF),
            head,
            shape((pairs, 2, tokens), F32),
            shape((half, width), F32),
            shape((tokens, width), BF),
        ],
        scratch_shapes=[
            scratch(head.shape, BF),
            scratch(head.shape, BF),
            scratch(head.shape, BF),
            scratch((width, tokens), BF),
            scratch((half, width), F32),
            scratch((tokens, width), F32),
            scratch(rows.shape, BF),
            scratch(wo.shape, BF),
            scratch(head.shape, BF),
            scratch((2, tokens, 2 * LANES), BF),
            scratch((tokens, 2 * LANES), BF),
            scratch((LANES, tokens), BF),
            scratch((2, tokens, BLOCK), F32),
            scratch((2, tokens, BLOCK), BF),
        ]
        + [pltpu.SemaphoreType.DMA((count + 2,)) for _ in range(2)]
        + [pltpu.SemaphoreType.DMA((pairs,)) for _ in range(2)]
        + [pltpu.SemaphoreType.DMA((7,))],
        compiler_params=pltpu.CompilerParams(
            vmem_limit_bytes=VMEM_LIMIT, collective_id=collective_id, has_side_effects=True
        ),
        name="front",
    )(rows, noise, scales, w_in, vectors, wq, wk, wv, fq, fk, wo)


class Gather:
    def __init__(self, place, every, sems):
        self.place, self.every, self.sems = place, every, sems

    def turn(self, step):
        return lax.rem(self.place.outer + step, self.place.outers)

    def copy(self, stage, piece, step, theirs=0):
        p = self.place
        turn = self.turn(step)
        mark = step
        if stage == 0:
            at = turn if theirs else p.outer
            part = self.every.at[at, p.mid, p.core, p.side, piece]
            peer, mark = p.at_outer(turn), at
        elif stage == 3:
            core = 1 - p.core if theirs else p.core
            part, peer = self.every.at[turn, :, core, :, piece], p.other_core()
        elif (stage == 1) == (piece % 2 == 0):
            side = 1 - p.side if theirs else p.side
            mid = slice(None) if piece % 2 else p.mid
            part, peer = self.every.at[turn, mid, p.core, side, piece], p.other_side()
        else:
            mid = 1 - p.mid if theirs else p.mid
            side = p.side if piece % 2 else slice(None)
            part, peer = self.every.at[turn, mid, p.core, side, piece], p.other_mid()
        sems = self.sems[2 * stage : 2 * stage + 2]
        return remote(part, part, sems[0].at[piece, step], sems[1].at[piece, mark], peer)


def tail_kernel(
    vocab_part,
    large,
    dq, dk, dv, n1t_in, wq, wk, wv, stream_in, hgrad_in, vectors, w_in, inputs, scales, ids, mine, sums_two,
    qkv_out, w_in_out, sides_out, noise, table,
    every, n1t, stream, hgrad, part, rpart, nsend, nrecv, stage_in, stage_out, picked, total, sums,
    src_q, src_w, src_s, side_w, side_s, *rest,
):
    early_refs, rest = rest[:9], rest[9:]
    late_refs, rest = rest[:12], rest[12:]
    gather_sems, rest = rest[:8], rest[8:]
    send_x, recv_x, send_n, recv_n, send_s, recv_s, local = rest
    width, tokens = n1t.shape
    columns = wq.shape[1]
    half = tokens // 2
    chunk, piece = 256, half // 4
    place = Place()
    outers = place.outers
    early = Scatter(place, [src_q], early_refs[0:1], early_refs[1:2], early_refs[2:3], early_refs[3:])
    late = Scatter(place, [src_w, src_s], late_refs[0:2], late_refs[2:4], late_refs[4:6], late_refs[6:])
    gather = Gather(place, every, gather_sems)
    mine_at, other_at = place.side * half, (1 - place.side) * half
    grads = Swap(place, part, rpart, send_x, recv_x)
    noises = Swap(place, nsend, nrecv, send_n, recv_n)
    loads = [
        pltpu.make_async_copy(src, dst, local.at[at])
        for at, (src, dst) in enumerate(((n1t_in, n1t), (stream_in, stream), (hgrad_in, hgrad)))
    ]
    for copy in loads:
        copy.start()
    sums[...] = jnp.zeros_like(sums)
    src_s[...] = jnp.zeros_like(src_s)
    total[...] = jnp.zeros_like(total)
    sums[2:4, :] = sums_two[...]
    greet(place, True)

    def loop(low, high, stage):
        lax.fori_loop(low, high, lambda step, carry: (stage(step), carry)[1], 0)

    def back_product(start):
        rows = rows_from(start, chunk)
        part[rows, :] = (
            times_back(dq[rows, :], wq[...])
            + times_back(dk[rows, :], wk[...])
            + times_back(dv[rows, :], wv[...])
        ).astype(BF)

    def sent(at):
        return grads.copy(at, rows_from(other_at + at * piece, piece), rows_from(at * piece, piece))

    def theirs(at):
        back_product(other_at + at * chunk)
        for step in range(chunk // piece):
            sent(at * (chunk // piece) + step).start()

    loop(0, half // chunk, theirs)
    for copy in loads:
        copy.wait()
    group = width // outers

    def weight_grads(step):
        turn = place.turn(step)
        rows = rows_from(turn * group, group)
        for at, grad in enumerate((dq, dk, dv)):
            src_q[turn, :, :, :, at * columns : (at + 1) * columns] = (
                product(n1t[rows, :], grad[...]).astype(BF).reshape(2, 2, group // 4, columns)
            )
        early.start_core(step)

    weight_grads(0)

    def more(step):
        weight_grads(step)
        early.core_to_mid(step - 1)

    loop(1, outers, more)
    loop(0, half // chunk, lambda at: back_product(mine_at + at * chunk))
    early.core_to_mid(outers - 1)

    def noise_copy(which):
        rows = pl.ds(which * piece, piece)
        return noises.copy(which, rows, rows)

    def norm_grads(which):
        sent(which).wait_recv()
        here = slice(which * piece, (which + 1) * piece)
        rows = rows_from(mine_at + which * piece, piece)
        grad = part[rows, :].astype(F32) + rpart[here, :].astype(F32)
        _, unit, inverse = normalize(stream[here, :], 1.0, 0.0)
        back, gain_sum, bias_sum = norm_back(grad, unit, inverse, vectors[0:1, :])
        low = (hgrad[here, :].astype(F32) + back).astype(BF)
        back_in = times_back(low, w_in[...])
        spot = every.at[place.outer, place.mid, place.core, place.side, which]
        found = (scales[0:1, 0:1] * back_in).astype(BF)
        if large:
            stage_out[...] = found
            moved = pltpu.make_async_copy(stage_out, spot, local.at[0])
            moved.start()
            moved.wait()
        else:
            spot[...] = found
        loop(1, outers, lambda step: gather.copy(0, which, step).start())
        gather.copy(1, which, 0).start()
        sums[0:1, :] += gain_sum[None, :]
        sums[1:2, :] += bias_sum[None, :]
        rpart[here, :] = low
        noised = (scales[0:1, 0:1] * scales[1:2, 0:1]) * back_in
        noise[rows, :] = noised
        nsend[here, :] = noised.astype(BF)

    dp_size = 4 * outers

    def start_late():
        for which in range(4):
            noise_copy(which).start()
        rows_w = w_in.shape[0] // dp_size
        lanes = width // dp_size
        work = contract_rows(inputs[...], rpart[...])
        for at in range(dp_size):
            spot = (at // 4, (at // 2) % 2, at % 2)
            src_w[spot] = work[at * rows_w : (at + 1) * rows_w, :].astype(src_w.dtype)
            src_s[spot + (slice(None), slice(0, lanes))] = sums[:, at * lanes : (at + 1) * lanes]
        loop(0, outers, late.start_core)

    def forward(stage, which, step):
        gather.copy(stage - 1, which, step, 1).wait_recv()
        gather.copy(stage, which, step).start()

    owned = table.shape[0]
    wanted = lax.broadcasted_iota(jnp.int32, (total.shape[0], 1), 0)
    first = place.side * vocab_part + place.dp * owned

    def collect(pair, step):
        turn = gather.turn(step)
        for which in (2 * pair, 2 * pair + 1):
            gather.copy(3, which, step, 1).wait_recv()
        pieces = every.at[turn, :, :, :, 2 * pair : 2 * pair + 2]
        if large:
            moved = pltpu.make_async_copy(pieces, stage_in, local.at[0])
            moved.start()
            moved.wait()
            pieces = stage_in
        for spot in range(8):
            mid, core, side = spot // 4, (spot // 2) % 2, spot % 2
            for at in range(2):
                line = 4 * side + 2 * pair + at
                lanes = slice((2 * spot + at) * LANES, (2 * spot + at + 1) * LANES)
                picked[:, lanes] = ((ids[turn, mid, core, line : line + 1, :] - first) == wanted).astype(BF)
        total[...] += product(picked[...], pieces[...].reshape(16 * piece, -1))

    sided = []
    for slot in range(8):
        if slot < 4:
            norm_grads(slot)
            last = slot == 3
            loop(
                slot * outers // 4,
                (slot + 1) * outers // 4 - last,
                lambda step: early.mid_to_outer(step, False),
            )
            if last:
                early.mid_to_outer(outers - 1, True)
                start_late()
        if 1 <= slot < 5:
            loop(1, outers, lambda step: forward(1, slot - 1, step))
            forward(2, slot - 1, 0)
        if 2 <= slot < 6:
            loop(1, outers, lambda step: forward(2, slot - 2, step))
            forward(3, slot - 2, 0)
        if 3 <= slot < 7:
            loop(1, outers, lambda step: forward(3, slot - 3, step))
        if slot == 4:
            loop(0, outers, late.core_to_mid)
        if slot == 5:
            loop(0, outers, lambda step: collect(0, step))
            loop(0, outers - 1, lambda step: late.mid_to_outer(step, False))
            late.mid_to_outer(outers - 1, True)
            early.finish([qkv_out])
        if slot == 6:
            late.finish([w_in_out, sides_out])
            for at, (out, buffer) in enumerate(((w_in_out, side_w), (sides_out, side_s))):
                buffer[0] = out[...]
                sided.append(remote(buffer.at[0], buffer.at[1], send_s.at[at], recv_s.at[at], place.other_side()))
                sided[at].start()
        if slot == 7:
            loop(0, outers, lambda step: collect(1, step))
    for which in range(4):
        noise_copy(which).wait()
    noise[rows_from(other_at, half), :] = nrecv[...].astype(F32)
    mine_rows = mine[...].astype(F32)
    scale = row_scale(mine_rows)
    grad = total[...][:owned]
    table[...] = scale * grad - mine_rows * (scale * scale * scale) * jnp.mean(
        grad * mine_rows, axis=1, keepdims=True
    )
    for at, (out, buffer) in enumerate(((w_in_out, side_w), (sides_out, side_s))):
        sided[at].wait()
        out[...] = out[...] + buffer[1]
    early.drain()
    late.drain()
    loop(0, half // piece, lambda at: sent(at).wait_send())

    def done(step):
        for which in range(4):
            for stage in range(1, 4):
                gather.copy(stage, which, step).wait_send()

    loop(0, outers, done)

    def done_outer(step):
        for which in range(4):
            gather.copy(0, which, step).wait_send()

    loop(1, outers, done_outer)


def tail(vocab_part, dp_size, collective_id, *operands):
    (_, _, _, n1t, wq, _, _, stream, _, _, w_in, _, _, _, mine, _) = operands
    width, tokens = n1t.shape
    columns = wq.shape[1]
    half = tokens // 2
    piece = half // 4
    outers = dp_size // 4
    embed = w_in.shape[0]
    owned = mine.shape[0]
    padded = -(-owned // LANES) * LANES
    large = outers > 4
    every_shape = (outers, 2, 2, 2, 4, piece, embed)
    anywhere = pl.BlockSpec(memory_space=pl.ANY)

    def blocks_of(rows, cols, dtype):
        return jax.ShapeDtypeStruct((outers, 2, 2, rows, cols), dtype)

    src_q = blocks_of(width // dp_size, 3 * columns, BF)
    src_w = blocks_of(embed // dp_size, width, F32 if embed // dp_size % 16 else BF)
    src_s = blocks_of(8, LANES, F32)

    def owned_shape(value):
        return jax.ShapeDtypeStruct(value.shape[3:], F32)

    def scratch(shape, dtype):
        return pltpu.VMEM(shape, dtype)

    return pl.pallas_call(
        functools.partial(tail_kernel, vocab_part, large),
        in_specs=[anywhere if at in (3, 7, 8) else full_spec() for at in range(len(operands))],
        out_specs=[full_spec()] * 5 + ([anywhere] if large else []),
        out_shape=[
            owned_shape(src_q),
            owned_shape(src_w),
            owned_shape(src_s),
            jax.ShapeDtypeStruct((tokens, embed), F32),
            jax.ShapeDtypeStruct((owned, embed), F32),
        ]
        + ([jax.ShapeDtypeStruct(every_shape, BF)] if large else []),
        scratch_shapes=([] if large else [scratch(every_shape, BF)])
        + [
            scratch(n1t.shape, BF),
            scratch(stream.shape, F32),
            scratch(stream.shape, BF),
            scratch((tokens, width), BF),
            scratch((half, width), BF),
            scratch((half, embed), BF),
            scratch((half, embed), BF),
            scratch((2, 2, 2, 2, piece, embed) if large else (16, LANES), BF),
            scratch((piece, embed) if large else (16, LANES), BF),
            scratch((padded, 16 * piece), BF),
            scratch((padded, embed), F32),
            scratch((8, width), F32),
            scratch(src_q.shape, BF),
            scratch(src_w.shape, src_w.dtype),
            scratch(src_s.shape, F32),
            scratch((2,) + src_w.shape[3:], F32),
            scratch((2,) + src_s.shape[3:], F32),
        ]
        + scatter_shapes([src_q])
        + scatter_shapes([src_w, src_s])
        + [pltpu.SemaphoreType.DMA((4, outers)) for _ in range(8)]
        + [pltpu.SemaphoreType.DMA((4,)) for _ in range(4)]
        + [pltpu.SemaphoreType.DMA((2,)) for _ in range(2)]
        + [pltpu.SemaphoreType.DMA((3,))],
        compiler_params=pltpu.CompilerParams(
            vmem_limit_bytes=VMEM_LIMIT, collective_id=collective_id, has_side_effects=True
        ),
        name="tail",
    )(*operands)


def results_kernel(columns, layer, noise, table, w_in, qkv, wo, wu, wd, sides, alone, *refs):
    outs, sems = refs[:16], refs[16]
    sources = (
        layer, noise, table, w_in, qkv.at[:, :columns], qkv.at[:, columns : 2 * columns], qkv.at[:, 2 * columns :], wo, wu, wd,
    )
    copies = [pltpu.make_async_copy(src, dst, sems.at[at]) for at, (src, dst) in enumerate(zip(sources, outs[:10]))]
    for copy in copies:
        copy.start()
    for at in range(4):
        outs[10 + at][...] = sides[at, : outs[10 + at].shape[0]]
    for at in range(2):
        outs[14 + at][...] = alone[at, : outs[14 + at].shape[0]]
    for copy in copies:
        copy.wait()


def results(layer, noise, table, w_in, qkv, wo, wu, wd, sides, alone, small, bias_up_size):
    columns = qkv.shape[1] // 3
    shape = jax.ShapeDtypeStruct
    head = shape((qkv.shape[0], columns), F32)
    large = [layer, noise, table, w_in, head, head, head, wo, wu, wd]
    anywhere = pl.BlockSpec(memory_space=pl.ANY)
    return pl.pallas_call(
        functools.partial(results_kernel, columns),
        in_specs=[full_spec()] * 10,
        out_specs=[anywhere] * 10 + [full_spec()] * 6,
        out_shape=[shape(value.shape, value.dtype) for value in large]
        + [shape((small,), F32)] * 4
        + [shape((bias_up_size,), F32), shape((small,), F32)],
        scratch_shapes=[pltpu.SemaphoreType.DMA((10,))],
        name="results",
    )(layer, noise, table, w_in, qkv, wo, wu, wd, sides, alone)


def on_device(
    token_ids,
    segment_ids,
    time_index,
    noise_vec,
    embed_table,
    w_in,
    norm1_gain,
    norm1_bias,
    w_query,
    w_key,
    w_value,
    w_out,
    norm2_gain,
    norm2_bias,
    w_up,
    bias_up,
    w_down,
    bias_down,
    cotangent,
):
    seq_count, length = segment_ids.shape
    tokens = seq_count * length
    half = tokens // 2
    vocab_part = embed_table.shape[0]
    dp_size = lax.axis_size("dp")
    dp_index = lax.axis_index("dp")
    side = lax.axis_index("mp")
    mine_at = side * half

    def own(value):
        return lax.dynamic_slice_in_dim(value, mine_at, half, 0)

    vectors = jnp.stack([norm1_gain, norm1_bias, norm2_gain, norm2_bias, bias_down]).astype(F32)
    fq, fk = lax.optimization_barrier(attention_masks(segment_ids[0]))
    level_step = jnp.log(time_high / time_low) / (TLEVELS - 1)
    level = time_low * jnp.exp(time_index.astype(F32) * level_step)
    scales = jnp.stack([lax.rsqrt(1.0 + level * level), level])
    rows = gather_rows(token_ids - side * vocab_part, embed_table)
    (
        queries, key_rows, value_rows, normed_one_t, stream_half, mixed_other, w_out_other, inputs_low, mixed_low, log_total, hidden_half, normed_two,
    ) = front(
        rows, noise_vec, scales, w_in, vectors, w_query, w_key, w_value, fq, fk, w_out, 3,
    )
    (
        every_id, layer_out, hidden_grad, norm_two_sums, w_out_grad, w_down_grad, w_up_grad, alone_grad,
        query_grad, key_grad, value_grad,
    ) = feed_forward(
        dp_size, 1, token_ids.reshape(-1, LANES), normed_two, cotangent, w_up, bias_up.astype(F32)[None, :], w_down,
        hidden_half, vectors, w_out, mixed_low, queries, key_rows, value_rows, log_total, fq, fk, mixed_other, w_out_other,
    )
    owned = vocab_part // dp_size
    mine = lax.dynamic_slice_in_dim(embed_table, dp_index * owned, owned, 0)
    qkv_grad, w_in_grad, sides_grad, noise_grad, table_grad, *_ = tail(
        vocab_part, dp_size, 2, query_grad, key_grad, value_grad, normed_one_t, w_query, w_key, w_value,
        stream_half, hidden_grad, vectors, w_in, own(inputs_low), scales, every_id, mine,
        norm_two_sums,
    )
    width = bias_down.shape[0] // dp_size
    (
        layer, noise, table, w_in_sum, query_sum, key_sum, value_sum, w_out_sum, w_up_sum, w_down_sum,
        gain_one_sum, bias_one_sum, gain_two_sum, bias_two_sum, bias_up_sum, bias_down_sum,
    ) = results(
        layer_out, noise_grad, table_grad, w_in_grad, qkv_grad, w_out_grad, w_up_grad, w_down_grad,
        sides_grad, alone_grad, width, bias_up.shape[0] // dp_size,
    )
    return (
        layer, noise, table, w_in_sum, gain_one_sum, bias_one_sum, query_sum, key_sum, value_sum, w_out_sum,
        gain_two_sum, bias_two_sum, w_up_sum, bias_up_sum, w_down_sum, bias_down_sum,
    )


def solution(mesh):
    placed = (
        P("dp"),
        P("dp", None),
        P("dp"),
        P("dp", None),
        P("mp", None),
        P(),
        P(),
        P(),
        P(None, "mp"),
        P(None, "mp"),
        P(None, "mp"),
        P("mp", None),
        P(),
        P(),
        P(None, "mp"),
        P("mp"),
        P("mp", None),
        P(),
        P("dp", None),
    )
    return jax.shard_map(
        on_device,
        mesh=mesh,
        in_specs=placed,
        out_specs=(
            P("dp", None),
            P("dp", None),
            P(("mp", "dp"), None),
            P("dp", None),
            P("dp"),
            P("dp"),
            P("dp", "mp"),
            P("dp", "mp"),
            P("dp", "mp"),
            P(("mp", "dp"), None),
            P("dp"),
            P("dp"),
            P("dp", "mp"),
            P(("mp", "dp")),
            P(("mp", "dp"), None),
            P("dp"),
        ),
        check_vma=False,
    )
```

```python
import functools

import jax
import jax.numpy as jnp
from jax import lax
from jax.experimental import pallas as pl
from jax.experimental.pallas import tpu as pltpu
from jax.sharding import PartitionSpec as P

HEAD_DIM = 64
TLEVELS = 16
DOCS = 4
MAX_RUN = 512

time_low = 0.5
time_high = 10.0
norm_eps = 1e-05
table_eps = 1e-06
masked_score = -1e30

BF = jnp.bfloat16
F32 = jnp.float32
VMEM_LIMIT = 56 * 1024 * 1024
BLOCK = 256
STRIP = 64
LANES = 128


def to_bf16(value):
    return value.astype(BF)


def product(left, right):
    return jnp.dot(left, right, preferred_element_type=F32)


def contract_rows(left, right):
    return lax.dot_general(left, right, (((0,), (0,)), ((), ())), preferred_element_type=F32)


def times_back(left, right):
    return lax.dot_general(left, right, (((1,), (1,)), ((), ())), preferred_element_type=F32)


def params(limit=VMEM_LIMIT):
    return pltpu.CompilerParams(vmem_limit_bytes=limit)


def cost(flops, nbytes, trans=0):
    return pl.CostEstimate(flops=int(flops), bytes_accessed=int(nbytes), transcendentals=int(trans))


def full_spec():
    return pl.BlockSpec(memory_space=pltpu.VMEM)


def row_scale(table_rows):
    return lax.rsqrt(jnp.mean(table_rows * table_rows, axis=1, keepdims=True) + table_eps)


def normalize(values, gain, bias):
    centred = values - jnp.mean(values, axis=-1, keepdims=True)
    inverse = lax.rsqrt(jnp.mean(centred * centred, axis=-1, keepdims=True) + norm_eps)
    unit_rows = centred * inverse
    return (unit_rows * gain + bias, unit_rows, inverse)


def norm_back(grad, unit_rows, inverse, gain):
    scaled = grad * gain
    spread = (
        scaled
        - jnp.mean(scaled, axis=-1, keepdims=True)
        - unit_rows * jnp.mean(scaled * unit_rows, axis=-1, keepdims=True)
    )
    return (inverse * spread, jnp.sum(grad * unit_rows, axis=0), jnp.sum(grad, axis=0))


def gather_kernel(parts, ids, table, out, staged, wide, picked, sems):
    rows, width = table.shape
    tokens = picked.shape[0]
    step = rows // parts

    def copy(part):
        span = pl.ds(part * step, step)
        return pltpu.make_async_copy(table.at[span], staged.at[span], sems.at[part])

    for part in range(parts):
        copy(part).start()
    wide[pl.ds(rows, 8), :] = jnp.zeros((8, width), F32)
    for part in range(parts):
        copy(part).wait()
        piece = step // 5

        @pl.loop(0, 5)
        def _(at):
            span = pl.ds(pl.multiple_of(part * step + at * piece, 16), piece)
            wide[span, :] = staged[span, :].astype(F32)

    def one(at, carry):
        picked[pl.ds(at, 1), :] = wide[pl.ds(ids[at], 1), :]
        return carry

    lax.fori_loop(0, tokens, one, 0, unroll=8)
    found = picked[...]
    out[...] = (found * row_scale(found)).astype(BF)


def gather_rows(local_ids, table):
    rows, width = table.shape
    local_ids = jnp.where(jnp.logical_and(local_ids >= 0, local_ids < rows), local_ids, rows)
    tokens = local_ids.shape[0]
    parts = 5
    return pl.pallas_call(
        functools.partial(gather_kernel, parts),
        grid_spec=pltpu.PrefetchScalarGridSpec(
            num_scalar_prefetch=1,
            grid=(1,),
            in_specs=[pl.BlockSpec(memory_space=pl.ANY)],
            out_specs=pl.BlockSpec((tokens, width), lambda i, ids: (0, 0)),
            scratch_shapes=[
                pltpu.VMEM((rows, width), BF),
                pltpu.VMEM((rows + 8, width), F32),
                pltpu.VMEM((tokens, width), F32),
                pltpu.SemaphoreType.DMA((parts,)),
            ],
        ),
        out_shape=jax.ShapeDtypeStruct((tokens, width), BF),
        compiler_params=params(),
        cost_estimate=cost(0, rows * width * 2),
        name="embed_rows",
    )(local_ids, table)


def head_lanes(rows, head):
    lane = lax.broadcasted_iota(jnp.int32, (rows, LANES), 1)
    return (lane // HEAD_DIM) == head


def near(block, count):
    reach = MAX_RUN // BLOCK
    return max(0, block - reach) * BLOCK, min(count, block + reach + 1) * BLOCK


def attention_masks(segment_ids):
    lane = lax.broadcasted_iota(jnp.int32, (1, LANES), 1)
    same = segment_ids[:, None] == lane
    fk = jnp.where(same, 1.0, 0.0).astype(BF)
    fq = jnp.where(jnp.logical_or(same, lane >= DOCS), 0.0, masked_score).astype(BF)
    return fq, fk


gelu_slope = 0.7978845608028654
gelu_cubic = 0.044715


MESH = pl.DeviceIdType.MESH


class Place:
    def __init__(self):
        self.dp = lax.axis_index("dp")
        self.side = lax.axis_index("mp")
        self.outers = lax.axis_size("dp") // 4
        self.outer = self.dp // 4
        self.mid = (self.dp // 2) % 2
        self.core = self.dp % 2

    def other_core(self):
        return (self.dp + 1 - 2 * self.core, self.side)

    def other_mid(self):
        return (self.dp + 2 - 4 * self.mid, self.side)

    def other_side(self):
        return (self.dp, 1 - self.side)

    def at_outer(self, outer):
        return (outer * 4 + self.mid * 2 + self.core, self.side)

    def turn(self, step):
        return lax.rem(self.outer + 1 + step, self.outers)


def greet(place, with_side):
    barrier = pltpu.get_barrier_semaphore()
    peers = [place.other_core(), place.other_mid()]
    if with_side:
        peers.append(place.other_side())
    for peer in peers:
        pl.semaphore_signal(barrier, inc=1, device_id=peer, device_id_type=MESH)
    for step in range(place.outers - 1):
        pl.semaphore_signal(
            barrier, inc=1, device_id=place.at_outer(place.turn(step)), device_id_type=MESH
        )
    pl.semaphore_wait(barrier, len(peers) + place.outers - 1)


def remote(src, dst, send, recv, device):
    return pltpu.make_async_remote_copy(
        src_ref=src, dst_ref=dst, send_sem=send, recv_sem=recv, device_id=device, device_id_type=MESH
    )


def add_into(dst, left, right):
    dst[...] = (left[...].astype(F32) + right[...].astype(F32)).astype(dst.dtype)


class Scatter:
    def __init__(self, place, sources, one, two, three, sems):
        self.place, self.sources = place, sources
        self.one, self.two, self.three = one, two, three
        self.sems = sems
        self.items = range(len(sources))

    def core_copy(self, step, item):
        p = self.place
        turn = p.turn(step)
        return remote(
            self.sources[item].at[turn, :, 1 - p.core],
            self.one[item].at[turn],
            self.sems[0].at[step, item],
            self.sems[1].at[step, item],
            p.other_core(),
        )

    def mid_copy(self, step, item):
        p = self.place
        turn = p.turn(step)
        return remote(
            self.one[item].at[turn, 1 - p.mid],
            self.two[item].at[turn],
            self.sems[2].at[step, item],
            self.sems[3].at[step, item],
            p.other_mid(),
        )

    def outer_copy(self, step, item):
        p = self.place
        turn = p.turn(step)
        return remote(
            self.two[item].at[turn],
            self.three[item].at[p.outer],
            self.sems[4].at[step, item],
            self.sems[5].at[p.outer, item],
            p.at_outer(turn),
        )

    def arrival(self, step, item):
        p = self.place
        turn = p.turn(step)
        return remote(
            self.two[item].at[turn],
            self.three[item].at[turn],
            self.sems[4].at[step, item],
            self.sems[5].at[turn, item],
            p.at_outer(turn),
        )

    def start_core(self, step):
        for item in self.items:
            self.core_copy(step, item).start()

    def core_to_mid(self, step):
        p = self.place
        turn = p.turn(step)
        for item in self.items:
            self.core_copy(step, item).wait_recv()
            one = self.one[item]
            for mid in range(2):
                add_into(one.at[turn, mid], one.at[turn, mid], self.sources[item].at[turn, mid, p.core])
            self.mid_copy(step, item).start()

    def mid_to_outer(self, step, last):
        p = self.place
        turn = p.turn(step)
        for item in self.items:
            self.mid_copy(step, item).wait_recv()
            two = self.two[item]
            add_into(two.at[turn], two.at[turn], self.one[item].at[turn, p.mid])
            if not last:
                self.outer_copy(step, item).start()

    def finish(self, outs):
        p = self.place
        for item in self.items:
            total = self.two[item][p.outer].astype(F32)
            for step in range(p.outers - 1):
                self.arrival(step, item).wait_recv()
                total = total + self.three[item][p.turn(step)].astype(F32)
            outs[item][...] = total

    def drain(self):
        def one(step, carry):
            for item in self.items:
                self.core_copy(step, item).wait_send()
                self.mid_copy(step, item).wait_send()
            return carry

        lax.fori_loop(0, self.place.outers, one, 0)
        for step in range(self.place.outers - 1):
            for item in self.items:
                self.outer_copy(step, item).wait_send()


def scatter_shapes(sources):
    one = [pltpu.VMEM((s.shape[0], 2) + s.shape[3:], s.dtype) for s in sources]
    two = [pltpu.VMEM((s.shape[0],) + s.shape[3:], s.dtype) for s in sources]
    three = [pltpu.VMEM((s.shape[0],) + s.shape[3:], s.dtype) for s in sources]
    sems = [pltpu.SemaphoreType.DMA((sources[0].shape[0], len(sources))) for _ in range(6)]
    return one + two + three + sems


class IdGather:
    def __init__(self, place, every, sems):
        self.place, self.every, self.sems = place, every, sems

    def copy(self, stage, step, theirs=0):
        p = self.place
        turn = lax.rem(p.outer + step, p.outers)
        if stage == 0:
            at = turn if theirs else p.outer
            part, peer, mark = self.every.at[at, p.mid, p.core], p.at_outer(turn), at
        elif stage == 1:
            mid = 1 - p.mid if theirs else p.mid
            part, peer, mark = self.every.at[turn, mid, p.core], p.other_mid(), step
        else:
            core = 1 - p.core if theirs else p.core
            part, peer, mark = self.every.at[turn, :, core], p.other_core(), step
        return remote(part, part, self.sems[2 * stage].at[step], self.sems[2 * stage + 1].at[mark], peer)


class Swap:
    def __init__(self, place, src, dst, send, recv):
        self.place, self.src, self.dst, self.send, self.recv = place, src, dst, send, recv

    def copy(self, at, src_rows, dst_rows):
        return remote(
            self.src.at[src_rows], self.dst.at[dst_rows], self.send.at[at], self.recv.at[at], self.place.other_side()
        )


def rows_from(start, size):
    return pl.ds(pl.multiple_of(start, size), size)


def feed_forward_kernel(
    ids, x_in, cot, wu_in, bu, wd_in, hidden, vectors, wo_in, mixed, q_in, k_in, v_in, lse, fq_ref, fk_ref, others,
    wo_other_in, every, layer, hg, norm_sums, wo_out, dwd_out, dwu_out, alone_out, dq_out, dk_out, dv_out,
    act_t, ug, xt, xg, rg, mgs, mgr, wu, wd, dbu, dbd, qs, ks, kt, gs, delta, scores, slopes,
    wo_sum, wo_recv, src_d, src_u, src_a, src_o, *rest,
):
    scatter_refs, rest = rest[:15], rest[15:]
    out_refs, rest = rest[:9], rest[9:]
    id_sems, (send_x, recv_x, send_h, recv_h, send_d, recv_d, send_l, recv_l, local) = rest[:6], rest[6:]
    tokens, width = x_in.shape
    features = wu.shape[1]
    columns = wo_in.shape[0]
    x = layer
    wo, wo_other = layer.at[:columns], layer.at[columns : 2 * columns]
    gain, bd = vectors[2:3, :], vectors[4:5, :]
    half = tokens // 2
    chunk, part, piece = 256, 512, 128
    place = Place()
    outers = place.outers
    work = Scatter(
        place, [src_d, src_u, src_a], scatter_refs[0:3], scatter_refs[3:6], scatter_refs[6:9], scatter_refs[9:]
    )
    after = Scatter(place, [src_o], out_refs[0:1], out_refs[1:2], out_refs[2:3], out_refs[3:])
    known = IdGather(place, every, id_sems)
    every[place.outer, place.mid, place.core] = ids[...]
    mine_at, other_at = place.side * half, (1 - place.side) * half
    grads = Swap(place, xg, rg, send_x, recv_x)
    mixes = Swap(place, mgs, mgr, send_h, recv_h)
    downs = Swap(place, xg, rg, send_d, recv_d)
    layers = Swap(place, layer, layer, send_l, recv_l)
    dbu[...] = jnp.zeros_like(dbu)
    dbd[...] = jnp.zeros_like(dbd)
    src_a[...] = jnp.zeros_like(src_a)
    norm_sums[...] = jnp.zeros_like(norm_sums)
    loads = [
        pltpu.make_async_copy(src, dst, local.at[at])
        for at, (src, dst) in enumerate(((x_in, x), (wu_in, wu), (wd_in, wd)))
    ]
    for copy in loads:
        copy.start()
    greet(place, True)
    for copy in loads:
        copy.wait()

    def loop(low, high, stage):
        lax.fori_loop(low, high, lambda step, carry: (stage(step), carry)[1], 0)

    def ids_mid(step):
        known.copy(0, step, 1).wait_recv()
        known.copy(1, step).start()

    def ids_core(step):
        known.copy(1, step, 1).wait_recv()
        known.copy(2, step).start()

    loop(1, outers, lambda step: known.copy(0, step).start())
    known.copy(1, 0).start()

    def forward(start):
        rows = rows_from(start, chunk)
        xc = x[rows, :]
        gc = cot[rows, :]
        xt[:, rows] = xc.T
        dbd[...] += jnp.sum(gc.astype(F32), axis=0, keepdims=True)
        total = jnp.zeros((chunk, width), F32)
        for at in range(features // part):
            cols = slice(at * part, (at + 1) * part)
            up = product(xc, wu[:, cols]) + bu[:, cols]
            square = up * up
            gate = 0.5 + 0.5 * jnp.tanh(up * (gelu_slope + (gelu_slope * gelu_cubic) * square))
            value = up * gate
            act_t[cols, rows] = value.astype(BF).T
            slope = gate + value * (1.0 - gate) * (
                2.0 * gelu_slope + (6.0 * gelu_slope * gelu_cubic) * square
            )
            low = (times_back(gc, wd[cols, :]) * slope).astype(BF)
            ug[rows, cols] = low
            dbu[:, cols] += jnp.sum(low.astype(F32), axis=0, keepdims=True)
            total = total + times_back(low, wu[:, cols])
        xg[rows, :] = total.astype(BF)

    def sent(at):
        return grads.copy(at, rows_from(other_at + at * chunk, chunk), rows_from(at * chunk, chunk))

    def theirs(at):
        forward(other_at + at * chunk)
        sent(at).start()

    loop(0, half // chunk, theirs)
    loop(0, half // chunk, lambda at: forward(mine_at + at * chunk))
    heads_in = [
        pltpu.make_async_copy(src, wu.at[:, at * columns : (at + 1) * columns], local.at[at])
        for at, src in enumerate((q_in, k_in, v_in))
    ] + [
        pltpu.make_async_copy(src, dst, local.at[3 + at])
        for at, (src, dst) in enumerate(((wo_in, wo), (wo_other_in, wo_other)))
    ]
    for copy in heads_in:
        copy.start()
    loop(1, outers, ids_mid)
    dp_size = 4 * outers
    up_lanes, down_lanes = features // dp_size, width // dp_size
    for at in range(dp_size):
        spot = (at // 4, (at // 2) % 2, at % 2)
        src_a[spot + (slice(0, 1), slice(0, up_lanes))] = dbu[:, at * up_lanes : (at + 1) * up_lanes]
        src_a[spot + (slice(1, 2), slice(0, down_lanes))] = dbd[:, at * down_lanes : (at + 1) * down_lanes]

    down_rows, up_rows = features // outers // 2, width // outers

    def weight_grads(step):
        turn = place.turn(step)
        for mid in range(2):
            rows = rows_from(turn * (2 * down_rows) + mid * down_rows, down_rows)
            src_d[turn, mid] = product(act_t[rows, :], cot[...]).astype(BF).reshape(2, down_rows // 2, width)
        rows = rows_from(turn * up_rows, up_rows)
        for at in range(features // part):
            cols = slice(at * part, (at + 1) * part)
            src_u[turn, :, :, :, cols] = (
                product(xt[rows, :], ug[:, cols]).astype(BF).reshape(2, 2, up_rows // 4, part)
            )
        work.start_core(step)

    def norm_grads(at):
        @pl.when(at % (chunk // piece) == 0)
        def _():
            sent(at // (chunk // piece)).wait_recv()

        here = rows_from(at * piece, piece)
        rows = rows_from(mine_at + at * piece, piece)
        grad = xg[rows, :].astype(F32) + rg[here, :].astype(F32)
        _, unit, inverse = normalize(hidden[here, :], 1.0, 0.0)
        back, gain_sum, bias_sum = norm_back(grad, unit, inverse, gain)
        norm_sums[0:1, :] += gain_sum[None, :]
        norm_sums[1:2, :] += bias_sum[None, :]
        total = cot[rows, :].astype(F32) + back
        hg[here, :] = total.astype(BF)

    def mix_copy(at):
        here = rows_from(at * chunk, chunk)
        return mixes.copy(at, here, here)

    def mixed_grads(at):
        here = rows_from(at * chunk, chunk)
        mgs[here, :] = times_back(hg[here, :], wo_other[...]).astype(BF)
        mix_copy(at).start()
        wu[rows_from(mine_at + at * chunk, chunk), 3 * columns :] = times_back(hg[here, :], wo[...]).astype(BF)

    weight_grads(0)
    weight_grads(1)
    work.core_to_mid(0)
    loop(0, half // piece, norm_grads)
    for copy in heads_in:
        copy.wait()
    loop(0, half // chunk, mixed_grads)
    rows_o = columns // dp_size
    turned = (mixed[rows_from(mine_at, half), :].T, others[...].T)
    for which in range(2):
        for at in range(0, width, BLOCK):
            src_o[:, :, :, which * rows_o : (which + 1) * rows_o, at : at + BLOCK] = (
                product(turned[which], hg[:, at : at + BLOCK]).astype(BF).reshape(outers, 2, 2, rows_o, BLOCK)
            )
    loop(0, outers, after.start_core)

    def more(step):
        weight_grads(step)
        work.core_to_mid(step - 1)

    loop(2, outers, more)
    work.core_to_mid(outers - 1)
    loop(0, outers, after.core_to_mid)
    loop(0, half // chunk, lambda at: sent(at).wait_send())

    def downward(start):
        rows = rows_from(start, chunk)
        xg[rows, :] = contract_rows(act_t[:, rows], wd[...]).astype(BF)

    def down_sent(at):
        return downs.copy(at, rows_from(other_at + at * piece, piece), rows_from(at * piece, piece))

    def down_theirs(at):
        downward(other_at + at * chunk)
        mix_copy(at).wait_recv()

    loop(0, half // chunk, down_theirs)
    loop(0, half // piece, lambda at: down_sent(at).start())
    wu[rows_from(other_at, half), 3 * columns :] = mgr[...]
    loop(0, half // chunk, lambda at: downward(mine_at + at * chunk))
    loop(0, outers, ids_core)
    loop(0, outers - 3, lambda step: work.mid_to_outer(step, False))

    def layer_copy(at, start):
        rows = rows_from(start + at * piece, piece)
        return layers.copy(at, rows, rows)

    def layer_rows(at):
        down_sent(at).wait_recv()
        here = rows_from(at * piece, piece)
        rows = rows_from(mine_at + at * piece, piece)
        layer[rows, :] = (
            hidden[here, :] + (xg[rows, :].astype(F32) + rg[here, :].astype(F32)) + bd
        ).astype(BF)
        layer_copy(at, mine_at).start()

    blocks = tokens // BLOCK
    scale = HEAD_DIM**-0.5

    def one_pair(at):
        def lanes_of(which):
            return pl.ds(pl.multiple_of(which * columns + at * LANES, LANES), LANES)

        keys, grad = wu[:, lanes_of(1)], wu[:, lanes_of(3)]
        scaled = (wu[:, lanes_of(0)].astype(F32) * scale).astype(BF)
        for head in range(2):
            mine = head_lanes(tokens, head)
            qs[head, :, :LANES] = jnp.where(mine, scaled, jnp.zeros_like(scaled))
            qs[head, :, LANES:] = fq_ref[...]
            gs[head] = jnp.where(mine, grad, jnp.zeros_like(grad))
        ks[:, :LANES] = keys
        ks[:, LANES:] = fk_ref[...]
        kt[...] = keys.T
        both = (grad.astype(F32) * mixed[:, lanes_of(0)].astype(F32)).T
        for head in range(2):
            delta[head : head + 1, :] = jnp.sum(
                both[head * HEAD_DIM : (head + 1) * HEAD_DIM], axis=0, keepdims=True
            )
        for block in range(blocks):
            here = slice(block * BLOCK, (block + 1) * BLOCK)
            low, high = near(block, blocks)
            dq = []
            for head in range(2):
                scores[head, low:high, :] = times_back(ks[low:high, :], qs[head, here, :])
                slopes[head, low:high, :] = times_back(wu[low:high, lanes_of(2)], gs[head, here, :])
            for head in range(2):
                offset, shift = lse[at, head : head + 1, here], delta[head : head + 1, here]
                columns_here = slice(head * tokens + block * BLOCK, head * tokens + (block + 1) * BLOCK)
                for at_key in range(low, high, STRIP):
                    strip = slice(at_key, at_key + STRIP)
                    prob = jnp.exp(scores[head, strip, :] - offset)
                    act_t[head * tokens + at_key : head * tokens + at_key + STRIP, here] = prob.astype(BF)
                    ug[strip, columns_here] = (prob * (slopes[head, strip, :] - shift)).astype(BF)
                dq.append(product(kt[head * HEAD_DIM : (head + 1) * HEAD_DIM, low:high], ug[low:high, columns_here]))
            wd[here, lanes_of(0)] = (jnp.concatenate(dq, axis=0).T * scale).astype(BF)
        for block in range(blocks):
            here = slice(block * BLOCK, (block + 1) * BLOCK)
            low, high = near(block, blocks)
            dk = jnp.zeros((BLOCK, LANES), F32)
            dv = jnp.zeros((BLOCK, LANES), F32)
            for head in range(2):
                dv = dv + product(act_t[head * tokens + block * BLOCK : head * tokens + (block + 1) * BLOCK, low:high], gs[head, low:high, :])
                dk = dk + product(ug[here, head * tokens + low : head * tokens + high], qs[head, low:high, :LANES])
            wd[here, lanes_of(1)] = dk.astype(BF)
            wd[tokens + block * BLOCK : tokens + (block + 1) * BLOCK, lanes_of(0)] = dv.astype(BF)

        @pl.when(at < 2)
        def _():
            work.mid_to_outer(outers - 3 + at, False)

        @pl.when(at == 1)
        def _():
            loop(0, half // piece, layer_rows)

        @pl.when(at == 2)
        def _():
            work.mid_to_outer(outers - 1, True)

        @pl.when(at == 3)
        def _():
            loop(0, outers - 1, lambda step: after.mid_to_outer(step, False))
            after.mid_to_outer(outers - 1, True)

    loop(0, columns // LANES, one_pair)
    grads_out = [
        pltpu.make_async_copy(src, dst, local.at[at])
        for at, (src, dst) in enumerate(
            (
                (wd.at[:tokens, :columns], dq_out),
                (wd.at[:tokens, columns : 2 * columns], dk_out),
                (wd.at[tokens : 2 * tokens, :columns], dv_out),
            )
        )
    ]
    for copy in grads_out:
        copy.start()
    after.finish([wo_sum])
    wo_swap = remote(
        wo_sum.at[pl.ds(rows_o, rows_o)], wo_recv, send_h.at[half // chunk], recv_h.at[half // chunk], place.other_side()
    )
    wo_swap.start()
    work.finish([dwd_out, dwu_out, alone_out])
    for copy in grads_out:
        copy.wait()
    wo_swap.wait()
    wo_out[...] = wo_sum[:rows_o, :] + wo_recv[...]
    work.drain()
    after.drain()
    loop(0, outers, lambda step: known.copy(2, step, 1).wait_recv())
    loop(1, outers, lambda step: known.copy(0, step).wait_send())
    loop(0, outers, lambda step: known.copy(1, step).wait_send())
    loop(0, outers, lambda step: known.copy(2, step).wait_send())

    def swaps_done(at):
        rows = rows_from(mine_at + at * piece, piece)
        down_sent(at).wait_send()
        layer_copy(at, other_at).wait_recv()
        layer_copy(at, mine_at).wait_send()

    loop(0, half // piece, swaps_done)
    loop(0, half // chunk, lambda at: mix_copy(at).wait_send())


def feed_forward(dp_size, collective_id, *operands):
    ids, x, _, wu, _, wd, _, _, wo, _, queries, *_ = operands
    tokens, width = x.shape
    columns = wo.shape[0]
    features = wu.shape[1]
    half = tokens // 2
    outers = dp_size // 4
    shape = jax.ShapeDtypeStruct
    items = [
        shape((outers, 2, 2, features // dp_size, width), BF),
        shape((outers, 2, 2, width // dp_size, features), BF),
        shape((outers, 2, 2, 8, LANES), F32),
    ]
    item_o = shape((outers, 2, 2, 2 * columns // dp_size, width), BF)
    anywhere = pl.BlockSpec(memory_space=pl.ANY)
    return pl.pallas_call(
        feed_forward_kernel,
        in_specs=[anywhere if at in (1, 3, 5, 8, 10, 11, 12, 17) else full_spec() for at in range(len(operands))],
        out_specs=[full_spec()] * 8 + [anywhere] * 3,
        out_shape=[
            shape((outers, 2, 2) + ids.shape, ids.dtype),
            shape((tokens, width), BF),
            shape((half, width), BF),
            shape((2, width), F32),
            shape((wo.shape[0] // dp_size, width), F32),
        ]
        + [shape(item.shape[3:], F32) for item in items]
        + [shape(queries.shape, BF)] * 3,
        scratch_shapes=[
            pltpu.VMEM((features, tokens), BF),
            pltpu.VMEM((tokens, features), BF),
            pltpu.VMEM((width, tokens), BF),
            pltpu.VMEM((tokens, width), BF),
            pltpu.VMEM((half, width), BF),
            pltpu.VMEM((half, columns), BF),
            pltpu.VMEM((half, columns), BF),
            pltpu.VMEM(wu.shape, BF),
            pltpu.VMEM(wd.shape, BF),
            pltpu.VMEM((1, features), F32),
            pltpu.VMEM((1, width), F32),
            pltpu.VMEM((2, tokens, 2 * LANES), BF),
            pltpu.VMEM((tokens, 2 * LANES), BF),
            pltpu.VMEM((LANES, tokens), BF),
            pltpu.VMEM((2, tokens, LANES), BF),
            pltpu.VMEM((2, tokens), F32),
            pltpu.VMEM((2, tokens, BLOCK), F32),
            pltpu.VMEM((2, tokens, BLOCK), F32),
            pltpu.VMEM(item_o.shape[3:], F32),
            pltpu.VMEM((columns // dp_size, width), F32),
        ]
        + [pltpu.VMEM(item.shape, item.dtype) for item in items + [item_o]]
        + scatter_shapes(items)
        + scatter_shapes([item_o])
        + [pltpu.SemaphoreType.DMA((outers,)) for _ in range(6)]
        + [pltpu.SemaphoreType.DMA((half // 256,)) for _ in range(2)]
        + [pltpu.SemaphoreType.DMA((half // 128,)) for _ in range(6)]
        + [pltpu.SemaphoreType.DMA((5,))],
        compiler_params=pltpu.CompilerParams(
            vmem_limit_bytes=60 * 1024 * 1024, collective_id=collective_id, has_side_effects=True
        ),
        name="feed_forward",
    )(*operands)


def front_kernel(
    rows_ref, noise, scales, w_in, vectors, wq, wk, wv, fq_ref, fk_ref, wo,
    q_out, k_out, v_out, n1t_out, stream_out, others_out, wo_out, inputs_out, mixed, lse, hidden_out, x2,
    q, k, v, n1t, stream_own, stream, theirs, wo_other, others, qs, ks, vt, scores, probs, inputs,
    send_r, recv_r, send_m, recv_m, local,
):
    tokens, width = stream.shape
    half = tokens // 2
    chunk = 256
    pairs = q.shape[1] // LANES
    place = Place()
    mine_at = place.side * half
    barrier = pltpu.get_barrier_semaphore()
    for peer in (place.other_side(), place.other_core()):
        pl.semaphore_signal(barrier, inc=1, device_id=peer, device_id_type=MESH)
    pl.semaphore_wait(barrier, 2)

    def loop(low, high, stage):
        lax.fori_loop(low, high, lambda step, carry: (stage(step), carry)[1], 0)

    def row_copy(at):
        span = rows_from(at * chunk, chunk)
        return remote(rows_ref.at[span], theirs.at[span], send_r.at[at], recv_r.at[at], place.other_side())

    count = tokens // chunk
    part = wo.shape[0] // 2

    def weights(step):
        rows = rows_from(place.core * part, part)
        src = wo_other if step else wo
        peer = place.other_core() if step else place.other_side()
        return remote(src.at[rows], wo_other.at[rows], send_r.at[count + step], recv_r.at[count + step], peer)

    loop(0, count, lambda at: row_copy(at).start())
    weights(0).start()

    def start_of(at):
        row_copy(at).wait_recv()
        span = rows_from(at * chunk, chunk)
        embedded = rows_ref[span, :].astype(F32) + theirs[span, :].astype(F32)
        low = (scales[0:1, 0:1] * (embedded + scales[1:2, 0:1] * noise[span, :].astype(F32))).astype(BF)
        inputs[span, :] = low
        flow = product(low, w_in[...])
        stream[span, :] = flow
        normed, _, _ = normalize(flow, vectors[0:1, :], vectors[1:2, :])
        normed = normed.astype(BF)
        n1t[:, span] = normed.T
        q[span, :] = product(normed, wq[...]).astype(BF)
        k[span, :] = product(normed, wk[...]).astype(BF)
        v[span, :] = product(normed, wv[...]).astype(BF)

    loop(0, count, start_of)

    def keep(at):
        span = rows_from(at * chunk, chunk)
        stream_own[span, :] = stream[rows_from(mine_at + at * chunk, chunk), :]

    loop(0, half // chunk, keep)
    kept = [
        pltpu.make_async_copy(src, dst, local.at[at])
        for at, (src, dst) in enumerate(
            ((q, q_out), (k, k_out), (v, v_out), (n1t, n1t_out), (stream_own, stream_out))
        )
    ]
    for copy in kept:
        copy.start()

    blocks = tokens // BLOCK
    scale = HEAD_DIM**-0.5

    def pair_copy(at):
        lanes = pl.ds(pl.multiple_of(at * LANES, LANES), LANES)
        return remote(mixed.at[:, lanes], others.at[:, lanes], send_m.at[at], recv_m.at[at], place.other_side())

    def one_pair(at):
        lanes = pl.ds(pl.multiple_of(at * LANES, LANES), LANES)
        scaled = (q[:, lanes].astype(F32) * scale).astype(BF)
        for head in range(2):
            qs[head, :, :LANES] = jnp.where(head_lanes(tokens, head), scaled, jnp.zeros_like(scaled))
            qs[head, :, LANES:] = fq_ref[...]
        ks[:, :LANES] = k[:, lanes]
        ks[:, LANES:] = fk_ref[...]
        vt[...] = v[:, lanes].T
        for block in range(blocks):
            here = slice(block * BLOCK, (block + 1) * BLOCK)
            low, high = near(block, blocks)
            found = []
            for head in range(2):
                scores[head, low:high, :] = times_back(ks[low:high, :], qs[head, here, :])
            for head in range(2):
                peak = jnp.full((8, BLOCK), masked_score, F32)
                for at_key in range(low, high, STRIP):
                    strip = scores[head, at_key : at_key + STRIP, :].reshape(STRIP // 8, 8, BLOCK)
                    peak = jnp.maximum(peak, jnp.max(strip, axis=0))
                peak = jnp.max(peak, axis=0, keepdims=True)
                total = jnp.zeros((8, BLOCK), F32)
                for at_key in range(low, high, STRIP):
                    strip = jnp.exp(scores[head, at_key : at_key + STRIP, :] - peak)
                    total = total + jnp.sum(strip.reshape(STRIP // 8, 8, BLOCK), axis=0)
                    probs[head, at_key : at_key + STRIP, :] = strip.astype(BF)
                total = jnp.sum(total, axis=0, keepdims=True)
                values = vt[head * HEAD_DIM : (head + 1) * HEAD_DIM, low:high]
                found.append(product(values, probs[head, low:high, :]) / total)
                lse[at, head : head + 1, here] = peak + jnp.log(total)
            mixed[here, lanes] = jnp.concatenate(found, axis=0).T.astype(BF)
        pair_copy(at).start()

        @pl.when(at == 1)
        def _():
            weights(0).wait_recv()
            weights(1).start()

    loop(0, pairs, one_pair)

    def ours(at):
        span = rows_from(at * chunk, chunk)
        stream[span, :] += product(mixed[span, :], wo[...])

    loop(0, count, ours)
    weights(1).wait_recv()
    loop(0, pairs, lambda at: pair_copy(at).wait_recv())
    kept += [
        pltpu.make_async_copy(src, dst, local.at[5 + at])
        for at, (src, dst) in enumerate(((others.at[rows_from(mine_at, half)], others_out), (wo_other, wo_out)))
    ]
    for copy in kept[5:]:
        copy.start()

    def finish(at):
        span = rows_from(at * chunk, chunk)
        hidden = stream[span, :] + product(others[span, :], wo_other[...])
        stream[span, :] = hidden
        normed, _, _ = normalize(hidden, vectors[2:3, :], vectors[3:4, :])
        x2[span, :] = normed.astype(BF)

    loop(0, count, finish)
    hidden_out[...] = stream[rows_from(mine_at, half), :]
    inputs_out[...] = inputs[rows_from(mine_at, half), :]
    loop(0, count, lambda at: row_copy(at).wait_send())
    weights(0).wait_send()
    weights(1).wait_send()
    loop(0, pairs, lambda at: pair_copy(at).wait_send())
    for copy in kept:
        copy.wait()


def front(rows, noise, scales, w_in, vectors, wq, wk, wv, fq, fk, wo, collective_id):
    tokens, embed = rows.shape
    width, columns = wq.shape
    half = tokens // 2
    pairs = columns // LANES
    count = tokens // 256
    shape = jax.ShapeDtypeStruct
    head = shape((tokens, columns), BF)
    scratch = pltpu.VMEM
    return pl.pallas_call(
        front_kernel,
        in_specs=[full_spec()] * 11,
        out_specs=[pl.BlockSpec(memory_space=pl.ANY)] * 7 + [full_spec()] * 5,
        out_shape=[
            head,
            head,
            head,
            shape((width, tokens), BF),
            shape((half, width), F32),
            shape((half, columns), BF),
            shape(wo.shape, BF),
            shape((half, embed), BF),
            head,
            shape((pairs, 2, tokens), F32),
            shape((half, width), F32),
            shape((tokens, width), BF),
        ],
        scratch_shapes=[
            scratch(head.shape, BF),
            scratch(head.shape, BF),
            scratch(head.shape, BF),
            scratch((width, tokens), BF),
            scratch((half, width), F32),
            scratch((tokens, width), F32),
            scratch(rows.shape, BF),
            scratch(wo.shape, BF),
            scratch(head.shape, BF),
            scratch((2, tokens, 2 * LANES), BF),
            scratch((tokens, 2 * LANES), BF),
            scratch((LANES, tokens), BF),
            scratch((2, tokens, BLOCK), F32),
            scratch((2, tokens, BLOCK), BF),
            scratch(rows.shape, BF),
        ]
        + [pltpu.SemaphoreType.DMA((count + 2,)) for _ in range(2)]
        + [pltpu.SemaphoreType.DMA((pairs,)) for _ in range(2)]
        + [pltpu.SemaphoreType.DMA((7,))],
        compiler_params=pltpu.CompilerParams(
            vmem_limit_bytes=VMEM_LIMIT, collective_id=collective_id, has_side_effects=True
        ),
        name="front",
    )(rows, noise, scales, w_in, vectors, wq, wk, wv, fq, fk, wo)


class Gather:
    def __init__(self, place, every, sems):
        self.place, self.every, self.sems = place, every, sems

    def turn(self, step):
        return lax.rem(self.place.outer + step, self.place.outers)

    def copy(self, stage, piece, step, theirs=0):
        p = self.place
        turn = self.turn(step)
        mark = step
        if stage == 0:
            at = turn if theirs else p.outer
            part = self.every.at[at, p.mid, p.core, p.side, piece]
            peer, mark = p.at_outer(turn), at
        elif stage == 3:
            core = 1 - p.core if theirs else p.core
            part, peer = self.every.at[turn, :, core, :, piece], p.other_core()
        elif (stage == 1) == (piece % 2 == 0):
            side = 1 - p.side if theirs else p.side
            mid = slice(None) if piece % 2 else p.mid
            part, peer = self.every.at[turn, mid, p.core, side, piece], p.other_side()
        else:
            mid = 1 - p.mid if theirs else p.mid
            side = p.side if piece % 2 else slice(None)
            part, peer = self.every.at[turn, mid, p.core, side, piece], p.other_mid()
        sems = self.sems[2 * stage : 2 * stage + 2]
        return remote(part, part, sems[0].at[piece, step], sems[1].at[piece, mark], peer)


def tail_kernel(
    vocab_part,
    large,
    dq, dk, dv, n1t_in, wq, wk, wv, stream_in, hgrad_in, vectors, w_in, inputs, scales, ids, mine, sums_two,
    qkv_out, w_in_out, sides_out, noise, table,
    every, n1t, stream, hgrad, part, rpart, nsend, nrecv, stage_in, stage_out, picked, total, sums,
    src_q, src_w, src_s, side_w, side_s, *rest,
):
    early_refs, rest = rest[:9], rest[9:]
    late_refs, rest = rest[:12], rest[12:]
    gather_sems, rest = rest[:8], rest[8:]
    send_x, recv_x, send_n, recv_n, send_s, recv_s, local = rest
    width, tokens = n1t.shape
    columns = wq.shape[1]
    half = tokens // 2
    chunk, piece = 256, half // 4
    place = Place()
    outers = place.outers
    early = Scatter(place, [src_q], early_refs[0:1], early_refs[1:2], early_refs[2:3], early_refs[3:])
    late = Scatter(place, [src_w, src_s], late_refs[0:2], late_refs[2:4], late_refs[4:6], late_refs[6:])
    gather = Gather(place, every, gather_sems)
    mine_at, other_at = place.side * half, (1 - place.side) * half
    grads = Swap(place, part, rpart, send_x, recv_x)
    noises = Swap(place, nsend, nrecv, send_n, recv_n)
    loads = [
        pltpu.make_async_copy(src, dst, local.at[at])
        for at, (src, dst) in enumerate(((n1t_in, n1t), (stream_in, stream), (hgrad_in, hgrad)))
    ]
    for copy in loads:
        copy.start()
    sums[...] = jnp.zeros_like(sums)
    src_s[...] = jnp.zeros_like(src_s)
    total[...] = jnp.zeros_like(total)
    sums[2:4, :] = sums_two[...]
    greet(place, True)

    def loop(low, high, stage):
        lax.fori_loop(low, high, lambda step, carry: (stage(step), carry)[1], 0)

    def back_product(start):
        rows = rows_from(start, chunk)
        part[rows, :] = (
            times_back(dq[rows, :], wq[...])
            + times_back(dk[rows, :], wk[...])
            + times_back(dv[rows, :], wv[...])
        ).astype(BF)

    def sent(at):
        return grads.copy(at, rows_from(other_at + at * piece, piece), rows_from(at * piece, piece))

    def theirs(at):
        back_product(other_at + at * chunk)
        for step in range(chunk // piece):
            sent(at * (chunk // piece) + step).start()

    loop(0, half // chunk, theirs)
    for copy in loads:
        copy.wait()
    group = width // outers

    def weight_grads(step):
        turn = place.turn(step)
        rows = rows_from(turn * group, group)
        for at, grad in enumerate((dq, dk, dv)):
            src_q[turn, :, :, :, at * columns : (at + 1) * columns] = (
                product(n1t[rows, :], grad[...]).astype(BF).reshape(2, 2, group // 4, columns)
            )
        early.start_core(step)

    weight_grads(0)

    def more(step):
        weight_grads(step)
        early.core_to_mid(step - 1)

    loop(1, outers, more)
    loop(0, half // chunk, lambda at: back_product(mine_at + at * chunk))
    early.core_to_mid(outers - 1)

    def noise_copy(which):
        rows = pl.ds(which * piece, piece)
        return noises.copy(which, rows, rows)

    def norm_grads(which):
        sent(which).wait_recv()
        here = slice(which * piece, (which + 1) * piece)
        rows = rows_from(mine_at + which * piece, piece)
        grad = part[rows, :].astype(F32) + rpart[here, :].astype(F32)
        _, unit, inverse = normalize(stream[here, :], 1.0, 0.0)
        back, gain_sum, bias_sum = norm_back(grad, unit, inverse, vectors[0:1, :])
        low = (hgrad[here, :].astype(F32) + back).astype(BF)
        back_in = times_back(low, w_in[...])
        spot = every.at[place.outer, place.mid, place.core, place.side, which]
        found = (scales[0:1, 0:1] * back_in).astype(BF)
        if large:
            stage_out[...] = found
            moved = pltpu.make_async_copy(stage_out, spot, local.at[0])
            moved.start()
            moved.wait()
        else:
            spot[...] = found
        loop(1, outers, lambda step: gather.copy(0, which, step).start())
        gather.copy(1, which, 0).start()
        sums[0:1, :] += gain_sum[None, :]
        sums[1:2, :] += bias_sum[None, :]
        rpart[here, :] = low
        noised = (scales[0:1, 0:1] * scales[1:2, 0:1]) * back_in
        noise[rows, :] = noised
        nsend[here, :] = noised.astype(BF)

    dp_size = 4 * outers

    def start_late():
        for which in range(4):
            noise_copy(which).start()
        rows_w = w_in.shape[0] // dp_size
        lanes = width // dp_size
        work = contract_rows(inputs[...], rpart[...])
        for at in range(dp_size):
            spot = (at // 4, (at // 2) % 2, at % 2)
            src_w[spot] = work[at * rows_w : (at + 1) * rows_w, :].astype(src_w.dtype)
            src_s[spot + (slice(None), slice(0, lanes))] = sums[:, at * lanes : (at + 1) * lanes]
        loop(0, outers, late.start_core)

    def forward(stage, which, step):
        gather.copy(stage - 1, which, step, 1).wait_recv()
        gather.copy(stage, which, step).start()

    owned = table.shape[0]
    wanted = lax.broadcasted_iota(jnp.int32, (total.shape[0], 1), 0)
    first = place.side * vocab_part + place.dp * owned

    def collect(pair, step):
        turn = gather.turn(step)
        for which in (2 * pair, 2 * pair + 1):
            gather.copy(3, which, step, 1).wait_recv()
        pieces = every.at[turn, :, :, :, 2 * pair : 2 * pair + 2]
        if large:
            moved = pltpu.make_async_copy(pieces, stage_in, local.at[0])
            moved.start()
            moved.wait()
            pieces = stage_in
        for spot in range(8):
            mid, core, side = spot // 4, (spot // 2) % 2, spot % 2
            for at in range(2):
                line = 4 * side + 2 * pair + at
                lanes = slice((2 * spot + at) * LANES, (2 * spot + at + 1) * LANES)
                picked[:, lanes] = ((ids[turn, mid, core, line : line + 1, :] - first) == wanted).astype(BF)
        total[...] += product(picked[...], pieces[...].reshape(16 * piece, -1))

    sided = []
    for slot in range(8):
        if slot < 4:
            norm_grads(slot)
            last = slot == 3
            loop(
                slot * outers // 4,
                (slot + 1) * outers // 4 - last,
                lambda step: early.mid_to_outer(step, False),
            )
            if last:
                early.mid_to_outer(outers - 1, True)
                start_late()
        if 1 <= slot < 5:
            loop(1, outers, lambda step: forward(1, slot - 1, step))
            forward(2, slot - 1, 0)
        if 2 <= slot < 6:
            loop(1, outers, lambda step: forward(2, slot - 2, step))
            forward(3, slot - 2, 0)
        if 3 <= slot < 7:
            loop(1, outers, lambda step: forward(3, slot - 3, step))
        if slot == 4:
            loop(0, outers, late.core_to_mid)
        if slot == 5:
            loop(0, outers, lambda step: collect(0, step))
            loop(0, outers - 1, lambda step: late.mid_to_outer(step, False))
            late.mid_to_outer(outers - 1, True)
            early.finish([qkv_out])
        if slot == 6:
            late.finish([w_in_out, sides_out])
            for at, (out, buffer) in enumerate(((w_in_out, side_w), (sides_out, side_s))):
                buffer[0] = out[...]
                sided.append(remote(buffer.at[0], buffer.at[1], send_s.at[at], recv_s.at[at], place.other_side()))
                sided[at].start()
        if slot == 7:
            loop(0, outers, lambda step: collect(1, step))
    for which in range(4):
        noise_copy(which).wait()
    noise[rows_from(other_at, half), :] = nrecv[...].astype(F32)
    mine_rows = mine[...].astype(F32)
    scale = row_scale(mine_rows)
    grad = total[...][:owned]
    table[...] = scale * grad - mine_rows * (scale * scale * scale) * jnp.mean(
        grad * mine_rows, axis=1, keepdims=True
    )
    for at, (out, buffer) in enumerate(((w_in_out, side_w), (sides_out, side_s))):
        sided[at].wait()
        out[...] = out[...] + buffer[1]
    early.drain()
    late.drain()
    loop(0, half // piece, lambda at: sent(at).wait_send())

    def done(step):
        for which in range(4):
            for stage in range(1, 4):
                gather.copy(stage, which, step).wait_send()

    loop(0, outers, done)

    def done_outer(step):
        for which in range(4):
            gather.copy(0, which, step).wait_send()

    loop(1, outers, done_outer)


def tail(vocab_part, dp_size, collective_id, *operands):
    (_, _, _, n1t, wq, _, _, stream, _, _, w_in, _, _, _, mine, _) = operands
    width, tokens = n1t.shape
    columns = wq.shape[1]
    half = tokens // 2
    piece = half // 4
    outers = dp_size // 4
    embed = w_in.shape[0]
    owned = mine.shape[0]
    padded = -(-owned // LANES) * LANES
    large = outers > 4
    every_shape = (outers, 2, 2, 2, 4, piece, embed)
    anywhere = pl.BlockSpec(memory_space=pl.ANY)

    def blocks_of(rows, cols, dtype):
        return jax.ShapeDtypeStruct((outers, 2, 2, rows, cols), dtype)

    src_q = blocks_of(width // dp_size, 3 * columns, BF)
    src_w = blocks_of(embed // dp_size, width, F32 if embed // dp_size % 16 else BF)
    src_s = blocks_of(8, LANES, F32)

    def owned_shape(value):
        return jax.ShapeDtypeStruct(value.shape[3:], F32)

    def scratch(shape, dtype):
        return pltpu.VMEM(shape, dtype)

    return pl.pallas_call(
        functools.partial(tail_kernel, vocab_part, large),
        in_specs=[anywhere if at in (3, 7, 8) else full_spec() for at in range(len(operands))],
        out_specs=[full_spec()] * 5 + ([anywhere] if large else []),
        out_shape=[
            owned_shape(src_q),
            owned_shape(src_w),
            owned_shape(src_s),
            jax.ShapeDtypeStruct((tokens, embed), F32),
            jax.ShapeDtypeStruct((owned, embed), F32),
        ]
        + ([jax.ShapeDtypeStruct(every_shape, BF)] if large else []),
        scratch_shapes=([] if large else [scratch(every_shape, BF)])
        + [
            scratch(n1t.shape, BF),
            scratch(stream.shape, F32),
            scratch(stream.shape, BF),
            scratch((tokens, width), BF),
            scratch((half, width), BF),
            scratch((half, embed), BF),
            scratch((half, embed), BF),
            scratch((2, 2, 2, 2, piece, embed) if large else (16, LANES), BF),
            scratch((piece, embed) if large else (16, LANES), BF),
            scratch((padded, 16 * piece), BF),
            scratch((padded, embed), F32),
            scratch((8, width), F32),
            scratch(src_q.shape, BF),
            scratch(src_w.shape, src_w.dtype),
            scratch(src_s.shape, F32),
            scratch((2,) + src_w.shape[3:], F32),
            scratch((2,) + src_s.shape[3:], F32),
        ]
        + scatter_shapes([src_q])
        + scatter_shapes([src_w, src_s])
        + [pltpu.SemaphoreType.DMA((4, outers)) for _ in range(8)]
        + [pltpu.SemaphoreType.DMA((4,)) for _ in range(4)]
        + [pltpu.SemaphoreType.DMA((2,)) for _ in range(2)]
        + [pltpu.SemaphoreType.DMA((3,))],
        compiler_params=pltpu.CompilerParams(
            vmem_limit_bytes=VMEM_LIMIT, collective_id=collective_id, has_side_effects=True
        ),
        name="tail",
    )(*operands)


def results_kernel(columns, layer, noise, table, w_in, qkv, wo, wu, wd, sides, alone, *refs):
    outs, sems = refs[:16], refs[16]
    sources = (
        layer, noise, table, w_in, qkv.at[:, :columns], qkv.at[:, columns : 2 * columns], qkv.at[:, 2 * columns :], wo, wu, wd,
    )
    copies = [pltpu.make_async_copy(src, dst, sems.at[at]) for at, (src, dst) in enumerate(zip(sources, outs[:10]))]
    for copy in copies:
        copy.start()
    for at in range(4):
        outs[10 + at][...] = sides[at, : outs[10 + at].shape[0]]
    for at in range(2):
        outs[14 + at][...] = alone[at, : outs[14 + at].shape[0]]
    for copy in copies:
        copy.wait()


def results(layer, noise, table, w_in, qkv, wo, wu, wd, sides, alone, small, bias_up_size):
    columns = qkv.shape[1] // 3
    shape = jax.ShapeDtypeStruct
    head = shape((qkv.shape[0], columns), F32)
    large = [layer, noise, table, w_in, head, head, head, wo, wu, wd]
    anywhere = pl.BlockSpec(memory_space=pl.ANY)
    return pl.pallas_call(
        functools.partial(results_kernel, columns),
        in_specs=[full_spec()] * 10,
        out_specs=[anywhere] * 10 + [full_spec()] * 6,
        out_shape=[shape(value.shape, value.dtype) for value in large]
        + [shape((small,), F32)] * 4
        + [shape((bias_up_size,), F32), shape((small,), F32)],
        scratch_shapes=[pltpu.SemaphoreType.DMA((10,))],
        name="results",
    )(layer, noise, table, w_in, qkv, wo, wu, wd, sides, alone)


def on_device(
    token_ids,
    segment_ids,
    time_index,
    noise_vec,
    embed_table,
    w_in,
    norm1_gain,
    norm1_bias,
    w_query,
    w_key,
    w_value,
    w_out,
    norm2_gain,
    norm2_bias,
    w_up,
    bias_up,
    w_down,
    bias_down,
    cotangent,
):
    seq_count, length = segment_ids.shape
    tokens = seq_count * length
    half = tokens // 2
    vocab_part = embed_table.shape[0]
    dp_size = lax.axis_size("dp")
    dp_index = lax.axis_index("dp")
    side = lax.axis_index("mp")
    vectors = jnp.stack([norm1_gain, norm1_bias, norm2_gain, norm2_bias, bias_down]).astype(F32)
    fq, fk = lax.optimization_barrier(attention_masks(segment_ids[0]))
    level_step = jnp.log(time_high / time_low) / (TLEVELS - 1)
    level = time_low * jnp.exp(time_index.astype(F32) * level_step)
    scales = jnp.stack([lax.rsqrt(1.0 + level * level), level])
    rows = gather_rows(token_ids - side * vocab_part, embed_table)
    (
        queries, key_rows, value_rows, normed_one_t, stream_half, mixed_other, w_out_other, inputs_half, mixed_low, log_total, hidden_half, normed_two,
    ) = front(
        rows, noise_vec, scales, w_in, vectors, w_query, w_key, w_value, fq, fk, w_out, 3,
    )
    (
        every_id, layer_out, hidden_grad, norm_two_sums, w_out_grad, w_down_grad, w_up_grad, alone_grad,
        query_grad, key_grad, value_grad,
    ) = feed_forward(
        dp_size, 1, token_ids.reshape(-1, LANES), normed_two, cotangent, w_up, bias_up.astype(F32)[None, :], w_down,
        hidden_half, vectors, w_out, mixed_low, queries, key_rows, value_rows, log_total, fq, fk, mixed_other, w_out_other,
    )
    owned = vocab_part // dp_size
    mine = lax.dynamic_slice_in_dim(embed_table, dp_index * owned, owned, 0)
    qkv_grad, w_in_grad, sides_grad, noise_grad, table_grad, *_ = tail(
        vocab_part, dp_size, 2, query_grad, key_grad, value_grad, normed_one_t, w_query, w_key, w_value,
        stream_half, hidden_grad, vectors, w_in, inputs_half, scales, every_id, mine,
        norm_two_sums,
    )
    width = bias_down.shape[0] // dp_size
    (
        layer, noise, table, w_in_sum, query_sum, key_sum, value_sum, w_out_sum, w_up_sum, w_down_sum,
        gain_one_sum, bias_one_sum, gain_two_sum, bias_two_sum, bias_up_sum, bias_down_sum,
    ) = results(
        layer_out, noise_grad, table_grad, w_in_grad, qkv_grad, w_out_grad, w_up_grad, w_down_grad,
        sides_grad, alone_grad, width, bias_up.shape[0] // dp_size,
    )
    return (
        layer, noise, table, w_in_sum, gain_one_sum, bias_one_sum, query_sum, key_sum, value_sum, w_out_sum,
        gain_two_sum, bias_two_sum, w_up_sum, bias_up_sum, w_down_sum, bias_down_sum,
    )


def solution(mesh):
    placed = (
        P("dp"),
        P("dp", None),
        P("dp"),
        P("dp", None),
        P("mp", None),
        P(),
        P(),
        P(),
        P(None, "mp"),
        P(None, "mp"),
        P(None, "mp"),
        P("mp", None),
        P(),
        P(),
        P(None, "mp"),
        P("mp"),
        P("mp", None),
        P(),
        P("dp", None),
    )
    return jax.shard_map(
        on_device,
        mesh=mesh,
        in_specs=placed,
        out_specs=(
            P("dp", None),
            P("dp", None),
            P(("mp", "dp"), None),
            P("dp", None),
            P("dp"),
            P("dp"),
            P("dp", "mp"),
            P("dp", "mp"),
            P("dp", "mp"),
            P(("mp", "dp"), None),
            P("dp"),
            P("dp"),
            P("dp", "mp"),
            P(("mp", "dp")),
            P(("mp", "dp"), None),
            P("dp"),
        ),
        check_vma=False,
    )
```

```python
import functools

import jax
import jax.numpy as jnp
from jax import lax
from jax.experimental import pallas as pl
from jax.experimental.pallas import tpu as pltpu
from jax.sharding import PartitionSpec as P

HEAD_DIM = 64
TLEVELS = 16
DOCS = 4
MAX_RUN = 512

time_low = 0.5
time_high = 10.0
norm_eps = 1e-05
table_eps = 1e-06
masked_score = -1e30

BF = jnp.bfloat16
F32 = jnp.float32
VMEM_LIMIT = 56 * 1024 * 1024
BLOCK = 256
STRIP = 64
LANES = 128


def to_bf16(value):
    return value.astype(BF)


def product(left, right):
    return jnp.dot(left, right, preferred_element_type=F32)


def contract_rows(left, right):
    return lax.dot_general(left, right, (((0,), (0,)), ((), ())), preferred_element_type=F32)


def times_back(left, right):
    return lax.dot_general(left, right, (((1,), (1,)), ((), ())), preferred_element_type=F32)


def params(limit=VMEM_LIMIT):
    return pltpu.CompilerParams(vmem_limit_bytes=limit)


def cost(flops, nbytes, trans=0):
    return pl.CostEstimate(flops=int(flops), bytes_accessed=int(nbytes), transcendentals=int(trans))


def full_spec():
    return pl.BlockSpec(memory_space=pltpu.VMEM)


def row_scale(table_rows):
    return lax.rsqrt(jnp.mean(table_rows * table_rows, axis=1, keepdims=True) + table_eps)


def normalize(values, gain, bias):
    centred = values - jnp.mean(values, axis=-1, keepdims=True)
    inverse = lax.rsqrt(jnp.mean(centred * centred, axis=-1, keepdims=True) + norm_eps)
    unit_rows = centred * inverse
    return (unit_rows * gain + bias, unit_rows, inverse)


def norm_back(grad, unit_rows, inverse, gain):
    scaled = grad * gain
    spread = (
        scaled
        - jnp.mean(scaled, axis=-1, keepdims=True)
        - unit_rows * jnp.mean(scaled * unit_rows, axis=-1, keepdims=True)
    )
    return (inverse * spread, jnp.sum(grad * unit_rows, axis=0), jnp.sum(grad, axis=0))


def gather_kernel(parts, ids, table, out, staged, wide, picked, sems):
    rows, width = table.shape
    tokens = picked.shape[0]
    step = rows // parts

    def copy(part):
        span = pl.ds(part * step, step)
        return pltpu.make_async_copy(table.at[span], staged.at[span], sems.at[part])

    for part in range(parts):
        copy(part).start()
    wide[pl.ds(rows, 8), :] = jnp.zeros((8, width), F32)
    for part in range(parts):
        copy(part).wait()
        piece = step // 5

        @pl.loop(0, 5)
        def _(at):
            span = pl.ds(pl.multiple_of(part * step + at * piece, 16), piece)
            wide[span, :] = staged[span, :].astype(F32)

    def one(at, carry):
        picked[pl.ds(at, 1), :] = wide[pl.ds(ids[at], 1), :]
        return carry

    lax.fori_loop(0, tokens, one, 0, unroll=8)
    found = picked[...]
    out[...] = (found * row_scale(found)).astype(BF)


def gather_rows(local_ids, table):
    rows, width = table.shape
    local_ids = jnp.where(jnp.logical_and(local_ids >= 0, local_ids < rows), local_ids, rows)
    tokens = local_ids.shape[0]
    parts = 5
    return pl.pallas_call(
        functools.partial(gather_kernel, parts),
        grid_spec=pltpu.PrefetchScalarGridSpec(
            num_scalar_prefetch=1,
            grid=(1,),
            in_specs=[pl.BlockSpec(memory_space=pl.ANY)],
            out_specs=pl.BlockSpec((tokens, width), lambda i, ids: (0, 0)),
            scratch_shapes=[
                pltpu.VMEM((rows, width), BF),
                pltpu.VMEM((rows + 8, width), F32),
                pltpu.VMEM((tokens, width), F32),
                pltpu.SemaphoreType.DMA((parts,)),
            ],
        ),
        out_shape=jax.ShapeDtypeStruct((tokens, width), BF),
        compiler_params=params(),
        cost_estimate=cost(0, rows * width * 2),
        name="embed_rows",
    )(local_ids, table)


def head_lanes(rows, head):
    lane = lax.broadcasted_iota(jnp.int32, (rows, LANES), 1)
    return (lane // HEAD_DIM) == head


def near(block, count):
    reach = MAX_RUN // BLOCK
    return max(0, block - reach) * BLOCK, min(count, block + reach + 1) * BLOCK


def attention_masks(segment_ids):
    lane = lax.broadcasted_iota(jnp.int32, (1, LANES), 1)
    same = segment_ids[:, None] == lane
    fk = jnp.where(same, 1.0, 0.0).astype(BF)
    fq = jnp.where(jnp.logical_or(same, lane >= DOCS), 0.0, masked_score).astype(BF)
    return fq, fk


gelu_slope = 0.7978845608028654
gelu_cubic = 0.044715


MESH = pl.DeviceIdType.MESH


class Place:
    def __init__(self):
        self.dp = lax.axis_index("dp")
        self.side = lax.axis_index("mp")
        self.outers = lax.axis_size("dp") // 4
        self.outer = self.dp // 4
        self.mid = (self.dp // 2) % 2
        self.core = self.dp % 2

    def other_core(self):
        return (self.dp + 1 - 2 * self.core, self.side)

    def other_mid(self):
        return (self.dp + 2 - 4 * self.mid, self.side)

    def other_side(self):
        return (self.dp, 1 - self.side)

    def at_outer(self, outer):
        return (outer * 4 + self.mid * 2 + self.core, self.side)

    def turn(self, step):
        return lax.rem(self.outer + 1 + step, self.outers)


def greet(place, with_side):
    barrier = pltpu.get_barrier_semaphore()
    peers = [place.other_core(), place.other_mid()]
    if with_side:
        peers.append(place.other_side())
    for peer in peers:
        pl.semaphore_signal(barrier, inc=1, device_id=peer, device_id_type=MESH)
    for step in range(place.outers - 1):
        pl.semaphore_signal(
            barrier, inc=1, device_id=place.at_outer(place.turn(step)), device_id_type=MESH
        )
    pl.semaphore_wait(barrier, len(peers) + place.outers - 1)


def remote(src, dst, send, recv, device):
    return pltpu.make_async_remote_copy(
        src_ref=src, dst_ref=dst, send_sem=send, recv_sem=recv, device_id=device, device_id_type=MESH
    )


def add_into(dst, left, right):
    dst[...] = (left[...].astype(F32) + right[...].astype(F32)).astype(dst.dtype)


class Scatter:
    def __init__(self, place, sources, one, two, three, sems):
        self.place, self.sources = place, sources
        self.one, self.two, self.three = one, two, three
        self.sems = sems
        self.items = range(len(sources))

    def core_copy(self, step, item):
        p = self.place
        turn = p.turn(step)
        return remote(
            self.sources[item].at[turn, :, 1 - p.core],
            self.one[item].at[turn],
            self.sems[0].at[step, item],
            self.sems[1].at[step, item],
            p.other_core(),
        )

    def mid_copy(self, step, item):
        p = self.place
        turn = p.turn(step)
        return remote(
            self.one[item].at[turn, 1 - p.mid],
            self.two[item].at[turn],
            self.sems[2].at[step, item],
            self.sems[3].at[step, item],
            p.other_mid(),
        )

    def outer_copy(self, step, item):
        p = self.place
        turn = p.turn(step)
        return remote(
            self.two[item].at[turn],
            self.three[item].at[p.outer],
            self.sems[4].at[step, item],
            self.sems[5].at[p.outer, item],
            p.at_outer(turn),
        )

    def arrival(self, step, item):
        p = self.place
        turn = p.turn(step)
        return remote(
            self.two[item].at[turn],
            self.three[item].at[turn],
            self.sems[4].at[step, item],
            self.sems[5].at[turn, item],
            p.at_outer(turn),
        )

    def start_core(self, step):
        for item in self.items:
            self.core_copy(step, item).start()

    def core_to_mid(self, step):
        p = self.place
        turn = p.turn(step)
        for item in self.items:
            self.core_copy(step, item).wait_recv()
            one = self.one[item]
            for mid in range(2):
                add_into(one.at[turn, mid], one.at[turn, mid], self.sources[item].at[turn, mid, p.core])
            self.mid_copy(step, item).start()

    def mid_to_outer(self, step, last):
        p = self.place
        turn = p.turn(step)
        for item in self.items:
            self.mid_copy(step, item).wait_recv()
            two = self.two[item]
            add_into(two.at[turn], two.at[turn], self.one[item].at[turn, p.mid])
            if not last:
                self.outer_copy(step, item).start()

    def finish(self, outs):
        p = self.place
        for item in self.items:
            total = self.two[item][p.outer].astype(F32)
            for step in range(p.outers - 1):
                self.arrival(step, item).wait_recv()
                total = total + self.three[item][p.turn(step)].astype(F32)
            outs[item][...] = total

    def drain(self):
        def one(step, carry):
            for item in self.items:
                self.core_copy(step, item).wait_send()
                self.mid_copy(step, item).wait_send()
            return carry

        lax.fori_loop(0, self.place.outers, one, 0)
        for step in range(self.place.outers - 1):
            for item in self.items:
                self.outer_copy(step, item).wait_send()


def scatter_shapes(sources):
    one = [pltpu.VMEM((s.shape[0], 2) + s.shape[3:], s.dtype) for s in sources]
    two = [pltpu.VMEM((s.shape[0],) + s.shape[3:], s.dtype) for s in sources]
    three = [pltpu.VMEM((s.shape[0],) + s.shape[3:], s.dtype) for s in sources]
    sems = [pltpu.SemaphoreType.DMA((sources[0].shape[0], len(sources))) for _ in range(6)]
    return one + two + three + sems


class IdGather:
    def __init__(self, place, every, sems):
        self.place, self.every, self.sems = place, every, sems

    def copy(self, stage, step, theirs=0):
        p = self.place
        turn = lax.rem(p.outer + step, p.outers)
        if stage == 0:
            at = turn if theirs else p.outer
            part, peer, mark = self.every.at[at, p.mid, p.core], p.at_outer(turn), at
        elif stage == 1:
            mid = 1 - p.mid if theirs else p.mid
            part, peer, mark = self.every.at[turn, mid, p.core], p.other_mid(), step
        else:
            core = 1 - p.core if theirs else p.core
            part, peer, mark = self.every.at[turn, :, core], p.other_core(), step
        return remote(part, part, self.sems[2 * stage].at[step], self.sems[2 * stage + 1].at[mark], peer)


class Swap:
    def __init__(self, place, src, dst, send, recv):
        self.place, self.src, self.dst, self.send, self.recv = place, src, dst, send, recv

    def copy(self, at, src_rows, dst_rows):
        return remote(
            self.src.at[src_rows], self.dst.at[dst_rows], self.send.at[at], self.recv.at[at], self.place.other_side()
        )


def rows_from(start, size):
    return pl.ds(pl.multiple_of(start, size), size)


def feed_forward_kernel(
    ids, x_in, cot, wu_in, bu, wd_in, hidden, vectors, wo_in, mixed, q_in, k_in, v_in, lse, fq_ref, fk_ref, others,
    wo_other_in, every, layer, hg, norm_sums, wo_out, dwd_out, dwu_out, alone_out, dq_out, dk_out, dv_out,
    act_t, ug, xt, xg, rg, mgs, mgr, wu, wd, dbu, dbd, qs, ks, kt, gs, delta, scores, slopes,
    wo_sum, wo_recv, src_d, src_u, src_a, src_o, *rest,
):
    scatter_refs, rest = rest[:15], rest[15:]
    out_refs, rest = rest[:9], rest[9:]
    id_sems, (send_x, recv_x, send_h, recv_h, send_d, recv_d, send_l, recv_l, local) = rest[:6], rest[6:]
    tokens, width = x_in.shape
    features = wu.shape[1]
    columns = wo_in.shape[0]
    x = layer
    wo, wo_other = layer.at[:columns], layer.at[columns : 2 * columns]
    gain, bd = vectors[2:3, :], vectors[4:5, :]
    half = tokens // 2
    chunk, part, piece = 256, 512, 128
    place = Place()
    outers = place.outers
    work = Scatter(
        place, [src_d, src_u, src_a], scatter_refs[0:3], scatter_refs[3:6], scatter_refs[6:9], scatter_refs[9:]
    )
    after = Scatter(place, [src_o], out_refs[0:1], out_refs[1:2], out_refs[2:3], out_refs[3:])
    known = IdGather(place, every, id_sems)
    every[place.outer, place.mid, place.core] = ids[...]
    mine_at, other_at = place.side * half, (1 - place.side) * half
    grads = Swap(place, xg, rg, send_x, recv_x)
    mixes = Swap(place, mgs, mgr, send_h, recv_h)
    downs = Swap(place, xg, rg, send_d, recv_d)
    layers = Swap(place, layer, layer, send_l, recv_l)
    dbu[...] = jnp.zeros_like(dbu)
    dbd[...] = jnp.zeros_like(dbd)
    src_a[...] = jnp.zeros_like(src_a)
    norm_sums[...] = jnp.zeros_like(norm_sums)
    loads = [
        pltpu.make_async_copy(src, dst, local.at[at])
        for at, (src, dst) in enumerate(((x_in, x), (wu_in, wu), (wd_in, wd)))
    ]
    for copy in loads:
        copy.start()
    greet(place, True)
    for copy in loads:
        copy.wait()

    def loop(low, high, stage):
        lax.fori_loop(low, high, lambda step, carry: (stage(step), carry)[1], 0)

    def ids_mid(step):
        known.copy(0, step, 1).wait_recv()
        known.copy(1, step).start()

    def ids_core(step):
        known.copy(1, step, 1).wait_recv()
        known.copy(2, step).start()

    loop(1, outers, lambda step: known.copy(0, step).start())
    known.copy(1, 0).start()

    def forward(start):
        rows = rows_from(start, chunk)
        xc = x[rows, :]
        gc = cot[rows, :]
        xt[:, rows] = xc.T
        dbd[...] += jnp.sum(gc.astype(F32), axis=0, keepdims=True)
        total = jnp.zeros((chunk, width), F32)
        for at in range(features // part):
            cols = slice(at * part, (at + 1) * part)
            up = product(xc, wu[:, cols]) + bu[:, cols]
            square = up * up
            gate = 0.5 + 0.5 * jnp.tanh(up * (gelu_slope + (gelu_slope * gelu_cubic) * square))
            value = up * gate
            act_t[cols, rows] = value.astype(BF).T
            slope = gate + value * (1.0 - gate) * (
                2.0 * gelu_slope + (6.0 * gelu_slope * gelu_cubic) * square
            )
            low = (times_back(gc, wd[cols, :]) * slope).astype(BF)
            ug[rows, cols] = low
            dbu[:, cols] += jnp.sum(low.astype(F32), axis=0, keepdims=True)
            total = total + times_back(low, wu[:, cols])
        xg[rows, :] = total.astype(BF)

    def sent(at):
        return grads.copy(at, rows_from(other_at + at * chunk, chunk), rows_from(at * chunk, chunk))

    def theirs(at):
        forward(other_at + at * chunk)
        sent(at).start()

    loop(0, half // chunk, theirs)
    loop(0, half // chunk, lambda at: forward(mine_at + at * chunk))
    heads_in = [
        pltpu.make_async_copy(src, wu.at[:, at * columns : (at + 1) * columns], local.at[at])
        for at, src in enumerate((q_in, k_in, v_in))
    ] + [
        pltpu.make_async_copy(src, dst, local.at[3 + at])
        for at, (src, dst) in enumerate(((wo_in, wo), (wo_other_in, wo_other)))
    ]
    for copy in heads_in:
        copy.start()
    loop(1, outers, ids_mid)
    dp_size = 4 * outers
    up_lanes, down_lanes = features // dp_size, width // dp_size
    for at in range(dp_size):
        spot = (at // 4, (at // 2) % 2, at % 2)
        src_a[spot + (slice(0, 1), slice(0, up_lanes))] = dbu[:, at * up_lanes : (at + 1) * up_lanes]
        src_a[spot + (slice(1, 2), slice(0, down_lanes))] = dbd[:, at * down_lanes : (at + 1) * down_lanes]

    down_rows, up_rows = features // outers // 2, width // outers

    def weight_grads(step):
        turn = place.turn(step)
        for mid in range(2):
            rows = rows_from(turn * (2 * down_rows) + mid * down_rows, down_rows)
            src_d[turn, mid] = product(act_t[rows, :], cot[...]).astype(BF).reshape(2, down_rows // 2, width)
        rows = rows_from(turn * up_rows, up_rows)
        for at in range(features // part):
            cols = slice(at * part, (at + 1) * part)
            src_u[turn, :, :, :, cols] = (
                product(xt[rows, :], ug[:, cols]).astype(BF).reshape(2, 2, up_rows // 4, part)
            )
        work.start_core(step)

    def norm_grads(at):
        @pl.when(at % (chunk // piece) == 0)
        def _():
            sent(at // (chunk // piece)).wait_recv()

        here = rows_from(at * piece, piece)
        rows = rows_from(mine_at + at * piece, piece)
        grad = xg[rows, :].astype(F32) + rg[here, :].astype(F32)
        _, unit, inverse = normalize(hidden[here, :], 1.0, 0.0)
        back, gain_sum, bias_sum = norm_back(grad, unit, inverse, gain)
        norm_sums[0:1, :] += gain_sum[None, :]
        norm_sums[1:2, :] += bias_sum[None, :]
        total = cot[rows, :].astype(F32) + back
        hg[here, :] = total.astype(BF)

    def mix_copy(at):
        here = rows_from(at * chunk, chunk)
        return mixes.copy(at, here, here)

    def mixed_grads(at):
        here = rows_from(at * chunk, chunk)
        mgs[here, :] = times_back(hg[here, :], wo_other[...]).astype(BF)
        mix_copy(at).start()
        wu[rows_from(mine_at + at * chunk, chunk), 3 * columns :] = times_back(hg[here, :], wo[...]).astype(BF)

    weight_grads(0)
    weight_grads(1)
    work.core_to_mid(0)
    loop(0, half // piece, norm_grads)
    for copy in heads_in:
        copy.wait()
    loop(0, half // chunk, mixed_grads)
    rows_o = columns // dp_size
    turned = (mixed[rows_from(mine_at, half), :].T, others[...].T)
    for which in range(2):
        for at in range(0, width, BLOCK):
            src_o[:, :, :, which * rows_o : (which + 1) * rows_o, at : at + BLOCK] = (
                product(turned[which], hg[:, at : at + BLOCK]).astype(BF).reshape(outers, 2, 2, rows_o, BLOCK)
            )
    loop(0, outers, after.start_core)

    def more(step):
        weight_grads(step)
        work.core_to_mid(step - 1)

    loop(2, outers, more)
    loop(0, outers, after.core_to_mid)
    work.core_to_mid(outers - 1)
    loop(0, outers - 3, lambda step: work.mid_to_outer(step, False))
    loop(0, half // chunk, lambda at: sent(at).wait_send())

    def downward(start):
        rows = rows_from(start, chunk)
        xg[rows, :] = contract_rows(act_t[:, rows], wd[...]).astype(BF)

    def down_sent(at):
        return downs.copy(at, rows_from(other_at + at * piece, piece), rows_from(at * piece, piece))

    def down_theirs(at):
        downward(other_at + at * chunk)
        mix_copy(at).wait_recv()

    loop(0, half // chunk, down_theirs)
    loop(0, half // piece, lambda at: down_sent(at).start())
    wu[rows_from(other_at, half), 3 * columns :] = mgr[...]
    loop(0, half // chunk, lambda at: downward(mine_at + at * chunk))
    work.mid_to_outer(outers - 3, False)
    loop(0, outers, ids_core)

    def layer_copy(at, start):
        rows = rows_from(start + at * piece, piece)
        return layers.copy(at, rows, rows)

    def layer_rows(at):
        down_sent(at).wait_recv()
        here = rows_from(at * piece, piece)
        rows = rows_from(mine_at + at * piece, piece)
        layer[rows, :] = (
            hidden[here, :] + (xg[rows, :].astype(F32) + rg[here, :].astype(F32)) + bd
        ).astype(BF)
        layer_copy(at, mine_at).start()

    blocks = tokens // BLOCK
    scale = HEAD_DIM**-0.5

    def one_pair(at):
        def lanes_of(which):
            return pl.ds(pl.multiple_of(which * columns + at * LANES, LANES), LANES)

        keys, grad = wu[:, lanes_of(1)], wu[:, lanes_of(3)]
        scaled = (wu[:, lanes_of(0)].astype(F32) * scale).astype(BF)
        for head in range(2):
            mine = head_lanes(tokens, head)
            qs[head, :, :LANES] = jnp.where(mine, scaled, jnp.zeros_like(scaled))
            qs[head, :, LANES:] = fq_ref[...]
            gs[head] = jnp.where(mine, grad, jnp.zeros_like(grad))
        ks[:, :LANES] = keys
        ks[:, LANES:] = fk_ref[...]
        kt[...] = keys.T
        both = (grad.astype(F32) * mixed[:, lanes_of(0)].astype(F32)).T
        for head in range(2):
            delta[head : head + 1, :] = jnp.sum(
                both[head * HEAD_DIM : (head + 1) * HEAD_DIM], axis=0, keepdims=True
            )
        for block in range(blocks):
            here = slice(block * BLOCK, (block + 1) * BLOCK)
            low, high = near(block, blocks)
            dq = []
            for head in range(2):
                scores[head, low:high, :] = times_back(ks[low:high, :], qs[head, here, :])
                slopes[head, low:high, :] = times_back(wu[low:high, lanes_of(2)], gs[head, here, :])
            for head in range(2):
                offset, shift = lse[at, head : head + 1, here], delta[head : head + 1, here]
                columns_here = slice(head * tokens + block * BLOCK, head * tokens + (block + 1) * BLOCK)
                for at_key in range(low, high, STRIP):
                    strip = slice(at_key, at_key + STRIP)
                    prob = jnp.exp(scores[head, strip, :] - offset)
                    act_t[head * tokens + at_key : head * tokens + at_key + STRIP, here] = prob.astype(BF)
                    ug[strip, columns_here] = (prob * (slopes[head, strip, :] - shift)).astype(BF)
                dq.append(product(kt[head * HEAD_DIM : (head + 1) * HEAD_DIM, low:high], ug[low:high, columns_here]))
            wd[here, lanes_of(0)] = (jnp.concatenate(dq, axis=0).T * scale).astype(BF)
        for block in range(blocks):
            here = slice(block * BLOCK, (block + 1) * BLOCK)
            low, high = near(block, blocks)
            dk = jnp.zeros((BLOCK, LANES), F32)
            dv = jnp.zeros((BLOCK, LANES), F32)
            for head in range(2):
                dv = dv + product(act_t[head * tokens + block * BLOCK : head * tokens + (block + 1) * BLOCK, low:high], gs[head, low:high, :])
                dk = dk + product(ug[here, head * tokens + low : head * tokens + high], qs[head, low:high, :LANES])
            wd[here, lanes_of(1)] = dk.astype(BF)
            wd[tokens + block * BLOCK : tokens + (block + 1) * BLOCK, lanes_of(0)] = dv.astype(BF)

        @pl.when(at == 0)
        def _():
            work.mid_to_outer(outers - 2, False)
            loop(0, outers - 1, lambda step: after.mid_to_outer(step, False))
            after.mid_to_outer(outers - 1, True)

        @pl.when(at == 1)
        def _():
            work.mid_to_outer(outers - 1, True)
            loop(0, half // piece, layer_rows)

    loop(0, columns // LANES, one_pair)
    grads_out = [
        pltpu.make_async_copy(src, dst, local.at[at])
        for at, (src, dst) in enumerate(
            (
                (wd.at[:tokens, :columns], dq_out),
                (wd.at[:tokens, columns : 2 * columns], dk_out),
                (wd.at[tokens : 2 * tokens, :columns], dv_out),
            )
        )
    ]
    for copy in grads_out:
        copy.start()
    after.finish([wo_sum])
    wo_swap = remote(
        wo_sum.at[pl.ds(rows_o, rows_o)], wo_recv, send_h.at[half // chunk], recv_h.at[half // chunk], place.other_side()
    )
    wo_swap.start()
    work.finish([dwd_out, dwu_out, alone_out])
    for copy in grads_out:
        copy.wait()
    wo_swap.wait()
    wo_out[...] = wo_sum[:rows_o, :] + wo_recv[...]
    work.drain()
    after.drain()
    loop(0, outers, lambda step: known.copy(2, step, 1).wait_recv())
    loop(1, outers, lambda step: known.copy(0, step).wait_send())
    loop(0, outers, lambda step: known.copy(1, step).wait_send())
    loop(0, outers, lambda step: known.copy(2, step).wait_send())

    def swaps_done(at):
        rows = rows_from(mine_at + at * piece, piece)
        down_sent(at).wait_send()
        layer_copy(at, other_at).wait_recv()
        layer_copy(at, mine_at).wait_send()

    loop(0, half // piece, swaps_done)
    loop(0, half // chunk, lambda at: mix_copy(at).wait_send())


def feed_forward(dp_size, collective_id, *operands):
    ids, x, _, wu, _, wd, _, _, wo, _, queries, *_ = operands
    tokens, width = x.shape
    columns = wo.shape[0]
    features = wu.shape[1]
    half = tokens // 2
    outers = dp_size // 4
    shape = jax.ShapeDtypeStruct
    items = [
        shape((outers, 2, 2, features // dp_size, width), BF),
        shape((outers, 2, 2, width // dp_size, features), BF),
        shape((outers, 2, 2, 8, LANES), F32),
    ]
    item_o = shape((outers, 2, 2, 2 * columns // dp_size, width), BF)
    anywhere = pl.BlockSpec(memory_space=pl.ANY)
    return pl.pallas_call(
        feed_forward_kernel,
        in_specs=[anywhere if at in (1, 3, 5, 8, 10, 11, 12, 17) else full_spec() for at in range(len(operands))],
        out_specs=[full_spec()] * 8 + [anywhere] * 3,
        out_shape=[
            shape((outers, 2, 2) + ids.shape, ids.dtype),
            shape((tokens, width), BF),
            shape((half, width), BF),
            shape((2, width), F32),
            shape((wo.shape[0] // dp_size, width), F32),
        ]
        + [shape(item.shape[3:], F32) for item in items]
        + [shape(queries.shape, BF)] * 3,
        scratch_shapes=[
            pltpu.VMEM((features, tokens), BF),
            pltpu.VMEM((tokens, features), BF),
            pltpu.VMEM((width, tokens), BF),
            pltpu.VMEM((tokens, width), BF),
            pltpu.VMEM((half, width), BF),
            pltpu.VMEM((half, columns), BF),
            pltpu.VMEM((half, columns), BF),
            pltpu.VMEM(wu.shape, BF),
            pltpu.VMEM(wd.shape, BF),
            pltpu.VMEM((1, features), F32),
            pltpu.VMEM((1, width), F32),
            pltpu.VMEM((2, tokens, 2 * LANES), BF),
            pltpu.VMEM((tokens, 2 * LANES), BF),
            pltpu.VMEM((LANES, tokens), BF),
            pltpu.VMEM((2, tokens, LANES), BF),
            pltpu.VMEM((2, tokens), F32),
            pltpu.VMEM((2, tokens, BLOCK), F32),
            pltpu.VMEM((2, tokens, BLOCK), F32),
            pltpu.VMEM(item_o.shape[3:], F32),
            pltpu.VMEM((columns // dp_size, width), F32),
        ]
        + [pltpu.VMEM(item.shape, item.dtype) for item in items + [item_o]]
        + scatter_shapes(items)
        + scatter_shapes([item_o])
        + [pltpu.SemaphoreType.DMA((outers,)) for _ in range(6)]
        + [pltpu.SemaphoreType.DMA((half // 256,)) for _ in range(2)]
        + [pltpu.SemaphoreType.DMA((half // 128,)) for _ in range(6)]
        + [pltpu.SemaphoreType.DMA((5,))],
        compiler_params=pltpu.CompilerParams(
            vmem_limit_bytes=60 * 1024 * 1024, collective_id=collective_id, has_side_effects=True
        ),
        name="feed_forward",
    )(*operands)


def front_kernel(
    rows_ref, noise, scales, w_in, vectors, wq, wk, wv, fq_ref, fk_ref, wo,
    q_out, k_out, v_out, n1t_out, stream_out, others_out, wo_out, inputs_out, mixed, lse, hidden_out, x2,
    q, k, v, n1t, stream_own, stream, theirs, wo_other, others, qs, ks, vt, scores, probs, inputs,
    send_r, recv_r, send_m, recv_m, local,
):
    tokens, width = stream.shape
    half = tokens // 2
    chunk = 256
    pairs = q.shape[1] // LANES
    place = Place()
    mine_at = place.side * half
    barrier = pltpu.get_barrier_semaphore()
    for peer in (place.other_side(), place.other_core()):
        pl.semaphore_signal(barrier, inc=1, device_id=peer, device_id_type=MESH)
    pl.semaphore_wait(barrier, 2)

    def loop(low, high, stage):
        lax.fori_loop(low, high, lambda step, carry: (stage(step), carry)[1], 0)

    def row_copy(at):
        span = rows_from(at * chunk, chunk)
        return remote(rows_ref.at[span], theirs.at[span], send_r.at[at], recv_r.at[at], place.other_side())

    count = tokens // chunk
    part = wo.shape[0] // 2

    def weights(step):
        rows = rows_from(place.core * part, part)
        src = wo_other if step else wo
        peer = place.other_core() if step else place.other_side()
        return remote(src.at[rows], wo_other.at[rows], send_r.at[count + step], recv_r.at[count + step], peer)

    loop(0, count, lambda at: row_copy(at).start())
    weights(0).start()

    def start_of(at):
        row_copy(at).wait_recv()
        span = rows_from(at * chunk, chunk)
        embedded = rows_ref[span, :].astype(F32) + theirs[span, :].astype(F32)
        low = (scales[0:1, 0:1] * (embedded + scales[1:2, 0:1] * noise[span, :].astype(F32))).astype(BF)
        inputs[span, :] = low
        flow = product(low, w_in[...])
        stream[span, :] = flow
        normed, _, _ = normalize(flow, vectors[0:1, :], vectors[1:2, :])
        normed = normed.astype(BF)
        n1t[:, span] = normed.T
        q[span, :] = product(normed, wq[...]).astype(BF)
        k[span, :] = product(normed, wk[...]).astype(BF)
        v[span, :] = product(normed, wv[...]).astype(BF)

    loop(0, count, start_of)

    def keep(at):
        span = rows_from(at * chunk, chunk)
        stream_own[span, :] = stream[rows_from(mine_at + at * chunk, chunk), :]

    loop(0, half // chunk, keep)
    kept = [
        pltpu.make_async_copy(src, dst, local.at[at])
        for at, (src, dst) in enumerate(
            ((q, q_out), (k, k_out), (v, v_out), (n1t, n1t_out), (stream_own, stream_out))
        )
    ]
    for copy in kept:
        copy.start()

    blocks = tokens // BLOCK
    scale = HEAD_DIM**-0.5

    def pair_copy(at):
        lanes = pl.ds(pl.multiple_of(at * LANES, LANES), LANES)
        return remote(mixed.at[:, lanes], others.at[:, lanes], send_m.at[at], recv_m.at[at], place.other_side())

    def one_pair(at):
        lanes = pl.ds(pl.multiple_of(at * LANES, LANES), LANES)
        scaled = (q[:, lanes].astype(F32) * scale).astype(BF)
        for head in range(2):
            qs[head, :, :LANES] = jnp.where(head_lanes(tokens, head), scaled, jnp.zeros_like(scaled))
            qs[head, :, LANES:] = fq_ref[...]
        ks[:, :LANES] = k[:, lanes]
        ks[:, LANES:] = fk_ref[...]
        vt[...] = v[:, lanes].T
        for block in range(blocks):
            here = slice(block * BLOCK, (block + 1) * BLOCK)
            low, high = near(block, blocks)
            found = []
            for head in range(2):
                scores[head, low:high, :] = times_back(ks[low:high, :], qs[head, here, :])
            for head in range(2):
                peak = jnp.full((8, BLOCK), masked_score, F32)
                for at_key in range(low, high, STRIP):
                    strip = scores[head, at_key : at_key + STRIP, :].reshape(STRIP // 8, 8, BLOCK)
                    peak = jnp.maximum(peak, jnp.max(strip, axis=0))
                peak = jnp.max(peak, axis=0, keepdims=True)
                total = jnp.zeros((8, BLOCK), F32)
                for at_key in range(low, high, STRIP):
                    strip = jnp.exp(scores[head, at_key : at_key + STRIP, :] - peak)
                    total = total + jnp.sum(strip.reshape(STRIP // 8, 8, BLOCK), axis=0)
                    probs[head, at_key : at_key + STRIP, :] = strip.astype(BF)
                total = jnp.sum(total, axis=0, keepdims=True)
                values = vt[head * HEAD_DIM : (head + 1) * HEAD_DIM, low:high]
                found.append(product(values, probs[head, low:high, :]) / total)
                lse[at, head : head + 1, here] = peak + jnp.log(total)
            mixed[here, lanes] = jnp.concatenate(found, axis=0).T.astype(BF)
        pair_copy(at).start()

        @pl.when(at == 1)
        def _():
            weights(0).wait_recv()
            weights(1).start()

    loop(0, pairs, one_pair)

    def ours(at):
        span = rows_from(at * chunk, chunk)
        stream[span, :] += product(mixed[span, :], wo[...])

    loop(0, count, ours)
    weights(1).wait_recv()
    loop(0, pairs, lambda at: pair_copy(at).wait_recv())
    kept += [
        pltpu.make_async_copy(src, dst, local.at[5 + at])
        for at, (src, dst) in enumerate(((others.at[rows_from(mine_at, half)], others_out), (wo_other, wo_out)))
    ]
    for copy in kept[5:]:
        copy.start()

    def finish(at):
        span = rows_from(at * chunk, chunk)
        hidden = stream[span, :] + product(others[span, :], wo_other[...])
        stream[span, :] = hidden
        normed, _, _ = normalize(hidden, vectors[2:3, :], vectors[3:4, :])
        x2[span, :] = normed.astype(BF)

    loop(0, count, finish)
    hidden_out[...] = stream[rows_from(mine_at, half), :]
    inputs_out[...] = inputs[rows_from(mine_at, half), :]
    loop(0, count, lambda at: row_copy(at).wait_send())
    weights(0).wait_send()
    weights(1).wait_send()
    loop(0, pairs, lambda at: pair_copy(at).wait_send())
    for copy in kept:
        copy.wait()


def front(rows, noise, scales, w_in, vectors, wq, wk, wv, fq, fk, wo, collective_id):
    tokens, embed = rows.shape
    width, columns = wq.shape
    half = tokens // 2
    pairs = columns // LANES
    count = tokens // 256
    shape = jax.ShapeDtypeStruct
    head = shape((tokens, columns), BF)
    scratch = pltpu.VMEM
    return pl.pallas_call(
        front_kernel,
        in_specs=[full_spec()] * 11,
        out_specs=[pl.BlockSpec(memory_space=pl.ANY)] * 7 + [full_spec()] * 5,
        out_shape=[
            head,
            head,
            head,
            shape((width, tokens), BF),
            shape((half, width), F32),
            shape((half, columns), BF),
            shape(wo.shape, BF),
            shape((half, embed), BF),
            head,
            shape((pairs, 2, tokens), F32),
            shape((half, width), F32),
            shape((tokens, width), BF),
        ],
        scratch_shapes=[
            scratch(head.shape, BF),
            scratch(head.shape, BF),
            scratch(head.shape, BF),
            scratch((width, tokens), BF),
            scratch((half, width), F32),
            scratch((tokens, width), F32),
            scratch(rows.shape, BF),
            scratch(wo.shape, BF),
            scratch(head.shape, BF),
            scratch((2, tokens, 2 * LANES), BF),
            scratch((tokens, 2 * LANES), BF),
            scratch((LANES, tokens), BF),
            scratch((2, tokens, BLOCK), F32),
            scratch((2, tokens, BLOCK), BF),
            scratch(rows.shape, BF),
        ]
        + [pltpu.SemaphoreType.DMA((count + 2,)) for _ in range(2)]
        + [pltpu.SemaphoreType.DMA((pairs,)) for _ in range(2)]
        + [pltpu.SemaphoreType.DMA((7,))],
        compiler_params=pltpu.CompilerParams(
            vmem_limit_bytes=VMEM_LIMIT, collective_id=collective_id, has_side_effects=True
        ),
        name="front",
    )(rows, noise, scales, w_in, vectors, wq, wk, wv, fq, fk, wo)


class Gather:
    def __init__(self, place, every, sems):
        self.place, self.every, self.sems = place, every, sems

    def turn(self, step):
        return lax.rem(self.place.outer + step, self.place.outers)

    def copy(self, stage, piece, step, theirs=0):
        p = self.place
        turn = self.turn(step)
        mark = step
        if stage == 0:
            at = turn if theirs else p.outer
            part = self.every.at[at, p.mid, p.core, p.side, piece]
            peer, mark = p.at_outer(turn), at
        elif stage == 3:
            core = 1 - p.core if theirs else p.core
            part, peer = self.every.at[turn, :, core, :, piece], p.other_core()
        elif (stage == 1) == (piece % 2 == 0):
            side = 1 - p.side if theirs else p.side
            mid = slice(None) if piece % 2 else p.mid
            part, peer = self.every.at[turn, mid, p.core, side, piece], p.other_side()
        else:
            mid = 1 - p.mid if theirs else p.mid
            side = p.side if piece % 2 else slice(None)
            part, peer = self.every.at[turn, mid, p.core, side, piece], p.other_mid()
        sems = self.sems[2 * stage : 2 * stage + 2]
        return remote(part, part, sems[0].at[piece, step], sems[1].at[piece, mark], peer)


def tail_kernel(
    vocab_part,
    large,
    dq, dk, dv, n1t_in, wq, wk, wv, stream_in, hgrad_in, vectors, w_in, inputs, scales, ids, mine, sums_two,
    qkv_out, w_in_out, sides_out, noise, table,
    every, n1t, stream, hgrad, part, rpart, nsend, nrecv, stage_in, stage_out, picked, total, sums,
    src_q, src_w, src_s, side_w, side_s, *rest,
):
    early_refs, rest = rest[:9], rest[9:]
    late_refs, rest = rest[:12], rest[12:]
    gather_sems, rest = rest[:8], rest[8:]
    send_x, recv_x, send_n, recv_n, send_s, recv_s, local = rest
    width, tokens = n1t.shape
    columns = wq.shape[1]
    half = tokens // 2
    chunk, piece = 256, half // 4
    place = Place()
    outers = place.outers
    early = Scatter(place, [src_q], early_refs[0:1], early_refs[1:2], early_refs[2:3], early_refs[3:])
    late = Scatter(place, [src_w, src_s], late_refs[0:2], late_refs[2:4], late_refs[4:6], late_refs[6:])
    gather = Gather(place, every, gather_sems)
    mine_at, other_at = place.side * half, (1 - place.side) * half
    grads = Swap(place, part, rpart, send_x, recv_x)
    noises = Swap(place, nsend, nrecv, send_n, recv_n)
    loads = [
        pltpu.make_async_copy(src, dst, local.at[at])
        for at, (src, dst) in enumerate(((n1t_in, n1t), (stream_in, stream), (hgrad_in, hgrad)))
    ]
    for copy in loads:
        copy.start()
    sums[...] = jnp.zeros_like(sums)
    src_s[...] = jnp.zeros_like(src_s)
    total[...] = jnp.zeros_like(total)
    sums[2:4, :] = sums_two[...]
    greet(place, True)

    def loop(low, high, stage):
        lax.fori_loop(low, high, lambda step, carry: (stage(step), carry)[1], 0)

    def back_product(start):
        rows = rows_from(start, chunk)
        part[rows, :] = (
            times_back(dq[rows, :], wq[...])
            + times_back(dk[rows, :], wk[...])
            + times_back(dv[rows, :], wv[...])
        ).astype(BF)

    def sent(at):
        return grads.copy(at, rows_from(other_at + at * piece, piece), rows_from(at * piece, piece))

    def theirs(at):
        back_product(other_at + at * chunk)
        for step in range(chunk // piece):
            sent(at * (chunk // piece) + step).start()

    loop(0, half // chunk, theirs)
    for copy in loads:
        copy.wait()
    group = width // outers

    def weight_grads(step):
        turn = place.turn(step)
        rows = rows_from(turn * group, group)
        for at, grad in enumerate((dq, dk, dv)):
            src_q[turn, :, :, :, at * columns : (at + 1) * columns] = (
                product(n1t[rows, :], grad[...]).astype(BF).reshape(2, 2, group // 4, columns)
            )
        early.start_core(step)

    weight_grads(0)

    def more(step):
        weight_grads(step)
        early.core_to_mid(step - 1)

    loop(1, outers, more)
    loop(0, half // chunk, lambda at: back_product(mine_at + at * chunk))
    early.core_to_mid(outers - 1)

    def noise_copy(which):
        rows = pl.ds(which * piece, piece)
        return noises.copy(which, rows, rows)

    def norm_grads(which):
        sent(which).wait_recv()
        here = slice(which * piece, (which + 1) * piece)
        rows = rows_from(mine_at + which * piece, piece)
        grad = part[rows, :].astype(F32) + rpart[here, :].astype(F32)
        _, unit, inverse = normalize(stream[here, :], 1.0, 0.0)
        back, gain_sum, bias_sum = norm_back(grad, unit, inverse, vectors[0:1, :])
        low = (hgrad[here, :].astype(F32) + back).astype(BF)
        back_in = times_back(low, w_in[...])
        spot = every.at[place.outer, place.mid, place.core, place.side, which]
        found = (scales[0:1, 0:1] * back_in).astype(BF)
        if large:
            stage_out[...] = found
            moved = pltpu.make_async_copy(stage_out, spot, local.at[0])
            moved.start()
            moved.wait()
        else:
            spot[...] = found
        loop(1, outers, lambda step: gather.copy(0, which, step).start())
        gather.copy(1, which, 0).start()
        sums[0:1, :] += gain_sum[None, :]
        sums[1:2, :] += bias_sum[None, :]
        rpart[here, :] = low
        noised = (scales[0:1, 0:1] * scales[1:2, 0:1]) * back_in
        noise[rows, :] = noised
        nsend[here, :] = noised.astype(BF)

    dp_size = 4 * outers

    def start_late():
        for which in range(4):
            noise_copy(which).start()
        rows_w = w_in.shape[0] // dp_size
        lanes = width // dp_size
        work = contract_rows(inputs[...], rpart[...])
        for at in range(dp_size):
            spot = (at // 4, (at // 2) % 2, at % 2)
            src_w[spot] = work[at * rows_w : (at + 1) * rows_w, :].astype(src_w.dtype)
            src_s[spot + (slice(None), slice(0, lanes))] = sums[:, at * lanes : (at + 1) * lanes]
        loop(0, outers, late.start_core)

    def forward(stage, which, step):
        gather.copy(stage - 1, which, step, 1).wait_recv()
        gather.copy(stage, which, step).start()

    owned = table.shape[0]
    wanted = lax.broadcasted_iota(jnp.int32, (total.shape[0], 1), 0)
    first = place.side * vocab_part + place.dp * owned

    def collect(pair, step):
        turn = gather.turn(step)
        for which in (2 * pair, 2 * pair + 1):
            gather.copy(3, which, step, 1).wait_recv()
        pieces = every.at[turn, :, :, :, 2 * pair : 2 * pair + 2]
        if large:
            moved = pltpu.make_async_copy(pieces, stage_in, local.at[0])
            moved.start()
            moved.wait()
            pieces = stage_in
        for spot in range(8):
            mid, core, side = spot // 4, (spot // 2) % 2, spot % 2
            for at in range(2):
                line = 4 * side + 2 * pair + at
                lanes = slice((2 * spot + at) * LANES, (2 * spot + at + 1) * LANES)
                picked[:, lanes] = ((ids[turn, mid, core, line : line + 1, :] - first) == wanted).astype(BF)
        total[...] += product(picked[...], pieces[...].reshape(16 * piece, -1))

    sided = []
    for slot in range(8):
        if slot < 4:
            norm_grads(slot)
            if slot == 3:
                start_late()
        if 1 <= slot < 5:
            loop(1, outers, lambda step: forward(1, slot - 1, step))
            forward(2, slot - 1, 0)
        if 2 <= slot < 6:
            loop(1, outers, lambda step: forward(2, slot - 2, step))
            forward(3, slot - 2, 0)
        if 3 <= slot < 7:
            loop(1, outers, lambda step: forward(3, slot - 3, step))
        if slot == 4:
            loop(0, outers - 1, lambda step: early.mid_to_outer(step, False))
            early.mid_to_outer(outers - 1, True)
            loop(0, outers, late.core_to_mid)
        if slot == 5:
            loop(0, outers, lambda step: collect(0, step))
            loop(0, outers - 1, lambda step: late.mid_to_outer(step, False))
            late.mid_to_outer(outers - 1, True)
        if slot == 6:
            early.finish([qkv_out])
            late.finish([w_in_out, sides_out])
            for at, (out, buffer) in enumerate(((w_in_out, side_w), (sides_out, side_s))):
                buffer[0] = out[...]
                sided.append(remote(buffer.at[0], buffer.at[1], send_s.at[at], recv_s.at[at], place.other_side()))
                sided[at].start()
        if slot == 7:
            loop(0, outers, lambda step: collect(1, step))
    for which in range(4):
        noise_copy(which).wait()
    noise[rows_from(other_at, half), :] = nrecv[...].astype(F32)
    mine_rows = mine[...].astype(F32)
    scale = row_scale(mine_rows)
    grad = total[...][:owned]
    table[...] = scale * grad - mine_rows * (scale * scale * scale) * jnp.mean(
        grad * mine_rows, axis=1, keepdims=True
    )
    for at, (out, buffer) in enumerate(((w_in_out, side_w), (sides_out, side_s))):
        sided[at].wait()
        out[...] = out[...] + buffer[1]
    early.drain()
    late.drain()
    loop(0, half // piece, lambda at: sent(at).wait_send())

    def done(step):
        for which in range(4):
            for stage in range(1, 4):
                gather.copy(stage, which, step).wait_send()

    loop(0, outers, done)

    def done_outer(step):
        for which in range(4):
            gather.copy(0, which, step).wait_send()

    loop(1, outers, done_outer)


def tail(vocab_part, dp_size, collective_id, *operands):
    (_, _, _, n1t, wq, _, _, stream, _, _, w_in, _, _, _, mine, _) = operands
    width, tokens = n1t.shape
    columns = wq.shape[1]
    half = tokens // 2
    piece = half // 4
    outers = dp_size // 4
    embed = w_in.shape[0]
    owned = mine.shape[0]
    padded = -(-owned // LANES) * LANES
    large = outers > 4
    every_shape = (outers, 2, 2, 2, 4, piece, embed)
    anywhere = pl.BlockSpec(memory_space=pl.ANY)

    def blocks_of(rows, cols, dtype):
        return jax.ShapeDtypeStruct((outers, 2, 2, rows, cols), dtype)

    src_q = blocks_of(width // dp_size, 3 * columns, BF)
    src_w = blocks_of(embed // dp_size, width, F32 if embed // dp_size % 16 else BF)
    src_s = blocks_of(8, LANES, F32)

    def owned_shape(value):
        return jax.ShapeDtypeStruct(value.shape[3:], F32)

    def scratch(shape, dtype):
        return pltpu.VMEM(shape, dtype)

    return pl.pallas_call(
        functools.partial(tail_kernel, vocab_part, large),
        in_specs=[anywhere if at in (3, 7, 8) else full_spec() for at in range(len(operands))],
        out_specs=[full_spec()] * 5 + ([anywhere] if large else []),
        out_shape=[
            owned_shape(src_q),
            owned_shape(src_w),
            owned_shape(src_s),
            jax.ShapeDtypeStruct((tokens, embed), F32),
            jax.ShapeDtypeStruct((owned, embed), F32),
        ]
        + ([jax.ShapeDtypeStruct(every_shape, BF)] if large else []),
        scratch_shapes=([] if large else [scratch(every_shape, BF)])
        + [
            scratch(n1t.shape, BF),
            scratch(stream.shape, F32),
            scratch(stream.shape, BF),
            scratch((tokens, width), BF),
            scratch((half, width), BF),
            scratch((half, embed), BF),
            scratch((half, embed), BF),
            scratch((2, 2, 2, 2, piece, embed) if large else (16, LANES), BF),
            scratch((piece, embed) if large else (16, LANES), BF),
            scratch((padded, 16 * piece), BF),
            scratch((padded, embed), F32),
            scratch((8, width), F32),
            scratch(src_q.shape, BF),
            scratch(src_w.shape, src_w.dtype),
            scratch(src_s.shape, F32),
            scratch((2,) + src_w.shape[3:], F32),
            scratch((2,) + src_s.shape[3:], F32),
        ]
        + scatter_shapes([src_q])
        + scatter_shapes([src_w, src_s])
        + [pltpu.SemaphoreType.DMA((4, outers)) for _ in range(8)]
        + [pltpu.SemaphoreType.DMA((4,)) for _ in range(4)]
        + [pltpu.SemaphoreType.DMA((2,)) for _ in range(2)]
        + [pltpu.SemaphoreType.DMA((3,))],
        compiler_params=pltpu.CompilerParams(
            vmem_limit_bytes=VMEM_LIMIT, collective_id=collective_id, has_side_effects=True
        ),
        name="tail",
    )(*operands)


def results_kernel(columns, layer, noise, table, w_in, qkv, wo, wu, wd, sides, alone, *refs):
    outs, sems = refs[:16], refs[16]
    sources = (
        layer, noise, table, w_in, qkv.at[:, :columns], qkv.at[:, columns : 2 * columns], qkv.at[:, 2 * columns :], wo, wu, wd,
    )
    copies = [pltpu.make_async_copy(src, dst, sems.at[at]) for at, (src, dst) in enumerate(zip(sources, outs[:10]))]
    for copy in copies:
        copy.start()
    for at in range(4):
        outs[10 + at][...] = sides[at, : outs[10 + at].shape[0]]
    for at in range(2):
        outs[14 + at][...] = alone[at, : outs[14 + at].shape[0]]
    for copy in copies:
        copy.wait()


def results(layer, noise, table, w_in, qkv, wo, wu, wd, sides, alone, small, bias_up_size):
    columns = qkv.shape[1] // 3
    shape = jax.ShapeDtypeStruct
    head = shape((qkv.shape[0], columns), F32)
    large = [layer, noise, table, w_in, head, head, head, wo, wu, wd]
    anywhere = pl.BlockSpec(memory_space=pl.ANY)
    return pl.pallas_call(
        functools.partial(results_kernel, columns),
        in_specs=[full_spec()] * 10,
        out_specs=[anywhere] * 10 + [full_spec()] * 6,
        out_shape=[shape(value.shape, value.dtype) for value in large]
        + [shape((small,), F32)] * 4
        + [shape((bias_up_size,), F32), shape((small,), F32)],
        scratch_shapes=[pltpu.SemaphoreType.DMA((10,))],
        name="results",
    )(layer, noise, table, w_in, qkv, wo, wu, wd, sides, alone)


def on_device(
    token_ids,
    segment_ids,
    time_index,
    noise_vec,
    embed_table,
    w_in,
    norm1_gain,
    norm1_bias,
    w_query,
    w_key,
    w_value,
    w_out,
    norm2_gain,
    norm2_bias,
    w_up,
    bias_up,
    w_down,
    bias_down,
    cotangent,
):
    seq_count, length = segment_ids.shape
    tokens = seq_count * length
    half = tokens // 2
    vocab_part = embed_table.shape[0]
    dp_size = lax.axis_size("dp")
    dp_index = lax.axis_index("dp")
    side = lax.axis_index("mp")
    fq, fk = lax.optimization_barrier(attention_masks(segment_ids[0]))
    level_step = jnp.log(time_high / time_low) / (TLEVELS - 1)
    level = time_low * jnp.exp(time_index.astype(F32) * level_step)
    scales = jnp.stack([lax.rsqrt(1.0 + level * level), level])
    rows = gather_rows(token_ids - side * vocab_part, embed_table)
    rows, *small_vectors = lax.optimization_barrier(
        (rows, norm1_gain, norm1_bias, norm2_gain, norm2_bias, bias_down)
    )
    vectors = jnp.stack(small_vectors).astype(F32)
    (
        queries, key_rows, value_rows, normed_one_t, stream_half, mixed_other, w_out_other, inputs_half, mixed_low, log_total, hidden_half, normed_two,
    ) = front(
        rows, noise_vec, scales, w_in, vectors, w_query, w_key, w_value, fq, fk, w_out, 3,
    )
    (
        every_id, layer_out, hidden_grad, norm_two_sums, w_out_grad, w_down_grad, w_up_grad, alone_grad,
        query_grad, key_grad, value_grad,
    ) = feed_forward(
        dp_size, 1, token_ids.reshape(-1, LANES), normed_two, cotangent, w_up, bias_up.astype(F32)[None, :], w_down,
        hidden_half, vectors, w_out, mixed_low, queries, key_rows, value_rows, log_total, fq, fk, mixed_other, w_out_other,
    )
    owned = vocab_part // dp_size
    mine = lax.dynamic_slice_in_dim(embed_table, dp_index * owned, owned, 0)
    qkv_grad, w_in_grad, sides_grad, noise_grad, table_grad, *_ = tail(
        vocab_part, dp_size, 2, query_grad, key_grad, value_grad, normed_one_t, w_query, w_key, w_value,
        stream_half, hidden_grad, vectors, w_in, inputs_half, scales, every_id, mine,
        norm_two_sums,
    )
    width = bias_down.shape[0] // dp_size
    (
        layer, noise, table, w_in_sum, query_sum, key_sum, value_sum, w_out_sum, w_up_sum, w_down_sum,
        gain_one_sum, bias_one_sum, gain_two_sum, bias_two_sum, bias_up_sum, bias_down_sum,
    ) = results(
        layer_out, noise_grad, table_grad, w_in_grad, qkv_grad, w_out_grad, w_up_grad, w_down_grad,
        sides_grad, alone_grad, width, bias_up.shape[0] // dp_size,
    )
    return (
        layer, noise, table, w_in_sum, gain_one_sum, bias_one_sum, query_sum, key_sum, value_sum, w_out_sum,
        gain_two_sum, bias_two_sum, w_up_sum, bias_up_sum, w_down_sum, bias_down_sum,
    )


def solution(mesh):
    placed = (
        P("dp"),
        P("dp", None),
        P("dp"),
        P("dp", None),
        P("mp", None),
        P(),
        P(),
        P(),
        P(None, "mp"),
        P(None, "mp"),
        P(None, "mp"),
        P("mp", None),
        P(),
        P(),
        P(None, "mp"),
        P("mp"),
        P("mp", None),
        P(),
        P("dp", None),
    )
    return jax.shard_map(
        on_device,
        mesh=mesh,
        in_specs=placed,
        out_specs=(
            P("dp", None),
            P("dp", None),
            P(("mp", "dp"), None),
            P("dp", None),
            P("dp"),
            P("dp"),
            P("dp", "mp"),
            P("dp", "mp"),
            P("dp", "mp"),
            P(("mp", "dp"), None),
            P("dp"),
            P("dp"),
            P("dp", "mp"),
            P(("mp", "dp")),
            P(("mp", "dp"), None),
            P("dp"),
        ),
        check_vma=False,
    )
```

```python
import functools

import jax
import jax.numpy as jnp
from jax import lax
from jax.experimental import pallas as pl
from jax.experimental.pallas import tpu as pltpu
from jax.sharding import PartitionSpec as P

HEAD_DIM = 64
TLEVELS = 16
DOCS = 4
MAX_RUN = 512

time_low = 0.5
time_high = 10.0
norm_eps = 1e-05
table_eps = 1e-06
masked_score = -1e30

BF = jnp.bfloat16
F32 = jnp.float32
VMEM_LIMIT = 56 * 1024 * 1024
BLOCK = 256
STRIP = 64
LANES = 128


def to_bf16(value):
    return value.astype(BF)


def product(left, right):
    return jnp.dot(left, right, preferred_element_type=F32)


def contract_rows(left, right):
    return lax.dot_general(left, right, (((0,), (0,)), ((), ())), preferred_element_type=F32)


def times_back(left, right):
    return lax.dot_general(left, right, (((1,), (1,)), ((), ())), preferred_element_type=F32)


def params(limit=VMEM_LIMIT):
    return pltpu.CompilerParams(vmem_limit_bytes=limit)


def cost(flops, nbytes, trans=0):
    return pl.CostEstimate(flops=int(flops), bytes_accessed=int(nbytes), transcendentals=int(trans))


def full_spec():
    return pl.BlockSpec(memory_space=pltpu.VMEM)


def row_scale(table_rows):
    return lax.rsqrt(jnp.mean(table_rows * table_rows, axis=1, keepdims=True) + table_eps)


def normalize(values, gain, bias):
    centred = values - jnp.mean(values, axis=-1, keepdims=True)
    inverse = lax.rsqrt(jnp.mean(centred * centred, axis=-1, keepdims=True) + norm_eps)
    unit_rows = centred * inverse
    return (unit_rows * gain + bias, unit_rows, inverse)


def norm_back(grad, unit_rows, inverse, gain):
    scaled = grad * gain
    spread = (
        scaled
        - jnp.mean(scaled, axis=-1, keepdims=True)
        - unit_rows * jnp.mean(scaled * unit_rows, axis=-1, keepdims=True)
    )
    return (inverse * spread, jnp.sum(grad * unit_rows, axis=0), jnp.sum(grad, axis=0))


def gather_kernel(parts, ids, table, out, staged, wide, picked, sems):
    rows, width = table.shape
    tokens = picked.shape[0]
    step = rows // parts

    def copy(part):
        span = pl.ds(part * step, step)
        return pltpu.make_async_copy(table.at[span], staged.at[span], sems.at[part])

    for part in range(parts):
        copy(part).start()
    wide[pl.ds(rows, 8), :] = jnp.zeros((8, width), F32)
    for part in range(parts):
        copy(part).wait()
        piece = step // 5

        @pl.loop(0, 5)
        def _(at):
            span = pl.ds(pl.multiple_of(part * step + at * piece, 16), piece)
            wide[span, :] = staged[span, :].astype(F32)

    def one(at, carry):
        picked[pl.ds(at, 1), :] = wide[pl.ds(ids[at], 1), :]
        return carry

    lax.fori_loop(0, tokens, one, 0, unroll=8)
    found = picked[...]
    out[...] = (found * row_scale(found)).astype(BF)


def gather_rows(local_ids, table):
    rows, width = table.shape
    local_ids = jnp.where(jnp.logical_and(local_ids >= 0, local_ids < rows), local_ids, rows)
    tokens = local_ids.shape[0]
    parts = 5
    return pl.pallas_call(
        functools.partial(gather_kernel, parts),
        grid_spec=pltpu.PrefetchScalarGridSpec(
            num_scalar_prefetch=1,
            grid=(1,),
            in_specs=[pl.BlockSpec(memory_space=pl.ANY)],
            out_specs=pl.BlockSpec((tokens, width), lambda i, ids: (0, 0)),
            scratch_shapes=[
                pltpu.VMEM((rows, width), BF),
                pltpu.VMEM((rows + 8, width), F32),
                pltpu.VMEM((tokens, width), F32),
                pltpu.SemaphoreType.DMA((parts,)),
            ],
        ),
        out_shape=jax.ShapeDtypeStruct((tokens, width), BF),
        compiler_params=params(),
        cost_estimate=cost(0, rows * width * 2),
        name="embed_rows",
    )(local_ids, table)


def head_lanes(rows, head):
    lane = lax.broadcasted_iota(jnp.int32, (rows, LANES), 1)
    return (lane // HEAD_DIM) == head


def near(block, count):
    reach = MAX_RUN // BLOCK
    return max(0, block - reach) * BLOCK, min(count, block + reach + 1) * BLOCK


def attention_masks(segment_ids):
    lane = lax.broadcasted_iota(jnp.int32, (1, LANES), 1)
    same = segment_ids[:, None] == lane
    fk = jnp.where(same, 1.0, 0.0).astype(BF)
    fq = jnp.where(jnp.logical_or(same, lane >= DOCS), 0.0, masked_score).astype(BF)
    return fq, fk


gelu_slope = 0.7978845608028654
gelu_cubic = 0.044715


MESH = pl.DeviceIdType.MESH


class Place:
    def __init__(self):
        self.dp = lax.axis_index("dp")
        self.side = lax.axis_index("mp")
        self.outers = lax.axis_size("dp") // 4
        self.outer = self.dp // 4
        self.mid = (self.dp // 2) % 2
        self.core = self.dp % 2

    def other_core(self):
        return (self.dp + 1 - 2 * self.core, self.side)

    def other_mid(self):
        return (self.dp + 2 - 4 * self.mid, self.side)

    def other_side(self):
        return (self.dp, 1 - self.side)

    def at_outer(self, outer):
        return (outer * 4 + self.mid * 2 + self.core, self.side)

    def turn(self, step):
        return lax.rem(self.outer + 1 + step, self.outers)


def greet(place, with_side):
    barrier = pltpu.get_barrier_semaphore()
    peers = [place.other_core(), place.other_mid()]
    if with_side:
        peers.append(place.other_side())
    for peer in peers:
        pl.semaphore_signal(barrier, inc=1, device_id=peer, device_id_type=MESH)
    for step in range(place.outers - 1):
        pl.semaphore_signal(
            barrier, inc=1, device_id=place.at_outer(place.turn(step)), device_id_type=MESH
        )
    pl.semaphore_wait(barrier, len(peers) + place.outers - 1)


def remote(src, dst, send, recv, device):
    return pltpu.make_async_remote_copy(
        src_ref=src, dst_ref=dst, send_sem=send, recv_sem=recv, device_id=device, device_id_type=MESH
    )


def add_into(dst, left, right):
    dst[...] = (left[...].astype(F32) + right[...].astype(F32)).astype(dst.dtype)


class Scatter:
    def __init__(self, place, sources, one, two, three, sems):
        self.place, self.sources = place, sources
        self.one, self.two, self.three = one, two, three
        self.sems = sems
        self.items = range(len(sources))

    def core_copy(self, step, item):
        p = self.place
        turn = p.turn(step)
        return remote(
            self.sources[item].at[turn, :, 1 - p.core],
            self.one[item].at[turn],
            self.sems[0].at[step, item],
            self.sems[1].at[step, item],
            p.other_core(),
        )

    def mid_copy(self, step, item):
        p = self.place
        turn = p.turn(step)
        return remote(
            self.one[item].at[turn, 1 - p.mid],
            self.two[item].at[turn],
            self.sems[2].at[step, item],
            self.sems[3].at[step, item],
            p.other_mid(),
        )

    def outer_copy(self, step, item):
        p = self.place
        turn = p.turn(step)
        return remote(
            self.two[item].at[turn],
            self.three[item].at[p.outer],
            self.sems[4].at[step, item],
            self.sems[5].at[p.outer, item],
            p.at_outer(turn),
        )

    def arrival(self, step, item):
        p = self.place
        turn = p.turn(step)
        return remote(
            self.two[item].at[turn],
            self.three[item].at[turn],
            self.sems[4].at[step, item],
            self.sems[5].at[turn, item],
            p.at_outer(turn),
        )

    def start_core(self, step):
        for item in self.items:
            self.core_copy(step, item).start()

    def core_to_mid(self, step):
        p = self.place
        turn = p.turn(step)
        for item in self.items:
            self.core_copy(step, item).wait_recv()
            one = self.one[item]
            for mid in range(2):
                add_into(one.at[turn, mid], one.at[turn, mid], self.sources[item].at[turn, mid, p.core])
            self.mid_copy(step, item).start()

    def mid_to_outer(self, step, last):
        p = self.place
        turn = p.turn(step)
        for item in self.items:
            self.mid_copy(step, item).wait_recv()
            two = self.two[item]
            add_into(two.at[turn], two.at[turn], self.one[item].at[turn, p.mid])
            if not last:
                self.outer_copy(step, item).start()

    def finish(self, outs):
        p = self.place
        for item in self.items:
            total = self.two[item][p.outer].astype(F32)
            for step in range(p.outers - 1):
                self.arrival(step, item).wait_recv()
                total = total + self.three[item][p.turn(step)].astype(F32)
            outs[item][...] = total

    def drain(self):
        def one(step, carry):
            for item in self.items:
                self.core_copy(step, item).wait_send()
                self.mid_copy(step, item).wait_send()
            return carry

        lax.fori_loop(0, self.place.outers, one, 0)
        for step in range(self.place.outers - 1):
            for item in self.items:
                self.outer_copy(step, item).wait_send()


def scatter_shapes(sources):
    one = [pltpu.VMEM((s.shape[0], 2) + s.shape[3:], s.dtype) for s in sources]
    two = [pltpu.VMEM((s.shape[0],) + s.shape[3:], s.dtype) for s in sources]
    three = [pltpu.VMEM((s.shape[0],) + s.shape[3:], s.dtype) for s in sources]
    sems = [pltpu.SemaphoreType.DMA((sources[0].shape[0], len(sources))) for _ in range(6)]
    return one + two + three + sems


class IdGather:
    def __init__(self, place, every, sems):
        self.place, self.every, self.sems = place, every, sems

    def copy(self, stage, step, theirs=0):
        p = self.place
        turn = lax.rem(p.outer + step, p.outers)
        if stage == 0:
            at = turn if theirs else p.outer
            part, peer, mark = self.every.at[at, p.mid, p.core], p.at_outer(turn), at
        elif stage == 1:
            mid = 1 - p.mid if theirs else p.mid
            part, peer, mark = self.every.at[turn, mid, p.core], p.other_mid(), step
        else:
            core = 1 - p.core if theirs else p.core
            part, peer, mark = self.every.at[turn, :, core], p.other_core(), step
        return remote(part, part, self.sems[2 * stage].at[step], self.sems[2 * stage + 1].at[mark], peer)


class Swap:
    def __init__(self, place, src, dst, send, recv):
        self.place, self.src, self.dst, self.send, self.recv = place, src, dst, send, recv

    def copy(self, at, src_rows, dst_rows):
        return remote(
            self.src.at[src_rows], self.dst.at[dst_rows], self.send.at[at], self.recv.at[at], self.place.other_side()
        )


def rows_from(start, size):
    return pl.ds(pl.multiple_of(start, size), size)


def feed_forward_kernel(
    ids, x_in, cot, wu_in, bu, wd_in, hidden, vectors, wo_in, mixed, q_in, k_in, v_in, lse, fq_ref, fk_ref, others,
    wo_other_in, every, layer, hg, norm_sums, wo_out, dwd_out, dwu_out, alone_out, dq_out, dk_out, dv_out,
    act, ug, xt, xg, rg, mgs, mgr, wu, wd, dbu, dbd, qs, ks, kt, gs, delta, scores, slopes,
    wo_sum, wo_recv, src_d, src_u, src_a, src_o, *rest,
):
    scatter_refs, rest = rest[:15], rest[15:]
    out_refs, rest = rest[:9], rest[9:]
    id_sems, (send_x, recv_x, send_h, recv_h, send_d, recv_d, send_l, recv_l, local) = rest[:6], rest[6:]
    tokens, width = x_in.shape
    features = wu.shape[1]
    columns = wo_in.shape[0]
    x = layer
    wo, wo_other = layer.at[:columns], layer.at[columns : 2 * columns]
    gain, bd = vectors[2:3, :], vectors[4:5, :]
    half = tokens // 2
    chunk, part, piece = 256, 512, 128
    place = Place()
    outers = place.outers
    work = Scatter(
        place, [src_d, src_u, src_a], scatter_refs[0:3], scatter_refs[3:6], scatter_refs[6:9], scatter_refs[9:]
    )
    after = Scatter(place, [src_o], out_refs[0:1], out_refs[1:2], out_refs[2:3], out_refs[3:])
    known = IdGather(place, every, id_sems)
    every[place.outer, place.mid, place.core] = ids[...]
    mine_at, other_at = place.side * half, (1 - place.side) * half
    grads = Swap(place, xg, rg, send_x, recv_x)
    mixes = Swap(place, mgs, mgr, send_h, recv_h)
    downs = Swap(place, xg, rg, send_d, recv_d)
    layers = Swap(place, layer, layer, send_l, recv_l)
    dbu[...] = jnp.zeros_like(dbu)
    dbd[...] = jnp.zeros_like(dbd)
    src_a[...] = jnp.zeros_like(src_a)
    norm_sums[...] = jnp.zeros_like(norm_sums)
    loads = [
        pltpu.make_async_copy(src, dst, local.at[at])
        for at, (src, dst) in enumerate(((x_in, x), (wu_in, wu), (wd_in, wd)))
    ]
    for copy in loads:
        copy.start()
    greet(place, True)
    for copy in loads:
        copy.wait()

    def loop(low, high, stage):
        lax.fori_loop(low, high, lambda step, carry: (stage(step), carry)[1], 0)

    def ids_mid(step):
        known.copy(0, step, 1).wait_recv()
        known.copy(1, step).start()

    def ids_core(step):
        known.copy(1, step, 1).wait_recv()
        known.copy(2, step).start()

    loop(1, outers, lambda step: known.copy(0, step).start())
    known.copy(1, 0).start()

    def forward(start):
        rows = rows_from(start, chunk)
        xc = x[rows, :]
        gc = cot[rows, :]
        xt[:, rows] = xc.T
        dbd[...] += jnp.sum(gc.astype(F32), axis=0, keepdims=True)
        total = jnp.zeros((chunk, width), F32)
        for at in range(features // part):
            cols = slice(at * part, (at + 1) * part)
            up = product(xc, wu[:, cols]) + bu[:, cols]
            square = up * up
            gate = 0.5 + 0.5 * jnp.tanh(up * (gelu_slope + (gelu_slope * gelu_cubic) * square))
            value = up * gate
            act[rows, cols] = value.astype(BF)
            slope = gate + value * (1.0 - gate) * (
                2.0 * gelu_slope + (6.0 * gelu_slope * gelu_cubic) * square
            )
            low = (times_back(gc, wd[cols, :]) * slope).astype(BF)
            ug[rows, cols] = low
            dbu[:, cols] += jnp.sum(low.astype(F32), axis=0, keepdims=True)
            total = total + times_back(low, wu[:, cols])
        xg[rows, :] = total.astype(BF)

    def sent(at):
        return grads.copy(at, rows_from(other_at + at * chunk, chunk), rows_from(at * chunk, chunk))

    def theirs(at):
        forward(other_at + at * chunk)
        sent(at).start()

    loop(0, half // chunk, theirs)
    loop(0, half // chunk, lambda at: forward(mine_at + at * chunk))
    heads_in = [
        pltpu.make_async_copy(src, wu.at[:, at * columns : (at + 1) * columns], local.at[at])
        for at, src in enumerate((q_in, k_in, v_in))
    ] + [
        pltpu.make_async_copy(src, dst, local.at[3 + at])
        for at, (src, dst) in enumerate(((wo_in, wo), (wo_other_in, wo_other)))
    ]
    for copy in heads_in:
        copy.start()
    loop(1, outers, ids_mid)
    dp_size = 4 * outers
    up_lanes, down_lanes = features // dp_size, width // dp_size
    for at in range(dp_size):
        spot = (at // 4, (at // 2) % 2, at % 2)
        src_a[spot + (slice(0, 1), slice(0, up_lanes))] = dbu[:, at * up_lanes : (at + 1) * up_lanes]
        src_a[spot + (slice(1, 2), slice(0, down_lanes))] = dbd[:, at * down_lanes : (at + 1) * down_lanes]

    down_rows, up_rows = features // outers // 2, width // outers

    def weight_grads(step):
        turn = place.turn(step)
        if down_rows % LANES:
            cols = rows_from(turn * (2 * down_rows), 2 * down_rows)
            src_d[turn] = contract_rows(act[:, cols], cot[...]).astype(BF).reshape(2, 2, down_rows // 2, width)
        else:
            for mid in range(2):
                cols = rows_from(turn * (2 * down_rows) + mid * down_rows, down_rows)
                src_d[turn, mid] = contract_rows(act[:, cols], cot[...]).astype(BF).reshape(2, down_rows // 2, width)
        rows = rows_from(turn * up_rows, up_rows)
        for at in range(features // part):
            cols = slice(at * part, (at + 1) * part)
            src_u[turn, :, :, :, cols] = (
                product(xt[rows, :], ug[:, cols]).astype(BF).reshape(2, 2, up_rows // 4, part)
            )
        work.start_core(step)

    def norm_grads(at):
        @pl.when(at % (chunk // piece) == 0)
        def _():
            sent(at // (chunk // piece)).wait_recv()

        here = rows_from(at * piece, piece)
        rows = rows_from(mine_at + at * piece, piece)
        grad = xg[rows, :].astype(F32) + rg[here, :].astype(F32)
        _, unit, inverse = normalize(hidden[here, :], 1.0, 0.0)
        back, gain_sum, bias_sum = norm_back(grad, unit, inverse, gain)
        norm_sums[0:1, :] += gain_sum[None, :]
        norm_sums[1:2, :] += bias_sum[None, :]
        total = cot[rows, :].astype(F32) + back
        hg[here, :] = total.astype(BF)

    def mix_copy(at):
        here = rows_from(at * chunk, chunk)
        return mixes.copy(at, here, here)

    def mixed_grads(at):
        here = rows_from(at * chunk, chunk)
        mgs[here, :] = times_back(hg[here, :], wo_other[...]).astype(BF)
        mix_copy(at).start()
        wu[rows_from(mine_at + at * chunk, chunk), 3 * columns :] = times_back(hg[here, :], wo[...]).astype(BF)

    weight_grads(0)
    weight_grads(1)
    work.core_to_mid(0)
    loop(0, half // piece, norm_grads)
    for copy in heads_in:
        copy.wait()
    loop(0, half // chunk, mixed_grads)
    rows_o = columns // dp_size
    turned = (mixed[rows_from(mine_at, half), :].T, others[...].T)
    for which in range(2):
        for at in range(0, width, BLOCK):
            src_o[:, :, :, which * rows_o : (which + 1) * rows_o, at : at + BLOCK] = (
                product(turned[which], hg[:, at : at + BLOCK]).astype(BF).reshape(outers, 2, 2, rows_o, BLOCK)
            )
    loop(0, outers, after.start_core)

    def more(step):
        weight_grads(step)
        work.core_to_mid(step - 1)

    loop(2, outers, more)
    loop(0, outers, after.core_to_mid)
    work.core_to_mid(outers - 1)
    loop(0, outers - 3, lambda step: work.mid_to_outer(step, False))
    loop(0, half // chunk, lambda at: sent(at).wait_send())

    def downward(start):
        rows = rows_from(start, chunk)
        xg[rows, :] = product(act[rows, :], wd[...]).astype(BF)

    def down_sent(at):
        return downs.copy(at, rows_from(other_at + at * piece, piece), rows_from(at * piece, piece))

    def down_theirs(at):
        downward(other_at + at * chunk)
        mix_copy(at).wait_recv()

    loop(0, half // chunk, down_theirs)
    loop(0, half // piece, lambda at: down_sent(at).start())
    wu[rows_from(other_at, half), 3 * columns :] = mgr[...]
    loop(0, half // chunk, lambda at: downward(mine_at + at * chunk))
    work.mid_to_outer(outers - 3, False)
    loop(0, outers, ids_core)

    def layer_copy(at, start):
        rows = rows_from(start + at * piece, piece)
        return layers.copy(at, rows, rows)

    def layer_rows(at):
        down_sent(at).wait_recv()
        here = rows_from(at * piece, piece)
        rows = rows_from(mine_at + at * piece, piece)
        layer[rows, :] = (
            hidden[here, :] + (xg[rows, :].astype(F32) + rg[here, :].astype(F32)) + bd
        ).astype(BF)
        layer_copy(at, mine_at).start()

    blocks = tokens // BLOCK
    scale = HEAD_DIM**-0.5

    def one_pair(at):
        def lanes_of(which):
            return pl.ds(pl.multiple_of(which * columns + at * LANES, LANES), LANES)

        keys, grad = wu[:, lanes_of(1)], wu[:, lanes_of(3)]
        scaled = (wu[:, lanes_of(0)].astype(F32) * scale).astype(BF)
        for head in range(2):
            mine = head_lanes(tokens, head)
            qs[head, :, :LANES] = jnp.where(mine, scaled, jnp.zeros_like(scaled))
            qs[head, :, LANES:] = fq_ref[...]
            gs[head] = jnp.where(mine, grad, jnp.zeros_like(grad))
        ks[:, :LANES] = keys
        ks[:, LANES:] = fk_ref[...]
        kt[...] = keys.T
        both = (grad.astype(F32) * mixed[:, lanes_of(0)].astype(F32)).T
        for head in range(2):
            delta[head : head + 1, :] = jnp.sum(
                both[head * HEAD_DIM : (head + 1) * HEAD_DIM], axis=0, keepdims=True
            )
        for block in range(blocks):
            here = slice(block * BLOCK, (block + 1) * BLOCK)
            low, high = near(block, blocks)
            dq = []
            for head in range(2):
                scores[head, low:high, :] = times_back(ks[low:high, :], qs[head, here, :])
                slopes[head, low:high, :] = times_back(wu[low:high, lanes_of(2)], gs[head, here, :])
            for head in range(2):
                offset, shift = lse[at, head : head + 1, here], delta[head : head + 1, here]
                columns_here = slice(head * tokens + block * BLOCK, head * tokens + (block + 1) * BLOCK)
                for at_key in range(low, high, STRIP):
                    strip = slice(at_key, at_key + STRIP)
                    prob = jnp.exp(scores[head, strip, :] - offset)
                    act[strip, columns_here] = prob.astype(BF)
                    ug[strip, columns_here] = (prob * (slopes[head, strip, :] - shift)).astype(BF)
                dq.append(product(kt[head * HEAD_DIM : (head + 1) * HEAD_DIM, low:high], ug[low:high, columns_here]))
            wd[here, lanes_of(0)] = (jnp.concatenate(dq, axis=0).T * scale).astype(BF)
        for block in range(blocks):
            here = slice(block * BLOCK, (block + 1) * BLOCK)
            low, high = near(block, blocks)
            dk = jnp.zeros((BLOCK, LANES), F32)
            dv = jnp.zeros((BLOCK, LANES), F32)
            for head in range(2):
                dv = dv + product(act[here, head * tokens + low : head * tokens + high], gs[head, low:high, :])
                dk = dk + product(ug[here, head * tokens + low : head * tokens + high], qs[head, low:high, :LANES])
            wd[here, lanes_of(1)] = dk.astype(BF)
            wd[tokens + block * BLOCK : tokens + (block + 1) * BLOCK, lanes_of(0)] = dv.astype(BF)

        @pl.when(at == 0)
        def _():
            work.mid_to_outer(outers - 2, False)
            loop(0, outers - 1, lambda step: after.mid_to_outer(step, False))
            after.mid_to_outer(outers - 1, True)

        @pl.when(at == 1)
        def _():
            work.mid_to_outer(outers - 1, True)
            loop(0, half // piece, layer_rows)

    loop(0, columns // LANES, one_pair)
    grads_out = [
        pltpu.make_async_copy(src, dst, local.at[at])
        for at, (src, dst) in enumerate(
            (
                (wd.at[:tokens, :columns], dq_out),
                (wd.at[:tokens, columns : 2 * columns], dk_out),
                (wd.at[tokens : 2 * tokens, :columns], dv_out),
            )
        )
    ]
    for copy in grads_out:
        copy.start()
    after.finish([wo_sum])
    wo_swap = remote(
        wo_sum.at[pl.ds(rows_o, rows_o)], wo_recv, send_h.at[half // chunk], recv_h.at[half // chunk], place.other_side()
    )
    wo_swap.start()
    work.finish([dwd_out, dwu_out, alone_out])
    for copy in grads_out:
        copy.wait()
    wo_swap.wait()
    wo_out[...] = wo_sum[:rows_o, :] + wo_recv[...]
    work.drain()
    after.drain()
    loop(0, outers, lambda step: known.copy(2, step, 1).wait_recv())
    loop(1, outers, lambda step: known.copy(0, step).wait_send())
    loop(0, outers, lambda step: known.copy(1, step).wait_send())
    loop(0, outers, lambda step: known.copy(2, step).wait_send())

    def swaps_done(at):
        rows = rows_from(mine_at + at * piece, piece)
        down_sent(at).wait_send()
        layer_copy(at, other_at).wait_recv()
        layer_copy(at, mine_at).wait_send()

    loop(0, half // piece, swaps_done)
    loop(0, half // chunk, lambda at: mix_copy(at).wait_send())


def feed_forward(dp_size, collective_id, *operands):
    ids, x, _, wu, _, wd, _, _, wo, _, queries, *_ = operands
    tokens, width = x.shape
    columns = wo.shape[0]
    features = wu.shape[1]
    half = tokens // 2
    outers = dp_size // 4
    shape = jax.ShapeDtypeStruct
    items = [
        shape((outers, 2, 2, features // dp_size, width), BF),
        shape((outers, 2, 2, width // dp_size, features), BF),
        shape((outers, 2, 2, 8, LANES), F32),
    ]
    item_o = shape((outers, 2, 2, 2 * columns // dp_size, width), BF)
    anywhere = pl.BlockSpec(memory_space=pl.ANY)
    return pl.pallas_call(
        feed_forward_kernel,
        in_specs=[anywhere if at in (1, 3, 5, 8, 10, 11, 12, 17) else full_spec() for at in range(len(operands))],
        out_specs=[full_spec()] * 8 + [anywhere] * 3,
        out_shape=[
            shape((outers, 2, 2) + ids.shape, ids.dtype),
            shape((tokens, width), BF),
            shape((half, width), BF),
            shape((2, width), F32),
            shape((wo.shape[0] // dp_size, width), F32),
        ]
        + [shape(item.shape[3:], F32) for item in items]
        + [shape(queries.shape, BF)] * 3,
        scratch_shapes=[
            pltpu.VMEM((tokens, features), BF),
            pltpu.VMEM((tokens, features), BF),
            pltpu.VMEM((width, tokens), BF),
            pltpu.VMEM((tokens, width), BF),
            pltpu.VMEM((half, width), BF),
            pltpu.VMEM((half, columns), BF),
            pltpu.VMEM((half, columns), BF),
            pltpu.VMEM(wu.shape, BF),
            pltpu.VMEM(wd.shape, BF),
            pltpu.VMEM((1, features), F32),
            pltpu.VMEM((1, width), F32),
            pltpu.VMEM((2, tokens, 2 * LANES), BF),
            pltpu.VMEM((tokens, 2 * LANES), BF),
            pltpu.VMEM((LANES, tokens), BF),
            pltpu.VMEM((2, tokens, LANES), BF),
            pltpu.VMEM((2, tokens), F32),
            pltpu.VMEM((2, tokens, BLOCK), F32),
            pltpu.VMEM((2, tokens, BLOCK), F32),
            pltpu.VMEM(item_o.shape[3:], F32),
            pltpu.VMEM((columns // dp_size, width), F32),
        ]
        + [pltpu.VMEM(item.shape, item.dtype) for item in items + [item_o]]
        + scatter_shapes(items)
        + scatter_shapes([item_o])
        + [pltpu.SemaphoreType.DMA((outers,)) for _ in range(6)]
        + [pltpu.SemaphoreType.DMA((half // 256,)) for _ in range(2)]
        + [pltpu.SemaphoreType.DMA((half // 128,)) for _ in range(6)]
        + [pltpu.SemaphoreType.DMA((5,))],
        compiler_params=pltpu.CompilerParams(
            vmem_limit_bytes=60 * 1024 * 1024, collective_id=collective_id, has_side_effects=True
        ),
        name="feed_forward",
    )(*operands)


def front_kernel(
    rows_ref, noise, scales, w_in, vectors, wq, wk, wv, fq_ref, fk_ref, wo,
    q_out, k_out, v_out, n1t_out, stream_out, others_out, wo_out, inputs_out, mixed, lse, hidden_out, x2,
    q, k, v, n1t, stream_own, stream, theirs, wo_other, others, qs, ks, vt, scores, probs, inputs,
    send_r, recv_r, send_m, recv_m, local,
):
    tokens, width = stream.shape
    half = tokens // 2
    chunk = 256
    pairs = q.shape[1] // LANES
    place = Place()
    mine_at = place.side * half
    barrier = pltpu.get_barrier_semaphore()
    for peer in (place.other_side(), place.other_core()):
        pl.semaphore_signal(barrier, inc=1, device_id=peer, device_id_type=MESH)
    pl.semaphore_wait(barrier, 2)

    def loop(low, high, stage):
        lax.fori_loop(low, high, lambda step, carry: (stage(step), carry)[1], 0)

    def row_copy(at):
        span = rows_from(at * chunk, chunk)
        return remote(rows_ref.at[span], theirs.at[span], send_r.at[at], recv_r.at[at], place.other_side())

    count = tokens // chunk
    part = wo.shape[0] // 2

    def weights(step):
        rows = rows_from(place.core * part, part)
        src = wo_other if step else wo
        peer = place.other_core() if step else place.other_side()
        return remote(src.at[rows], wo_other.at[rows], send_r.at[count + step], recv_r.at[count + step], peer)

    loop(0, count, lambda at: row_copy(at).start())
    weights(0).start()

    def start_of(at):
        row_copy(at).wait_recv()
        span = rows_from(at * chunk, chunk)
        embedded = rows_ref[span, :].astype(F32) + theirs[span, :].astype(F32)
        low = (scales[0:1, 0:1] * (embedded + scales[1:2, 0:1] * noise[span, :].astype(F32))).astype(BF)
        inputs[span, :] = low
        flow = product(low, w_in[...])
        stream[span, :] = flow
        normed, _, _ = normalize(flow, vectors[0:1, :], vectors[1:2, :])
        normed = normed.astype(BF)
        n1t[:, span] = normed.T
        q[span, :] = product(normed, wq[...]).astype(BF)
        k[span, :] = product(normed, wk[...]).astype(BF)
        v[span, :] = product(normed, wv[...]).astype(BF)

    loop(0, count, start_of)

    def keep(at):
        span = rows_from(at * chunk, chunk)
        stream_own[span, :] = stream[rows_from(mine_at + at * chunk, chunk), :]

    loop(0, half // chunk, keep)
    kept = [
        pltpu.make_async_copy(src, dst, local.at[at])
        for at, (src, dst) in enumerate(
            ((q, q_out), (k, k_out), (v, v_out), (n1t, n1t_out), (stream_own, stream_out))
        )
    ]
    for copy in kept:
        copy.start()

    blocks = tokens // BLOCK
    scale = HEAD_DIM**-0.5

    def pair_copy(at):
        lanes = pl.ds(pl.multiple_of(at * LANES, LANES), LANES)
        return remote(mixed.at[:, lanes], others.at[:, lanes], send_m.at[at], recv_m.at[at], place.other_side())

    def one_pair(at):
        lanes = pl.ds(pl.multiple_of(at * LANES, LANES), LANES)
        scaled = (q[:, lanes].astype(F32) * scale).astype(BF)
        for head in range(2):
            qs[head, :, :LANES] = jnp.where(head_lanes(tokens, head), scaled, jnp.zeros_like(scaled))
            qs[head, :, LANES:] = fq_ref[...]
        ks[:, :LANES] = k[:, lanes]
        ks[:, LANES:] = fk_ref[...]
        vt[...] = v[:, lanes].T
        for block in range(blocks):
            here = slice(block * BLOCK, (block + 1) * BLOCK)
            low, high = near(block, blocks)
            found = []
            for head in range(2):
                scores[head, low:high, :] = times_back(ks[low:high, :], qs[head, here, :])
            for head in range(2):
                peak = jnp.full((8, BLOCK), masked_score, F32)
                for at_key in range(low, high, STRIP):
                    strip = scores[head, at_key : at_key + STRIP, :].reshape(STRIP // 8, 8, BLOCK)
                    peak = jnp.maximum(peak, jnp.max(strip, axis=0))
                peak = jnp.max(peak, axis=0, keepdims=True)
                total = jnp.zeros((8, BLOCK), F32)
                for at_key in range(low, high, STRIP):
                    strip = jnp.exp(scores[head, at_key : at_key + STRIP, :] - peak)
                    total = total + jnp.sum(strip.reshape(STRIP // 8, 8, BLOCK), axis=0)
                    probs[head, at_key : at_key + STRIP, :] = strip.astype(BF)
                total = jnp.sum(total, axis=0, keepdims=True)
                values = vt[head * HEAD_DIM : (head + 1) * HEAD_DIM, low:high]
                found.append(product(values, probs[head, low:high, :]) / total)
                lse[at, head : head + 1, here] = peak + jnp.log(total)
            mixed[here, lanes] = jnp.concatenate(found, axis=0).T.astype(BF)
        pair_copy(at).start()

        @pl.when(at == 1)
        def _():
            weights(0).wait_recv()
            weights(1).start()

    loop(0, pairs, one_pair)

    def ours(at):
        span = rows_from(at * chunk, chunk)
        stream[span, :] += product(mixed[span, :], wo[...])

    loop(0, count, ours)
    weights(1).wait_recv()
    loop(0, pairs, lambda at: pair_copy(at).wait_recv())
    kept += [
        pltpu.make_async_copy(src, dst, local.at[5 + at])
        for at, (src, dst) in enumerate(((others.at[rows_from(mine_at, half)], others_out), (wo_other, wo_out)))
    ]
    for copy in kept[5:]:
        copy.start()

    def finish(at):
        span = rows_from(at * chunk, chunk)
        hidden = stream[span, :] + product(others[span, :], wo_other[...])
        stream[span, :] = hidden
        normed, _, _ = normalize(hidden, vectors[2:3, :], vectors[3:4, :])
        x2[span, :] = normed.astype(BF)

    loop(0, count, finish)
    hidden_out[...] = stream[rows_from(mine_at, half), :]
    inputs_out[...] = inputs[rows_from(mine_at, half), :]
    loop(0, count, lambda at: row_copy(at).wait_send())
    weights(0).wait_send()
    weights(1).wait_send()
    loop(0, pairs, lambda at: pair_copy(at).wait_send())
    for copy in kept:
        copy.wait()


def front(rows, noise, scales, w_in, vectors, wq, wk, wv, fq, fk, wo, collective_id):
    tokens, embed = rows.shape
    width, columns = wq.shape
    half = tokens // 2
    pairs = columns // LANES
    count = tokens // 256
    shape = jax.ShapeDtypeStruct
    head = shape((tokens, columns), BF)
    scratch = pltpu.VMEM
    return pl.pallas_call(
        front_kernel,
        in_specs=[full_spec()] * 11,
        out_specs=[pl.BlockSpec(memory_space=pl.ANY)] * 7 + [full_spec()] * 5,
        out_shape=[
            head,
            head,
            head,
            shape((width, tokens), BF),
            shape((half, width), F32),
            shape((half, columns), BF),
            shape(wo.shape, BF),
            shape((half, embed), BF),
            head,
            shape((pairs, 2, tokens), F32),
            shape((half, width), F32),
            shape((tokens, width), BF),
        ],
        scratch_shapes=[
            scratch(head.shape, BF),
            scratch(head.shape, BF),
            scratch(head.shape, BF),
            scratch((width, tokens), BF),
            scratch((half, width), F32),
            scratch((tokens, width), F32),
            scratch(rows.shape, BF),
            scratch(wo.shape, BF),
            scratch(head.shape, BF),
            scratch((2, tokens, 2 * LANES), BF),
            scratch((tokens, 2 * LANES), BF),
            scratch((LANES, tokens), BF),
            scratch((2, tokens, BLOCK), F32),
            scratch((2, tokens, BLOCK), BF),
            scratch(rows.shape, BF),
        ]
        + [pltpu.SemaphoreType.DMA((count + 2,)) for _ in range(2)]
        + [pltpu.SemaphoreType.DMA((pairs,)) for _ in range(2)]
        + [pltpu.SemaphoreType.DMA((7,))],
        compiler_params=pltpu.CompilerParams(
            vmem_limit_bytes=VMEM_LIMIT, collective_id=collective_id, has_side_effects=True
        ),
        name="front",
    )(rows, noise, scales, w_in, vectors, wq, wk, wv, fq, fk, wo)


class Gather:
    def __init__(self, place, every, sems):
        self.place, self.every, self.sems = place, every, sems

    def turn(self, step):
        return lax.rem(self.place.outer + step, self.place.outers)

    def copy(self, stage, piece, step, theirs=0):
        p = self.place
        turn = self.turn(step)
        mark = step
        if stage == 0:
            at = turn if theirs else p.outer
            part = self.every.at[at, p.mid, p.core, p.side, piece]
            peer, mark = p.at_outer(turn), at
        elif stage == 3:
            core = 1 - p.core if theirs else p.core
            part, peer = self.every.at[turn, :, core, :, piece], p.other_core()
        elif (stage == 1) == (piece % 2 == 0):
            side = 1 - p.side if theirs else p.side
            mid = slice(None) if piece % 2 else p.mid
            part, peer = self.every.at[turn, mid, p.core, side, piece], p.other_side()
        else:
            mid = 1 - p.mid if theirs else p.mid
            side = p.side if piece % 2 else slice(None)
            part, peer = self.every.at[turn, mid, p.core, side, piece], p.other_mid()
        sems = self.sems[2 * stage : 2 * stage + 2]
        return remote(part, part, sems[0].at[piece, step], sems[1].at[piece, mark], peer)


def tail_kernel(
    vocab_part,
    large,
    dq, dk, dv, n1t_in, wq, wk, wv, stream_in, hgrad_in, vectors, w_in, inputs, scales, ids, mine, sums_two,
    qkv_out, w_in_out, sides_out, noise, table,
    every, n1t, stream, hgrad, part, rpart, nsend, nrecv, stage_in, stage_out, picked, total, sums,
    src_q, src_w, src_s, side_w, side_s, *rest,
):
    early_refs, rest = rest[:9], rest[9:]
    late_refs, rest = rest[:12], rest[12:]
    gather_sems, rest = rest[:8], rest[8:]
    send_x, recv_x, send_n, recv_n, send_s, recv_s, local = rest
    width, tokens = n1t.shape
    columns = wq.shape[1]
    half = tokens // 2
    chunk, piece = 256, half // 4
    place = Place()
    outers = place.outers
    early = Scatter(place, [src_q], early_refs[0:1], early_refs[1:2], early_refs[2:3], early_refs[3:])
    late = Scatter(place, [src_w, src_s], late_refs[0:2], late_refs[2:4], late_refs[4:6], late_refs[6:])
    gather = Gather(place, every, gather_sems)
    mine_at, other_at = place.side * half, (1 - place.side) * half
    grads = Swap(place, part, rpart, send_x, recv_x)
    noises = Swap(place, nsend, nrecv, send_n, recv_n)
    loads = [
        pltpu.make_async_copy(src, dst, local.at[at])
        for at, (src, dst) in enumerate(((n1t_in, n1t), (stream_in, stream), (hgrad_in, hgrad)))
    ]
    for copy in loads:
        copy.start()
    sums[...] = jnp.zeros_like(sums)
    src_s[...] = jnp.zeros_like(src_s)
    total[...] = jnp.zeros_like(total)
    sums[2:4, :] = sums_two[...]
    greet(place, True)

    def loop(low, high, stage):
        lax.fori_loop(low, high, lambda step, carry: (stage(step), carry)[1], 0)

    def back_product(start):
        rows = rows_from(start, chunk)
        part[rows, :] = (
            times_back(dq[rows, :], wq[...])
            + times_back(dk[rows, :], wk[...])
            + times_back(dv[rows, :], wv[...])
        ).astype(BF)

    def sent(at):
        return grads.copy(at, rows_from(other_at + at * piece, piece), rows_from(at * piece, piece))

    def theirs(at):
        back_product(other_at + at * chunk)
        for step in range(chunk // piece):
            sent(at * (chunk // piece) + step).start()

    loop(0, half // chunk, theirs)
    for copy in loads:
        copy.wait()
    group = width // outers

    def weight_grads(step):
        turn = place.turn(step)
        rows = rows_from(turn * group, group)
        for at, grad in enumerate((dq, dk, dv)):
            src_q[turn, :, :, :, at * columns : (at + 1) * columns] = (
                product(n1t[rows, :], grad[...]).astype(BF).reshape(2, 2, group // 4, columns)
            )
        early.start_core(step)

    weight_grads(0)

    def more(step):
        weight_grads(step)
        early.core_to_mid(step - 1)

    loop(1, outers, more)
    loop(0, half // chunk, lambda at: back_product(mine_at + at * chunk))
    early.core_to_mid(outers - 1)

    def noise_copy(which):
        rows = pl.ds(which * piece, piece)
        return noises.copy(which, rows, rows)

    def norm_grads(which):
        sent(which).wait_recv()
        here = slice(which * piece, (which + 1) * piece)
        rows = rows_from(mine_at + which * piece, piece)
        grad = part[rows, :].astype(F32) + rpart[here, :].astype(F32)
        _, unit, inverse = normalize(stream[here, :], 1.0, 0.0)
        back, gain_sum, bias_sum = norm_back(grad, unit, inverse, vectors[0:1, :])
        low = (hgrad[here, :].astype(F32) + back).astype(BF)
        back_in = times_back(low, w_in[...])
        spot = every.at[place.outer, place.mid, place.core, place.side, which]
        found = (scales[0:1, 0:1] * back_in).astype(BF)
        if large:
            stage_out[...] = found
            moved = pltpu.make_async_copy(stage_out, spot, local.at[0])
            moved.start()
            moved.wait()
        else:
            spot[...] = found
        loop(1, outers, lambda step: gather.copy(0, which, step).start())
        gather.copy(1, which, 0).start()
        sums[0:1, :] += gain_sum[None, :]
        sums[1:2, :] += bias_sum[None, :]
        rpart[here, :] = low
        noised = (scales[0:1, 0:1] * scales[1:2, 0:1]) * back_in
        noise[rows, :] = noised
        nsend[here, :] = noised.astype(BF)

    dp_size = 4 * outers

    def start_late():
        for which in range(4):
            noise_copy(which).start()
        rows_w = w_in.shape[0] // dp_size
        lanes = width // dp_size
        work = contract_rows(inputs[...], rpart[...])
        for at in range(dp_size):
            spot = (at // 4, (at // 2) % 2, at % 2)
            src_w[spot] = work[at * rows_w : (at + 1) * rows_w, :].astype(src_w.dtype)
            src_s[spot + (slice(None), slice(0, lanes))] = sums[:, at * lanes : (at + 1) * lanes]
        loop(0, outers, late.start_core)

    def forward(stage, which, step):
        gather.copy(stage - 1, which, step, 1).wait_recv()
        gather.copy(stage, which, step).start()

    owned = table.shape[0]
    wanted = lax.broadcasted_iota(jnp.int32, (total.shape[0], 1), 0)
    first = place.side * vocab_part + place.dp * owned

    def collect(pair, step):
        turn = gather.turn(step)
        for which in (2 * pair, 2 * pair + 1):
            gather.copy(3, which, step, 1).wait_recv()
        pieces = every.at[turn, :, :, :, 2 * pair : 2 * pair + 2]
        if large:
            moved = pltpu.make_async_copy(pieces, stage_in, local.at[0])
            moved.start()
            moved.wait()
            pieces = stage_in
        for spot in range(8):
            mid, core, side = spot // 4, (spot // 2) % 2, spot % 2
            for at in range(2):
                line = 4 * side + 2 * pair + at
                lanes = slice((2 * spot + at) * LANES, (2 * spot + at + 1) * LANES)
                picked[:, lanes] = ((ids[turn, mid, core, line : line + 1, :] - first) == wanted).astype(BF)
        total[...] += product(picked[...], pieces[...].reshape(16 * piece, -1))

    sided = []
    for slot in range(8):
        if slot < 4:
            norm_grads(slot)
            if slot == 3:
                start_late()
        if 1 <= slot < 5:
            loop(1, outers, lambda step: forward(1, slot - 1, step))
            forward(2, slot - 1, 0)
        if 2 <= slot < 6:
            loop(1, outers, lambda step: forward(2, slot - 2, step))
            forward(3, slot - 2, 0)
        if 3 <= slot < 7:
            loop(1, outers, lambda step: forward(3, slot - 3, step))
        if slot == 4:
            loop(0, outers - 1, lambda step: early.mid_to_outer(step, False))
            early.mid_to_outer(outers - 1, True)
            loop(0, outers, late.core_to_mid)
        if slot == 5:
            loop(0, outers, lambda step: collect(0, step))
            loop(0, outers - 1, lambda step: late.mid_to_outer(step, False))
            late.mid_to_outer(outers - 1, True)
        if slot == 6:
            early.finish([qkv_out])
            late.finish([w_in_out, sides_out])
            for at, (out, buffer) in enumerate(((w_in_out, side_w), (sides_out, side_s))):
                buffer[0] = out[...]
                sided.append(remote(buffer.at[0], buffer.at[1], send_s.at[at], recv_s.at[at], place.other_side()))
                sided[at].start()
        if slot == 7:
            loop(0, outers, lambda step: collect(1, step))
    for which in range(4):
        noise_copy(which).wait()
    noise[rows_from(other_at, half), :] = nrecv[...].astype(F32)
    mine_rows = mine[...].astype(F32)
    scale = row_scale(mine_rows)
    grad = total[...][:owned]
    table[...] = scale * grad - mine_rows * (scale * scale * scale) * jnp.mean(
        grad * mine_rows, axis=1, keepdims=True
    )
    for at, (out, buffer) in enumerate(((w_in_out, side_w), (sides_out, side_s))):
        sided[at].wait()
        out[...] = out[...] + buffer[1]
    early.drain()
    late.drain()
    loop(0, half // piece, lambda at: sent(at).wait_send())

    def done(step):
        for which in range(4):
            for stage in range(1, 4):
                gather.copy(stage, which, step).wait_send()

    loop(0, outers, done)

    def done_outer(step):
        for which in range(4):
            gather.copy(0, which, step).wait_send()

    loop(1, outers, done_outer)


def tail(vocab_part, dp_size, collective_id, *operands):
    (_, _, _, n1t, wq, _, _, stream, _, _, w_in, _, _, _, mine, _) = operands
    width, tokens = n1t.shape
    columns = wq.shape[1]
    half = tokens // 2
    piece = half // 4
    outers = dp_size // 4
    embed = w_in.shape[0]
    owned = mine.shape[0]
    padded = -(-owned // LANES) * LANES
    large = outers > 4
    every_shape = (outers, 2, 2, 2, 4, piece, embed)
    anywhere = pl.BlockSpec(memory_space=pl.ANY)

    def blocks_of(rows, cols, dtype):
        return jax.ShapeDtypeStruct((outers, 2, 2, rows, cols), dtype)

    src_q = blocks_of(width // dp_size, 3 * columns, BF)
    src_w = blocks_of(embed // dp_size, width, F32 if embed // dp_size % 16 else BF)
    src_s = blocks_of(8, LANES, F32)

    def owned_shape(value):
        return jax.ShapeDtypeStruct(value.shape[3:], F32)

    def scratch(shape, dtype):
        return pltpu.VMEM(shape, dtype)

    return pl.pallas_call(
        functools.partial(tail_kernel, vocab_part, large),
        in_specs=[anywhere if at in (3, 7, 8) else full_spec() for at in range(len(operands))],
        out_specs=[full_spec()] * 5 + ([anywhere] if large else []),
        out_shape=[
            owned_shape(src_q),
            owned_shape(src_w),
            owned_shape(src_s),
            jax.ShapeDtypeStruct((tokens, embed), F32),
            jax.ShapeDtypeStruct((owned, embed), F32),
        ]
        + ([jax.ShapeDtypeStruct(every_shape, BF)] if large else []),
        scratch_shapes=([] if large else [scratch(every_shape, BF)])
        + [
            scratch(n1t.shape, BF),
            scratch(stream.shape, F32),
            scratch(stream.shape, BF),
            scratch((tokens, width), BF),
            scratch((half, width), BF),
            scratch((half, embed), BF),
            scratch((half, embed), BF),
            scratch((2, 2, 2, 2, piece, embed) if large else (16, LANES), BF),
            scratch((piece, embed) if large else (16, LANES), BF),
            scratch((padded, 16 * piece), BF),
            scratch((padded, embed), F32),
            scratch((8, width), F32),
            scratch(src_q.shape, BF),
            scratch(src_w.shape, src_w.dtype),
            scratch(src_s.shape, F32),
            scratch((2,) + src_w.shape[3:], F32),
            scratch((2,) + src_s.shape[3:], F32),
        ]
        + scatter_shapes([src_q])
        + scatter_shapes([src_w, src_s])
        + [pltpu.SemaphoreType.DMA((4, outers)) for _ in range(8)]
        + [pltpu.SemaphoreType.DMA((4,)) for _ in range(4)]
        + [pltpu.SemaphoreType.DMA((2,)) for _ in range(2)]
        + [pltpu.SemaphoreType.DMA((3,))],
        compiler_params=pltpu.CompilerParams(
            vmem_limit_bytes=VMEM_LIMIT, collective_id=collective_id, has_side_effects=True
        ),
        name="tail",
    )(*operands)


def results_kernel(columns, layer, noise, table, w_in, qkv, wo, wu, wd, sides, alone, *refs):
    outs, sems = refs[:16], refs[16]
    sources = (
        layer, noise, table, w_in, qkv.at[:, :columns], qkv.at[:, columns : 2 * columns], qkv.at[:, 2 * columns :], wo, wu, wd,
    )
    copies = [pltpu.make_async_copy(src, dst, sems.at[at]) for at, (src, dst) in enumerate(zip(sources, outs[:10]))]
    for copy in copies:
        copy.start()
    for at in range(4):
        outs[10 + at][...] = sides[at, : outs[10 + at].shape[0]]
    for at in range(2):
        outs[14 + at][...] = alone[at, : outs[14 + at].shape[0]]
    for copy in copies:
        copy.wait()


def results(layer, noise, table, w_in, qkv, wo, wu, wd, sides, alone, small, bias_up_size):
    columns = qkv.shape[1] // 3
    shape = jax.ShapeDtypeStruct
    head = shape((qkv.shape[0], columns), F32)
    large = [layer, noise, table, w_in, head, head, head, wo, wu, wd]
    anywhere = pl.BlockSpec(memory_space=pl.ANY)
    return pl.pallas_call(
        functools.partial(results_kernel, columns),
        in_specs=[full_spec()] * 10,
        out_specs=[anywhere] * 10 + [full_spec()] * 6,
        out_shape=[shape(value.shape, value.dtype) for value in large]
        + [shape((small,), F32)] * 4
        + [shape((bias_up_size,), F32), shape((small,), F32)],
        scratch_shapes=[pltpu.SemaphoreType.DMA((10,))],
        name="results",
    )(layer, noise, table, w_in, qkv, wo, wu, wd, sides, alone)


def on_device(
    token_ids,
    segment_ids,
    time_index,
    noise_vec,
    embed_table,
    w_in,
    norm1_gain,
    norm1_bias,
    w_query,
    w_key,
    w_value,
    w_out,
    norm2_gain,
    norm2_bias,
    w_up,
    bias_up,
    w_down,
    bias_down,
    cotangent,
):
    seq_count, length = segment_ids.shape
    tokens = seq_count * length
    half = tokens // 2
    vocab_part = embed_table.shape[0]
    dp_size = lax.axis_size("dp")
    dp_index = lax.axis_index("dp")
    side = lax.axis_index("mp")
    fq, fk = lax.optimization_barrier(attention_masks(segment_ids[0]))
    level_step = jnp.log(time_high / time_low) / (TLEVELS - 1)
    level = time_low * jnp.exp(time_index.astype(F32) * level_step)
    scales = jnp.stack([lax.rsqrt(1.0 + level * level), level])
    rows = gather_rows(token_ids - side * vocab_part, embed_table)
    rows, *small_vectors = lax.optimization_barrier(
        (rows, norm1_gain, norm1_bias, norm2_gain, norm2_bias, bias_down)
    )
    vectors = jnp.stack(small_vectors).astype(F32)
    (
        queries, key_rows, value_rows, normed_one_t, stream_half, mixed_other, w_out_other, inputs_half, mixed_low, log_total, hidden_half, normed_two,
    ) = front(
        rows, noise_vec, scales, w_in, vectors, w_query, w_key, w_value, fq, fk, w_out, 3,
    )
    (
        every_id, layer_out, hidden_grad, norm_two_sums, w_out_grad, w_down_grad, w_up_grad, alone_grad,
        query_grad, key_grad, value_grad,
    ) = feed_forward(
        dp_size, 1, token_ids.reshape(-1, LANES), normed_two, cotangent, w_up, bias_up.astype(F32)[None, :], w_down,
        hidden_half, vectors, w_out, mixed_low, queries, key_rows, value_rows, log_total, fq, fk, mixed_other, w_out_other,
    )
    owned = vocab_part // dp_size
    mine = lax.dynamic_slice_in_dim(embed_table, dp_index * owned, owned, 0)
    qkv_grad, w_in_grad, sides_grad, noise_grad, table_grad, *_ = tail(
        vocab_part, dp_size, 2, query_grad, key_grad, value_grad, normed_one_t, w_query, w_key, w_value,
        stream_half, hidden_grad, vectors, w_in, inputs_half, scales, every_id, mine,
        norm_two_sums,
    )
    width = bias_down.shape[0] // dp_size
    (
        layer, noise, table, w_in_sum, query_sum, key_sum, value_sum, w_out_sum, w_up_sum, w_down_sum,
        gain_one_sum, bias_one_sum, gain_two_sum, bias_two_sum, bias_up_sum, bias_down_sum,
    ) = results(
        layer_out, noise_grad, table_grad, w_in_grad, qkv_grad, w_out_grad, w_up_grad, w_down_grad,
        sides_grad, alone_grad, width, bias_up.shape[0] // dp_size,
    )
    return (
        layer, noise, table, w_in_sum, gain_one_sum, bias_one_sum, query_sum, key_sum, value_sum, w_out_sum,
        gain_two_sum, bias_two_sum, w_up_sum, bias_up_sum, w_down_sum, bias_down_sum,
    )


def solution(mesh):
    placed = (
        P("dp"),
        P("dp", None),
        P("dp"),
        P("dp", None),
        P("mp", None),
        P(),
        P(),
        P(),
        P(None, "mp"),
        P(None, "mp"),
        P(None, "mp"),
        P("mp", None),
        P(),
        P(),
        P(None, "mp"),
        P("mp"),
        P("mp", None),
        P(),
        P("dp", None),
    )
    return jax.shard_map(
        on_device,
        mesh=mesh,
        in_specs=placed,
        out_specs=(
            P("dp", None),
            P("dp", None),
            P(("mp", "dp"), None),
            P("dp", None),
            P("dp"),
            P("dp"),
            P("dp", "mp"),
            P("dp", "mp"),
            P("dp", "mp"),
            P(("mp", "dp"), None),
            P("dp"),
            P("dp"),
            P("dp", "mp"),
            P(("mp", "dp")),
            P(("mp", "dp"), None),
            P("dp"),
        ),
        check_vma=False,
    )
```

```python
import functools

import jax
import jax.numpy as jnp
from jax import lax
from jax.experimental import pallas as pl
from jax.experimental.pallas import tpu as pltpu
from jax.sharding import PartitionSpec as P

HEAD_DIM = 64
TLEVELS = 16
DOCS = 4
MAX_RUN = 512

time_low = 0.5
time_high = 10.0
norm_eps = 1e-05
table_eps = 1e-06
masked_score = -1e30

BF = jnp.bfloat16
F32 = jnp.float32
VMEM_LIMIT = 56 * 1024 * 1024
BLOCK = 256
STRIP = 64
LANES = 128


def to_bf16(value):
    return value.astype(BF)


def product(left, right):
    return jnp.dot(left, right, preferred_element_type=F32)


def contract_rows(left, right):
    return lax.dot_general(left, right, (((0,), (0,)), ((), ())), preferred_element_type=F32)


def times_back(left, right):
    return lax.dot_general(left, right, (((1,), (1,)), ((), ())), preferred_element_type=F32)


def params(limit=VMEM_LIMIT):
    return pltpu.CompilerParams(vmem_limit_bytes=limit)


def cost(flops, nbytes, trans=0):
    return pl.CostEstimate(flops=int(flops), bytes_accessed=int(nbytes), transcendentals=int(trans))


def full_spec():
    return pl.BlockSpec(memory_space=pltpu.VMEM)


def row_scale(table_rows):
    return lax.rsqrt(jnp.mean(table_rows * table_rows, axis=1, keepdims=True) + table_eps)


def normalize(values, gain, bias):
    centred = values - jnp.mean(values, axis=-1, keepdims=True)
    inverse = lax.rsqrt(jnp.mean(centred * centred, axis=-1, keepdims=True) + norm_eps)
    unit_rows = centred * inverse
    return (unit_rows * gain + bias, unit_rows, inverse)


def norm_back(grad, unit_rows, inverse, gain):
    scaled = grad * gain
    spread = (
        scaled
        - jnp.mean(scaled, axis=-1, keepdims=True)
        - unit_rows * jnp.mean(scaled * unit_rows, axis=-1, keepdims=True)
    )
    return (inverse * spread, jnp.sum(grad * unit_rows, axis=0), jnp.sum(grad, axis=0))


def gather_kernel(parts, ids, table, out, staged, wide, picked, sems):
    rows, width = table.shape
    tokens = picked.shape[0]
    step = rows // parts

    def copy(part):
        span = pl.ds(part * step, step)
        return pltpu.make_async_copy(table.at[span], staged.at[span], sems.at[part])

    for part in range(parts):
        copy(part).start()
    wide[pl.ds(rows, 8), :] = jnp.zeros((8, width), F32)
    for part in range(parts):
        copy(part).wait()
        piece = step // 5

        @pl.loop(0, 5)
        def _(at):
            span = pl.ds(pl.multiple_of(part * step + at * piece, 16), piece)
            wide[span, :] = staged[span, :].astype(F32)

    def one(at, carry):
        picked[pl.ds(at, 1), :] = wide[pl.ds(ids[at], 1), :]
        return carry

    lax.fori_loop(0, tokens, one, 0, unroll=8)
    found = picked[...]
    out[...] = (found * row_scale(found)).astype(BF)


def gather_rows(local_ids, table):
    rows, width = table.shape
    local_ids = jnp.where(jnp.logical_and(local_ids >= 0, local_ids < rows), local_ids, rows)
    tokens = local_ids.shape[0]
    parts = 5
    return pl.pallas_call(
        functools.partial(gather_kernel, parts),
        grid_spec=pltpu.PrefetchScalarGridSpec(
            num_scalar_prefetch=1,
            grid=(1,),
            in_specs=[pl.BlockSpec(memory_space=pl.ANY)],
            out_specs=pl.BlockSpec((tokens, width), lambda i, ids: (0, 0)),
            scratch_shapes=[
                pltpu.VMEM((rows, width), BF),
                pltpu.VMEM((rows + 8, width), F32),
                pltpu.VMEM((tokens, width), F32),
                pltpu.SemaphoreType.DMA((parts,)),
            ],
        ),
        out_shape=jax.ShapeDtypeStruct((tokens, width), BF),
        compiler_params=params(),
        cost_estimate=cost(0, rows * width * 2),
        name="embed_rows",
    )(local_ids, table)


def head_lanes(rows, head):
    lane = lax.broadcasted_iota(jnp.int32, (rows, LANES), 1)
    return (lane // HEAD_DIM) == head


def near(block, count):
    reach = MAX_RUN // BLOCK
    return max(0, block - reach) * BLOCK, min(count, block + reach + 1) * BLOCK


def attention_masks(segment_ids):
    lane = lax.broadcasted_iota(jnp.int32, (1, LANES), 1)
    same = segment_ids[:, None] == lane
    fk = jnp.where(same, 1.0, 0.0).astype(BF)
    fq = jnp.where(jnp.logical_or(same, lane >= DOCS), 0.0, masked_score).astype(BF)
    return fq, fk


gelu_slope = 0.7978845608028654
gelu_cubic = 0.044715


MESH = pl.DeviceIdType.MESH


class Place:
    def __init__(self):
        self.dp = lax.axis_index("dp")
        self.side = lax.axis_index("mp")
        self.outers = lax.axis_size("dp") // 4
        self.outer = self.dp // 4
        self.mid = (self.dp // 2) % 2
        self.core = self.dp % 2

    def other_core(self):
        return (self.dp + 1 - 2 * self.core, self.side)

    def other_mid(self):
        return (self.dp + 2 - 4 * self.mid, self.side)

    def other_side(self):
        return (self.dp, 1 - self.side)

    def at_outer(self, outer):
        return (outer * 4 + self.mid * 2 + self.core, self.side)

    def turn(self, step):
        return lax.rem(self.outer + 1 + step, self.outers)


def greet(place, with_side):
    barrier = pltpu.get_barrier_semaphore()
    peers = [place.other_core(), place.other_mid()]
    if with_side:
        peers.append(place.other_side())
    for peer in peers:
        pl.semaphore_signal(barrier, inc=1, device_id=peer, device_id_type=MESH)
    for step in range(place.outers - 1):
        pl.semaphore_signal(
            barrier, inc=1, device_id=place.at_outer(place.turn(step)), device_id_type=MESH
        )
    pl.semaphore_wait(barrier, len(peers) + place.outers - 1)


def remote(src, dst, send, recv, device):
    return pltpu.make_async_remote_copy(
        src_ref=src, dst_ref=dst, send_sem=send, recv_sem=recv, device_id=device, device_id_type=MESH
    )


def add_into(dst, left, right):
    dst[...] = (left[...].astype(F32) + right[...].astype(F32)).astype(dst.dtype)


class Scatter:
    def __init__(self, place, sources, one, two, three, sems):
        self.place, self.sources = place, sources
        self.one, self.two, self.three = one, two, three
        self.sems = sems
        self.items = range(len(sources))

    def core_copy(self, step, item):
        p = self.place
        turn = p.turn(step)
        return remote(
            self.sources[item].at[turn, :, 1 - p.core],
            self.one[item].at[turn],
            self.sems[0].at[step, item],
            self.sems[1].at[step, item],
            p.other_core(),
        )

    def mid_copy(self, step, item):
        p = self.place
        turn = p.turn(step)
        return remote(
            self.one[item].at[turn, 1 - p.mid],
            self.two[item].at[turn],
            self.sems[2].at[step, item],
            self.sems[3].at[step, item],
            p.other_mid(),
        )

    def outer_copy(self, step, item):
        p = self.place
        turn = p.turn(step)
        return remote(
            self.two[item].at[turn],
            self.three[item].at[p.outer],
            self.sems[4].at[step, item],
            self.sems[5].at[p.outer, item],
            p.at_outer(turn),
        )

    def arrival(self, step, item):
        p = self.place
        turn = p.turn(step)
        return remote(
            self.two[item].at[turn],
            self.three[item].at[turn],
            self.sems[4].at[step, item],
            self.sems[5].at[turn, item],
            p.at_outer(turn),
        )

    def start_core(self, step):
        for item in self.items:
            self.core_copy(step, item).start()

    def core_to_mid(self, step):
        p = self.place
        turn = p.turn(step)
        for item in self.items:
            self.core_copy(step, item).wait_recv()
            one = self.one[item]
            for mid in range(2):
                add_into(one.at[turn, mid], one.at[turn, mid], self.sources[item].at[turn, mid, p.core])
            self.mid_copy(step, item).start()

    def mid_to_outer(self, step, last):
        p = self.place
        turn = p.turn(step)
        for item in self.items:
            self.mid_copy(step, item).wait_recv()
            two = self.two[item]
            add_into(two.at[turn], two.at[turn], self.one[item].at[turn, p.mid])
            if not last:
                self.outer_copy(step, item).start()

    def finish(self, outs):
        p = self.place
        for item in self.items:
            total = self.two[item][p.outer].astype(F32)
            for step in range(p.outers - 1):
                self.arrival(step, item).wait_recv()
                total = total + self.three[item][p.turn(step)].astype(F32)
            outs[item][...] = total

    def drain(self):
        def one(step, carry):
            for item in self.items:
                self.core_copy(step, item).wait_send()
                self.mid_copy(step, item).wait_send()
            return carry

        lax.fori_loop(0, self.place.outers, one, 0)
        for step in range(self.place.outers - 1):
            for item in self.items:
                self.outer_copy(step, item).wait_send()


def scatter_shapes(sources):
    one = [pltpu.VMEM((s.shape[0], 2) + s.shape[3:], s.dtype) for s in sources]
    two = [pltpu.VMEM((s.shape[0],) + s.shape[3:], s.dtype) for s in sources]
    three = [pltpu.VMEM((s.shape[0],) + s.shape[3:], s.dtype) for s in sources]
    sems = [pltpu.SemaphoreType.DMA((sources[0].shape[0], len(sources))) for _ in range(6)]
    return one + two + three + sems


class IdGather:
    def __init__(self, place, every, sems):
        self.place, self.every, self.sems = place, every, sems

    def copy(self, stage, step, theirs=0):
        p = self.place
        turn = lax.rem(p.outer + step, p.outers)
        if stage == 0:
            at = turn if theirs else p.outer
            part, peer, mark = self.every.at[at, p.mid, p.core], p.at_outer(turn), at
        elif stage == 1:
            mid = 1 - p.mid if theirs else p.mid
            part, peer, mark = self.every.at[turn, mid, p.core], p.other_mid(), step
        else:
            core = 1 - p.core if theirs else p.core
            part, peer, mark = self.every.at[turn, :, core], p.other_core(), step
        return remote(part, part, self.sems[2 * stage].at[step], self.sems[2 * stage + 1].at[mark], peer)


class Swap:
    def __init__(self, place, src, dst, send, recv):
        self.place, self.src, self.dst, self.send, self.recv = place, src, dst, send, recv

    def copy(self, at, src_rows, dst_rows):
        return remote(
            self.src.at[src_rows], self.dst.at[dst_rows], self.send.at[at], self.recv.at[at], self.place.other_side()
        )


def rows_from(start, size):
    return pl.ds(pl.multiple_of(start, size), size)


def feed_forward_kernel(
    ids, x_in, cot, wu_in, bu, wd_in, hidden, vectors, wo_in, mixed, q_in, k_in, v_in, lse, fq_ref, fk_ref, others,
    wo_other_in, every, layer, hg, norm_sums, wo_out, dwd_out, dwu_out, alone_out, dq_out, dk_out, dv_out,
    act, ug, xt, xg, rg, mgs, mgr, wu, wd, dbu, dbd, qs, ks, kt, gs, delta, scores, slopes,
    wo_sum, wo_recv, src_d, src_u, src_a, src_o, *rest,
):
    scatter_refs, rest = rest[:15], rest[15:]
    out_refs, rest = rest[:9], rest[9:]
    id_sems, (send_x, recv_x, send_h, recv_h, send_d, recv_d, send_l, recv_l, local) = rest[:6], rest[6:]
    tokens, width = x_in.shape
    features = wu.shape[1]
    columns = wo_in.shape[0]
    x = layer
    wo, wo_other = layer.at[:columns], layer.at[columns : 2 * columns]
    gain, bd = vectors[2:3, :], vectors[4:5, :]
    half = tokens // 2
    chunk, part, piece = 256, 512, 128
    place = Place()
    outers = place.outers
    work = Scatter(
        place, [src_d, src_u, src_a], scatter_refs[0:3], scatter_refs[3:6], scatter_refs[6:9], scatter_refs[9:]
    )
    after = Scatter(place, [src_o], out_refs[0:1], out_refs[1:2], out_refs[2:3], out_refs[3:])
    known = IdGather(place, every, id_sems)
    every[place.outer, place.mid, place.core] = ids[...]
    mine_at, other_at = place.side * half, (1 - place.side) * half
    grads = Swap(place, xg, rg, send_x, recv_x)
    mixes = Swap(place, mgs, mgr, send_h, recv_h)
    downs = Swap(place, xg, rg, send_d, recv_d)
    layers = Swap(place, layer, layer, send_l, recv_l)
    dbu[...] = jnp.zeros_like(dbu)
    dbd[...] = jnp.zeros_like(dbd)
    src_a[...] = jnp.zeros_like(src_a)
    norm_sums[...] = jnp.zeros_like(norm_sums)
    loads = [
        pltpu.make_async_copy(src, dst, local.at[at])
        for at, (src, dst) in enumerate(((x_in, x), (wu_in, wu), (wd_in, wd)))
    ]
    for copy in loads:
        copy.start()
    greet(place, True)
    for copy in loads:
        copy.wait()

    def loop(low, high, stage):
        lax.fori_loop(low, high, lambda step, carry: (stage(step), carry)[1], 0)

    def ids_mid(step):
        known.copy(0, step, 1).wait_recv()
        known.copy(1, step).start()

    def ids_core(step):
        known.copy(1, step, 1).wait_recv()
        known.copy(2, step).start()

    loop(1, outers, lambda step: known.copy(0, step).start())
    known.copy(1, 0).start()

    def forward(start):
        rows = rows_from(start, chunk)
        xc = x[rows, :]
        gc = cot[rows, :]
        xt[:, rows] = xc.T
        dbd[...] += jnp.sum(gc.astype(F32), axis=0, keepdims=True)
        total = jnp.zeros((chunk, width), F32)
        for at in range(features // part):
            cols = slice(at * part, (at + 1) * part)
            up = product(xc, wu[:, cols]) + bu[:, cols]
            square = up * up
            gate = 0.5 + 0.5 * jnp.tanh(up * (gelu_slope + (gelu_slope * gelu_cubic) * square))
            value = up * gate
            act[rows, cols] = value.astype(BF)
            slope = gate + value * (1.0 - gate) * (
                2.0 * gelu_slope + (6.0 * gelu_slope * gelu_cubic) * square
            )
            low = (times_back(gc, wd[cols, :]) * slope).astype(BF)
            ug[rows, cols] = low
            dbu[:, cols] += jnp.sum(low.astype(F32), axis=0, keepdims=True)
            total = total + times_back(low, wu[:, cols])
        xg[rows, :] = total.astype(BF)

    def sent(at):
        return grads.copy(at, rows_from(other_at + at * chunk, chunk), rows_from(at * chunk, chunk))

    def theirs(at):
        forward(other_at + at * chunk)
        sent(at).start()

    loop(0, half // chunk, theirs)
    loop(0, half // chunk, lambda at: forward(mine_at + at * chunk))
    heads_in = [
        pltpu.make_async_copy(src, wu.at[:, at * columns : (at + 1) * columns], local.at[at])
        for at, src in enumerate((q_in, k_in, v_in))
    ] + [
        pltpu.make_async_copy(src, dst, local.at[3 + at])
        for at, (src, dst) in enumerate(((wo_in, wo), (wo_other_in, wo_other)))
    ]
    for copy in heads_in:
        copy.start()
    loop(1, outers, ids_mid)
    dp_size = 4 * outers
    up_lanes, down_lanes = features // dp_size, width // dp_size
    for at in range(dp_size):
        spot = (at // 4, (at // 2) % 2, at % 2)
        src_a[spot + (slice(0, 1), slice(0, up_lanes))] = dbu[:, at * up_lanes : (at + 1) * up_lanes]
        src_a[spot + (slice(1, 2), slice(0, down_lanes))] = dbd[:, at * down_lanes : (at + 1) * down_lanes]

    down_rows, up_rows = features // outers // 2, width // outers

    def weight_grads(step):
        turn = place.turn(step)
        if down_rows % LANES:
            cols = rows_from(turn * (2 * down_rows), 2 * down_rows)
            src_d[turn] = contract_rows(act[:, cols], cot[...]).astype(BF).reshape(2, 2, down_rows // 2, width)
        else:
            for mid in range(2):
                cols = rows_from(turn * (2 * down_rows) + mid * down_rows, down_rows)
                src_d[turn, mid] = contract_rows(act[:, cols], cot[...]).astype(BF).reshape(2, down_rows // 2, width)
        rows = rows_from(turn * up_rows, up_rows)
        for at in range(features // part):
            cols = slice(at * part, (at + 1) * part)
            src_u[turn, :, :, :, cols] = (
                product(xt[rows, :], ug[:, cols]).astype(BF).reshape(2, 2, up_rows // 4, part)
            )
        work.start_core(step)

    def norm_grads(at):
        @pl.when(at % (chunk // piece) == 0)
        def _():
            sent(at // (chunk // piece)).wait_recv()

        here = rows_from(at * piece, piece)
        rows = rows_from(mine_at + at * piece, piece)
        grad = xg[rows, :].astype(F32) + rg[here, :].astype(F32)
        _, unit, inverse = normalize(hidden[here, :], 1.0, 0.0)
        back, gain_sum, bias_sum = norm_back(grad, unit, inverse, gain)
        norm_sums[0:1, :] += gain_sum[None, :]
        norm_sums[1:2, :] += bias_sum[None, :]
        total = cot[rows, :].astype(F32) + back
        hg[here, :] = total.astype(BF)

    def mix_copy(at):
        here = rows_from(at * chunk, chunk)
        return mixes.copy(at, here, here)

    def mixed_grads(at):
        here = rows_from(at * chunk, chunk)
        mgs[here, :] = times_back(hg[here, :], wo_other[...]).astype(BF)
        mix_copy(at).start()
        wu[rows_from(mine_at + at * chunk, chunk), 3 * columns :] = times_back(hg[here, :], wo[...]).astype(BF)

    weight_grads(0)
    weight_grads(1)
    work.core_to_mid(0)
    loop(0, half // piece, norm_grads)
    for copy in heads_in:
        copy.wait()
    loop(0, half // chunk, mixed_grads)
    rows_o = columns // dp_size
    turned = (mixed[rows_from(mine_at, half), :].T, others[...].T)
    for which in range(2):
        for at in range(0, width, BLOCK):
            src_o[:, :, :, which * rows_o : (which + 1) * rows_o, at : at + BLOCK] = (
                product(turned[which], hg[:, at : at + BLOCK]).astype(BF).reshape(outers, 2, 2, rows_o, BLOCK)
            )
    loop(0, outers, after.start_core)

    def more(step):
        weight_grads(step)
        work.core_to_mid(step - 1)

    loop(2, outers, more)
    loop(0, outers, after.core_to_mid)
    work.core_to_mid(outers - 1)
    loop(0, outers - 3, lambda step: work.mid_to_outer(step, False))
    loop(0, half // chunk, lambda at: sent(at).wait_send())

    def downward(start):
        rows = rows_from(start, chunk)
        xg[rows, :] = product(act[rows, :], wd[...]).astype(BF)

    def down_sent(at):
        return downs.copy(at, rows_from(other_at + at * piece, piece), rows_from(at * piece, piece))

    def down_theirs(at):
        downward(other_at + at * chunk)
        mix_copy(at).wait_recv()

    loop(0, half // chunk, down_theirs)
    loop(0, half // piece, lambda at: down_sent(at).start())
    wu[rows_from(other_at, half), 3 * columns :] = mgr[...]
    loop(0, half // chunk, lambda at: downward(mine_at + at * chunk))
    work.mid_to_outer(outers - 3, False)
    loop(0, outers, ids_core)

    def layer_copy(at, start):
        rows = rows_from(start + at * piece, piece)
        return layers.copy(at, rows, rows)

    def layer_rows(at):
        down_sent(at).wait_recv()
        here = rows_from(at * piece, piece)
        rows = rows_from(mine_at + at * piece, piece)
        layer[rows, :] = (
            hidden[here, :] + (xg[rows, :].astype(F32) + rg[here, :].astype(F32)) + bd
        ).astype(BF)
        layer_copy(at, mine_at).start()

    blocks = tokens // BLOCK
    scale = HEAD_DIM**-0.5

    def one_pair(at):
        def lanes_of(which):
            return pl.ds(pl.multiple_of(which * columns + at * LANES, LANES), LANES)

        keys, grad = wu[:, lanes_of(1)], wu[:, lanes_of(3)]
        scaled = (wu[:, lanes_of(0)].astype(F32) * scale).astype(BF)
        for head in range(2):
            mine = head_lanes(tokens, head)
            qs[head, :, :LANES] = jnp.where(mine, scaled, jnp.zeros_like(scaled))
            qs[head, :, LANES:] = fq_ref[...]
            gs[head] = jnp.where(mine, grad, jnp.zeros_like(grad))
        ks[:, :LANES] = keys
        ks[:, LANES:] = fk_ref[...]
        kt[...] = keys.T
        both = (grad.astype(F32) * mixed[:, lanes_of(0)].astype(F32)).T
        for head in range(2):
            delta[head : head + 1, :] = jnp.sum(
                both[head * HEAD_DIM : (head + 1) * HEAD_DIM], axis=0, keepdims=True
            )
        for block in range(blocks):
            here = slice(block * BLOCK, (block + 1) * BLOCK)
            low, high = near(block, blocks)
            dq = []
            for head in range(2):
                scores[head, low:high, :] = times_back(ks[low:high, :], qs[head, here, :])
                slopes[head, low:high, :] = times_back(wu[low:high, lanes_of(2)], gs[head, here, :])
            for head in range(2):
                offset, shift = lse[at, head : head + 1, here], delta[head : head + 1, here]
                columns_here = slice(head * tokens + block * BLOCK, head * tokens + (block + 1) * BLOCK)
                for at_key in range(low, high, STRIP):
                    strip = slice(at_key, at_key + STRIP)
                    prob = jnp.exp(scores[head, strip, :] - offset)
                    act[strip, columns_here] = prob.astype(BF)
                    ug[strip, columns_here] = (prob * (slopes[head, strip, :] - shift)).astype(BF)
                dq.append(product(kt[head * HEAD_DIM : (head + 1) * HEAD_DIM, low:high], ug[low:high, columns_here]))
            wd[here, lanes_of(0)] = (jnp.concatenate(dq, axis=0).T * scale).astype(BF)
        for block in range(blocks):
            here = slice(block * BLOCK, (block + 1) * BLOCK)
            low, high = near(block, blocks)
            dk = jnp.zeros((BLOCK, LANES), F32)
            dv = jnp.zeros((BLOCK, LANES), F32)
            for head in range(2):
                dv = dv + product(act[here, head * tokens + low : head * tokens + high], gs[head, low:high, :])
                dk = dk + product(ug[here, head * tokens + low : head * tokens + high], qs[head, low:high, :LANES])
            wd[here, lanes_of(1)] = dk.astype(BF)
            wd[tokens + block * BLOCK : tokens + (block + 1) * BLOCK, lanes_of(0)] = dv.astype(BF)

        @pl.when(at == 1)
        def _():
            work.mid_to_outer(outers - 2, False)
            loop(0, half // piece, layer_rows)

        @pl.when(at == 3)
        def _():
            loop(0, outers - 1, lambda step: after.mid_to_outer(step, False))
            after.mid_to_outer(outers - 1, True)
            work.mid_to_outer(outers - 1, True)

    loop(0, columns // LANES, one_pair)
    grads_out = [
        pltpu.make_async_copy(src, dst, local.at[at])
        for at, (src, dst) in enumerate(
            (
                (wd.at[:tokens, :columns], dq_out),
                (wd.at[:tokens, columns : 2 * columns], dk_out),
                (wd.at[tokens : 2 * tokens, :columns], dv_out),
            )
        )
    ]
    for copy in grads_out:
        copy.start()
    after.finish([wo_sum])
    wo_swap = remote(
        wo_sum.at[pl.ds(rows_o, rows_o)], wo_recv, send_h.at[half // chunk], recv_h.at[half // chunk], place.other_side()
    )
    wo_swap.start()
    work.finish([dwd_out, dwu_out, alone_out])
    for copy in grads_out:
        copy.wait()
    wo_swap.wait()
    wo_out[...] = wo_sum[:rows_o, :] + wo_recv[...]
    work.drain()
    after.drain()
    loop(0, outers, lambda step: known.copy(2, step, 1).wait_recv())
    loop(1, outers, lambda step: known.copy(0, step).wait_send())
    loop(0, outers, lambda step: known.copy(1, step).wait_send())
    loop(0, outers, lambda step: known.copy(2, step).wait_send())

    def swaps_done(at):
        rows = rows_from(mine_at + at * piece, piece)
        down_sent(at).wait_send()
        layer_copy(at, other_at).wait_recv()
        layer_copy(at, mine_at).wait_send()

    loop(0, half // piece, swaps_done)
    loop(0, half // chunk, lambda at: mix_copy(at).wait_send())


def feed_forward(dp_size, collective_id, *operands):
    ids, x, _, wu, _, wd, _, _, wo, _, queries, *_ = operands
    tokens, width = x.shape
    columns = wo.shape[0]
    features = wu.shape[1]
    half = tokens // 2
    outers = dp_size // 4
    shape = jax.ShapeDtypeStruct
    items = [
        shape((outers, 2, 2, features // dp_size, width), BF),
        shape((outers, 2, 2, width // dp_size, features), BF),
        shape((outers, 2, 2, 8, LANES), F32),
    ]
    item_o = shape((outers, 2, 2, 2 * columns // dp_size, width), BF)
    anywhere = pl.BlockSpec(memory_space=pl.ANY)
    return pl.pallas_call(
        feed_forward_kernel,
        in_specs=[anywhere if at in (1, 3, 5, 8, 10, 11, 12, 17) else full_spec() for at in range(len(operands))],
        out_specs=[full_spec()] * 8 + [anywhere] * 3,
        out_shape=[
            shape((outers, 2, 2) + ids.shape, ids.dtype),
            shape((tokens, width), BF),
            shape((half, width), BF),
            shape((2, width), F32),
            shape((wo.shape[0] // dp_size, width), F32),
        ]
        + [shape(item.shape[3:], F32) for item in items]
        + [shape(queries.shape, BF)] * 3,
        scratch_shapes=[
            pltpu.VMEM((tokens, features), BF),
            pltpu.VMEM((tokens, features), BF),
            pltpu.VMEM((width, tokens), BF),
            pltpu.VMEM((tokens, width), BF),
            pltpu.VMEM((half, width), BF),
            pltpu.VMEM((half, columns), BF),
            pltpu.VMEM((half, columns), BF),
            pltpu.VMEM(wu.shape, BF),
            pltpu.VMEM(wd.shape, BF),
            pltpu.VMEM((1, features), F32),
            pltpu.VMEM((1, width), F32),
            pltpu.VMEM((2, tokens, 2 * LANES), BF),
            pltpu.VMEM((tokens, 2 * LANES), BF),
            pltpu.VMEM((LANES, tokens), BF),
            pltpu.VMEM((2, tokens, LANES), BF),
            pltpu.VMEM((2, tokens), F32),
            pltpu.VMEM((2, tokens, BLOCK), F32),
            pltpu.VMEM((2, tokens, BLOCK), F32),
            pltpu.VMEM(item_o.shape[3:], F32),
            pltpu.VMEM((columns // dp_size, width), F32),
        ]
        + [pltpu.VMEM(item.shape, item.dtype) for item in items + [item_o]]
        + scatter_shapes(items)
        + scatter_shapes([item_o])
        + [pltpu.SemaphoreType.DMA((outers,)) for _ in range(6)]
        + [pltpu.SemaphoreType.DMA((half // 256,)) for _ in range(2)]
        + [pltpu.SemaphoreType.DMA((half // 128,)) for _ in range(6)]
        + [pltpu.SemaphoreType.DMA((5,))],
        compiler_params=pltpu.CompilerParams(
            vmem_limit_bytes=60 * 1024 * 1024, collective_id=collective_id, has_side_effects=True
        ),
        name="feed_forward",
    )(*operands)


def front_kernel(
    rows_ref, noise, scales, w_in, vectors, wq, wk, wv, fq_ref, fk_ref, wo,
    q_out, k_out, v_out, n1t_out, stream_out, others_out, wo_out, inputs_out, mixed, lse, hidden_out, x2,
    q, k, v, n1t, stream_own, stream, theirs, wo_other, others, qs, ks, vt, scores, probs, inputs,
    send_r, recv_r, send_m, recv_m, local,
):
    tokens, width = stream.shape
    half = tokens // 2
    chunk = 256
    pairs = q.shape[1] // LANES
    place = Place()
    mine_at = place.side * half
    barrier = pltpu.get_barrier_semaphore()
    for peer in (place.other_side(), place.other_core()):
        pl.semaphore_signal(barrier, inc=1, device_id=peer, device_id_type=MESH)
    pl.semaphore_wait(barrier, 2)

    def loop(low, high, stage):
        lax.fori_loop(low, high, lambda step, carry: (stage(step), carry)[1], 0)

    def row_copy(at):
        span = rows_from(at * chunk, chunk)
        return remote(rows_ref.at[span], theirs.at[span], send_r.at[at], recv_r.at[at], place.other_side())

    count = tokens // chunk
    part = wo.shape[0] // 2

    def weights(step):
        rows = rows_from(place.core * part, part)
        src = wo_other if step else wo
        peer = place.other_core() if step else place.other_side()
        return remote(src.at[rows], wo_other.at[rows], send_r.at[count + step], recv_r.at[count + step], peer)

    loop(0, count, lambda at: row_copy(at).start())
    weights(0).start()

    def start_of(at):
        row_copy(at).wait_recv()
        span = rows_from(at * chunk, chunk)
        embedded = rows_ref[span, :].astype(F32) + theirs[span, :].astype(F32)
        low = (scales[0:1, 0:1] * (embedded + scales[1:2, 0:1] * noise[span, :].astype(F32))).astype(BF)
        inputs[span, :] = low
        flow = product(low, w_in[...])
        stream[span, :] = flow
        normed, _, _ = normalize(flow, vectors[0:1, :], vectors[1:2, :])
        normed = normed.astype(BF)
        n1t[:, span] = normed.T
        q[span, :] = product(normed, wq[...]).astype(BF)
        k[span, :] = product(normed, wk[...]).astype(BF)
        v[span, :] = product(normed, wv[...]).astype(BF)

    loop(0, count, start_of)

    def keep(at):
        span = rows_from(at * chunk, chunk)
        stream_own[span, :] = stream[rows_from(mine_at + at * chunk, chunk), :]

    loop(0, half // chunk, keep)
    kept = [
        pltpu.make_async_copy(src, dst, local.at[at])
        for at, (src, dst) in enumerate(
            ((q, q_out), (k, k_out), (v, v_out), (n1t, n1t_out), (stream_own, stream_out))
        )
    ]
    for copy in kept:
        copy.start()

    blocks = tokens // BLOCK
    scale = HEAD_DIM**-0.5

    def pair_copy(at):
        lanes = pl.ds(pl.multiple_of(at * LANES, LANES), LANES)
        return remote(mixed.at[:, lanes], others.at[:, lanes], send_m.at[at], recv_m.at[at], place.other_side())

    def one_pair(at):
        lanes = pl.ds(pl.multiple_of(at * LANES, LANES), LANES)
        scaled = (q[:, lanes].astype(F32) * scale).astype(BF)
        for head in range(2):
            qs[head, :, :LANES] = jnp.where(head_lanes(tokens, head), scaled, jnp.zeros_like(scaled))
            qs[head, :, LANES:] = fq_ref[...]
        ks[:, :LANES] = k[:, lanes]
        ks[:, LANES:] = fk_ref[...]
        vt[...] = v[:, lanes].T
        for block in range(blocks):
            here = slice(block * BLOCK, (block + 1) * BLOCK)
            low, high = near(block, blocks)
            found = []
            for head in range(2):
                scores[head, low:high, :] = times_back(ks[low:high, :], qs[head, here, :])
            for head in range(2):
                peak = jnp.full((8, BLOCK), masked_score, F32)
                for at_key in range(low, high, STRIP):
                    strip = scores[head, at_key : at_key + STRIP, :].reshape(STRIP // 8, 8, BLOCK)
                    peak = jnp.maximum(peak, jnp.max(strip, axis=0))
                peak = jnp.max(peak, axis=0, keepdims=True)
                total = jnp.zeros((8, BLOCK), F32)
                for at_key in range(low, high, STRIP):
                    strip = jnp.exp(scores[head, at_key : at_key + STRIP, :] - peak)
                    total = total + jnp.sum(strip.reshape(STRIP // 8, 8, BLOCK), axis=0)
                    probs[head, at_key : at_key + STRIP, :] = strip.astype(BF)
                total = jnp.sum(total, axis=0, keepdims=True)
                values = vt[head * HEAD_DIM : (head + 1) * HEAD_DIM, low:high]
                found.append(product(values, probs[head, low:high, :]) / total)
                lse[at, head : head + 1, here] = peak + jnp.log(total)
            mixed[here, lanes] = jnp.concatenate(found, axis=0).T.astype(BF)
        pair_copy(at).start()

        @pl.when(at == 1)
        def _():
            weights(0).wait_recv()
            weights(1).start()

    loop(0, pairs, one_pair)

    def ours(at):
        span = rows_from(at * chunk, chunk)
        stream[span, :] += product(mixed[span, :], wo[...])

    loop(0, count, ours)
    weights(1).wait_recv()
    loop(0, pairs, lambda at: pair_copy(at).wait_recv())
    kept += [
        pltpu.make_async_copy(src, dst, local.at[5 + at])
        for at, (src, dst) in enumerate(((others.at[rows_from(mine_at, half)], others_out), (wo_other, wo_out)))
    ]
    for copy in kept[5:]:
        copy.start()

    def finish(at):
        span = rows_from(at * chunk, chunk)
        hidden = stream[span, :] + product(others[span, :], wo_other[...])
        stream[span, :] = hidden
        normed, _, _ = normalize(hidden, vectors[2:3, :], vectors[3:4, :])
        x2[span, :] = normed.astype(BF)

    loop(0, count, finish)
    hidden_out[...] = stream[rows_from(mine_at, half), :]
    inputs_out[...] = inputs[rows_from(mine_at, half), :]
    loop(0, count, lambda at: row_copy(at).wait_send())
    weights(0).wait_send()
    weights(1).wait_send()
    loop(0, pairs, lambda at: pair_copy(at).wait_send())
    for copy in kept:
        copy.wait()


def front(rows, noise, scales, w_in, vectors, wq, wk, wv, fq, fk, wo, collective_id):
    tokens, embed = rows.shape
    width, columns = wq.shape
    half = tokens // 2
    pairs = columns // LANES
    count = tokens // 256
    shape = jax.ShapeDtypeStruct
    head = shape((tokens, columns), BF)
    scratch = pltpu.VMEM
    return pl.pallas_call(
        front_kernel,
        in_specs=[full_spec()] * 11,
        out_specs=[pl.BlockSpec(memory_space=pl.ANY)] * 7 + [full_spec()] * 5,
        out_shape=[
            head,
            head,
            head,
            shape((width, tokens), BF),
            shape((half, width), F32),
            shape((half, columns), BF),
            shape(wo.shape, BF),
            shape((half, embed), BF),
            head,
            shape((pairs, 2, tokens), F32),
            shape((half, width), F32),
            shape((tokens, width), BF),
        ],
        scratch_shapes=[
            scratch(head.shape, BF),
            scratch(head.shape, BF),
            scratch(head.shape, BF),
            scratch((width, tokens), BF),
            scratch((half, width), F32),
            scratch((tokens, width), F32),
            scratch(rows.shape, BF),
            scratch(wo.shape, BF),
            scratch(head.shape, BF),
            scratch((2, tokens, 2 * LANES), BF),
            scratch((tokens, 2 * LANES), BF),
            scratch((LANES, tokens), BF),
            scratch((2, tokens, BLOCK), F32),
            scratch((2, tokens, BLOCK), BF),
            scratch(rows.shape, BF),
        ]
        + [pltpu.SemaphoreType.DMA((count + 2,)) for _ in range(2)]
        + [pltpu.SemaphoreType.DMA((pairs,)) for _ in range(2)]
        + [pltpu.SemaphoreType.DMA((7,))],
        compiler_params=pltpu.CompilerParams(
            vmem_limit_bytes=VMEM_LIMIT, collective_id=collective_id, has_side_effects=True
        ),
        name="front",
    )(rows, noise, scales, w_in, vectors, wq, wk, wv, fq, fk, wo)


class Gather:
    def __init__(self, place, every, sems):
        self.place, self.every, self.sems = place, every, sems

    def turn(self, step):
        return lax.rem(self.place.outer + step, self.place.outers)

    def copy(self, stage, piece, step, theirs=0):
        p = self.place
        turn = self.turn(step)
        mark = step
        if stage == 0:
            at = turn if theirs else p.outer
            part = self.every.at[at, p.mid, p.core, p.side, piece]
            peer, mark = p.at_outer(turn), at
        elif stage == 3:
            core = 1 - p.core if theirs else p.core
            part, peer = self.every.at[turn, :, core, :, piece], p.other_core()
        elif (stage == 1) == (piece % 2 == 0):
            side = 1 - p.side if theirs else p.side
            mid = slice(None) if piece % 2 else p.mid
            part, peer = self.every.at[turn, mid, p.core, side, piece], p.other_side()
        else:
            mid = 1 - p.mid if theirs else p.mid
            side = p.side if piece % 2 else slice(None)
            part, peer = self.every.at[turn, mid, p.core, side, piece], p.other_mid()
        sems = self.sems[2 * stage : 2 * stage + 2]
        return remote(part, part, sems[0].at[piece, step], sems[1].at[piece, mark], peer)


def tail_kernel(
    vocab_part,
    large,
    dq, dk, dv, n1t_in, wq, wk, wv, stream_in, hgrad_in, vectors, w_in, inputs, scales, ids, mine, sums_two,
    qkv_out, w_in_out, sides_out, noise, table,
    every, n1t, stream, hgrad, part, rpart, nsend, nrecv, stage_in, stage_out, picked, total, sums,
    src_q, src_w, src_s, side_w, side_s, *rest,
):
    early_refs, rest = rest[:9], rest[9:]
    late_refs, rest = rest[:12], rest[12:]
    gather_sems, rest = rest[:8], rest[8:]
    send_x, recv_x, send_n, recv_n, send_s, recv_s, local = rest
    width, tokens = n1t.shape
    columns = wq.shape[1]
    half = tokens // 2
    chunk, piece = 256, half // 4
    place = Place()
    outers = place.outers
    early = Scatter(place, [src_q], early_refs[0:1], early_refs[1:2], early_refs[2:3], early_refs[3:])
    late = Scatter(place, [src_w, src_s], late_refs[0:2], late_refs[2:4], late_refs[4:6], late_refs[6:])
    gather = Gather(place, every, gather_sems)
    mine_at, other_at = place.side * half, (1 - place.side) * half
    grads = Swap(place, part, rpart, send_x, recv_x)
    noises = Swap(place, nsend, nrecv, send_n, recv_n)
    loads = [
        pltpu.make_async_copy(src, dst, local.at[at])
        for at, (src, dst) in enumerate(((n1t_in, n1t), (stream_in, stream), (hgrad_in, hgrad)))
    ]
    for copy in loads:
        copy.start()
    sums[...] = jnp.zeros_like(sums)
    src_s[...] = jnp.zeros_like(src_s)
    total[...] = jnp.zeros_like(total)
    sums[2:4, :] = sums_two[...]
    greet(place, True)

    def loop(low, high, stage):
        lax.fori_loop(low, high, lambda step, carry: (stage(step), carry)[1], 0)

    def back_product(start):
        rows = rows_from(start, chunk)
        part[rows, :] = (
            times_back(dq[rows, :], wq[...])
            + times_back(dk[rows, :], wk[...])
            + times_back(dv[rows, :], wv[...])
        ).astype(BF)

    def sent(at):
        return grads.copy(at, rows_from(other_at + at * piece, piece), rows_from(at * piece, piece))

    def theirs(at):
        back_product(other_at + at * chunk)
        for step in range(chunk // piece):
            sent(at * (chunk // piece) + step).start()

    loop(0, half // chunk, theirs)
    for copy in loads:
        copy.wait()
    group = width // outers

    def weight_grads(step):
        turn = place.turn(step)
        rows = rows_from(turn * group, group)
        for at, grad in enumerate((dq, dk, dv)):
            src_q[turn, :, :, :, at * columns : (at + 1) * columns] = (
                product(n1t[rows, :], grad[...]).astype(BF).reshape(2, 2, group // 4, columns)
            )
        early.start_core(step)

    weight_grads(0)

    def more(step):
        weight_grads(step)
        early.core_to_mid(step - 1)

    loop(1, outers, more)
    loop(0, half // chunk, lambda at: back_product(mine_at + at * chunk))
    early.core_to_mid(outers - 1)

    def noise_copy(which):
        rows = pl.ds(which * piece, piece)
        return noises.copy(which, rows, rows)

    def norm_grads(which):
        sent(which).wait_recv()
        here = slice(which * piece, (which + 1) * piece)
        rows = rows_from(mine_at + which * piece, piece)
        grad = part[rows, :].astype(F32) + rpart[here, :].astype(F32)
        _, unit, inverse = normalize(stream[here, :], 1.0, 0.0)
        back, gain_sum, bias_sum = norm_back(grad, unit, inverse, vectors[0:1, :])
        low = (hgrad[here, :].astype(F32) + back).astype(BF)
        back_in = times_back(low, w_in[...])
        spot = every.at[place.outer, place.mid, place.core, place.side, which]
        found = (scales[0:1, 0:1] * back_in).astype(BF)
        if large:
            stage_out[...] = found
            moved = pltpu.make_async_copy(stage_out, spot, local.at[0])
            moved.start()
            moved.wait()
        else:
            spot[...] = found
        loop(1, outers, lambda step: gather.copy(0, which, step).start())
        gather.copy(1, which, 0).start()
        sums[0:1, :] += gain_sum[None, :]
        sums[1:2, :] += bias_sum[None, :]
        rpart[here, :] = low
        noised = (scales[0:1, 0:1] * scales[1:2, 0:1]) * back_in
        noise[rows, :] = noised
        nsend[here, :] = noised.astype(BF)

    dp_size = 4 * outers

    def start_late():
        for which in range(4):
            noise_copy(which).start()
        rows_w = w_in.shape[0] // dp_size
        lanes = width // dp_size
        work = contract_rows(inputs[...], rpart[...])
        for at in range(dp_size):
            spot = (at // 4, (at // 2) % 2, at % 2)
            src_w[spot] = work[at * rows_w : (at + 1) * rows_w, :].astype(src_w.dtype)
            src_s[spot + (slice(None), slice(0, lanes))] = sums[:, at * lanes : (at + 1) * lanes]
        loop(0, outers, late.start_core)

    def forward(stage, which, step):
        gather.copy(stage - 1, which, step, 1).wait_recv()
        gather.copy(stage, which, step).start()

    owned = table.shape[0]
    wanted = lax.broadcasted_iota(jnp.int32, (total.shape[0], 1), 0)
    first = place.side * vocab_part + place.dp * owned

    def collect(pair, step):
        turn = gather.turn(step)
        for which in (2 * pair, 2 * pair + 1):
            gather.copy(3, which, step, 1).wait_recv()
        pieces = every.at[turn, :, :, :, 2 * pair : 2 * pair + 2]
        if large:
            moved = pltpu.make_async_copy(pieces, stage_in, local.at[0])
            moved.start()
            moved.wait()
            pieces = stage_in
        for spot in range(8):
            mid, core, side = spot // 4, (spot // 2) % 2, spot % 2
            for at in range(2):
                line = 4 * side + 2 * pair + at
                lanes = slice((2 * spot + at) * LANES, (2 * spot + at + 1) * LANES)
                picked[:, lanes] = ((ids[turn, mid, core, line : line + 1, :] - first) == wanted).astype(BF)
        total[...] += product(picked[...], pieces[...].reshape(16 * piece, -1))

    sided = []
    for slot in range(8):
        if slot < 4:
            norm_grads(slot)
            if slot == 3:
                start_late()
        if 1 <= slot < 5:
            loop(1, outers, lambda step: forward(1, slot - 1, step))
            forward(2, slot - 1, 0)
        if 2 <= slot < 6:
            loop(1, outers, lambda step: forward(2, slot - 2, step))
            forward(3, slot - 2, 0)
        if 3 <= slot < 7:
            loop(1, outers, lambda step: forward(3, slot - 3, step))
        if slot == 4:
            loop(0, outers - 1, lambda step: early.mid_to_outer(step, False))
            early.mid_to_outer(outers - 1, True)
            loop(0, outers, late.core_to_mid)
        if slot == 5:
            loop(0, outers, lambda step: collect(0, step))
            loop(0, outers - 1, lambda step: late.mid_to_outer(step, False))
            late.mid_to_outer(outers - 1, True)
        if slot == 6:
            early.finish([qkv_out])
            late.finish([w_in_out, sides_out])
            for at, (out, buffer) in enumerate(((w_in_out, side_w), (sides_out, side_s))):
                buffer[0] = out[...]
                sided.append(remote(buffer.at[0], buffer.at[1], send_s.at[at], recv_s.at[at], place.other_side()))
                sided[at].start()
        if slot == 7:
            loop(0, outers, lambda step: collect(1, step))
    for which in range(4):
        noise_copy(which).wait()
    noise[rows_from(other_at, half), :] = nrecv[...].astype(F32)
    mine_rows = mine[...].astype(F32)
    scale = row_scale(mine_rows)
    grad = total[...][:owned]
    table[...] = scale * grad - mine_rows * (scale * scale * scale) * jnp.mean(
        grad * mine_rows, axis=1, keepdims=True
    )
    for at, (out, buffer) in enumerate(((w_in_out, side_w), (sides_out, side_s))):
        sided[at].wait()
        out[...] = out[...] + buffer[1]
    early.drain()
    late.drain()
    loop(0, half // piece, lambda at: sent(at).wait_send())

    def done(step):
        for which in range(4):
            for stage in range(1, 4):
                gather.copy(stage, which, step).wait_send()

    loop(0, outers, done)

    def done_outer(step):
        for which in range(4):
            gather.copy(0, which, step).wait_send()

    loop(1, outers, done_outer)


def tail(vocab_part, dp_size, collective_id, *operands):
    (_, _, _, n1t, wq, _, _, stream, _, _, w_in, _, _, _, mine, _) = operands
    width, tokens = n1t.shape
    columns = wq.shape[1]
    half = tokens // 2
    piece = half // 4
    outers = dp_size // 4
    embed = w_in.shape[0]
    owned = mine.shape[0]
    padded = -(-owned // LANES) * LANES
    large = outers > 4
    every_shape = (outers, 2, 2, 2, 4, piece, embed)
    anywhere = pl.BlockSpec(memory_space=pl.ANY)

    def blocks_of(rows, cols, dtype):
        return jax.ShapeDtypeStruct((outers, 2, 2, rows, cols), dtype)

    src_q = blocks_of(width // dp_size, 3 * columns, BF)
    src_w = blocks_of(embed // dp_size, width, F32 if embed // dp_size % 16 else BF)
    src_s = blocks_of(8, LANES, F32)

    def owned_shape(value):
        return jax.ShapeDtypeStruct(value.shape[3:], F32)

    def scratch(shape, dtype):
        return pltpu.VMEM(shape, dtype)

    return pl.pallas_call(
        functools.partial(tail_kernel, vocab_part, large),
        in_specs=[anywhere if at in (3, 7, 8) else full_spec() for at in range(len(operands))],
        out_specs=[full_spec()] * 5 + ([anywhere] if large else []),
        out_shape=[
            owned_shape(src_q),
            owned_shape(src_w),
            owned_shape(src_s),
            jax.ShapeDtypeStruct((tokens, embed), F32),
            jax.ShapeDtypeStruct((owned, embed), F32),
        ]
        + ([jax.ShapeDtypeStruct(every_shape, BF)] if large else []),
        scratch_shapes=([] if large else [scratch(every_shape, BF)])
        + [
            scratch(n1t.shape, BF),
            scratch(stream.shape, F32),
            scratch(stream.shape, BF),
            scratch((tokens, width), BF),
            scratch((half, width), BF),
            scratch((half, embed), BF),
            scratch((half, embed), BF),
            scratch((2, 2, 2, 2, piece, embed) if large else (16, LANES), BF),
            scratch((piece, embed) if large else (16, LANES), BF),
            scratch((padded, 16 * piece), BF),
            scratch((padded, embed), F32),
            scratch((8, width), F32),
            scratch(src_q.shape, BF),
            scratch(src_w.shape, src_w.dtype),
            scratch(src_s.shape, F32),
            scratch((2,) + src_w.shape[3:], F32),
            scratch((2,) + src_s.shape[3:], F32),
        ]
        + scatter_shapes([src_q])
        + scatter_shapes([src_w, src_s])
        + [pltpu.SemaphoreType.DMA((4, outers)) for _ in range(8)]
        + [pltpu.SemaphoreType.DMA((4,)) for _ in range(4)]
        + [pltpu.SemaphoreType.DMA((2,)) for _ in range(2)]
        + [pltpu.SemaphoreType.DMA((3,))],
        compiler_params=pltpu.CompilerParams(
            vmem_limit_bytes=VMEM_LIMIT, collective_id=collective_id, has_side_effects=True
        ),
        name="tail",
    )(*operands)


def results_kernel(columns, layer, noise, table, w_in, qkv, wo, wu, wd, sides, alone, *refs):
    outs, sems = refs[:16], refs[16]
    sources = (
        layer, noise, table, w_in, qkv.at[:, :columns], qkv.at[:, columns : 2 * columns], qkv.at[:, 2 * columns :], wo, wu, wd,
    )
    copies = [pltpu.make_async_copy(src, dst, sems.at[at]) for at, (src, dst) in enumerate(zip(sources, outs[:10]))]
    for copy in copies:
        copy.start()
    for at in range(4):
        outs[10 + at][...] = sides[at, : outs[10 + at].shape[0]]
    for at in range(2):
        outs[14 + at][...] = alone[at, : outs[14 + at].shape[0]]
    for copy in copies:
        copy.wait()


def results(layer, noise, table, w_in, qkv, wo, wu, wd, sides, alone, small, bias_up_size):
    columns = qkv.shape[1] // 3
    shape = jax.ShapeDtypeStruct
    head = shape((qkv.shape[0], columns), F32)
    large = [layer, noise, table, w_in, head, head, head, wo, wu, wd]
    anywhere = pl.BlockSpec(memory_space=pl.ANY)
    return pl.pallas_call(
        functools.partial(results_kernel, columns),
        in_specs=[full_spec()] * 10,
        out_specs=[anywhere] * 10 + [full_spec()] * 6,
        out_shape=[shape(value.shape, value.dtype) for value in large]
        + [shape((small,), F32)] * 4
        + [shape((bias_up_size,), F32), shape((small,), F32)],
        scratch_shapes=[pltpu.SemaphoreType.DMA((10,))],
        name="results",
    )(layer, noise, table, w_in, qkv, wo, wu, wd, sides, alone)


def on_device(
    token_ids,
    segment_ids,
    time_index,
    noise_vec,
    embed_table,
    w_in,
    norm1_gain,
    norm1_bias,
    w_query,
    w_key,
    w_value,
    w_out,
    norm2_gain,
    norm2_bias,
    w_up,
    bias_up,
    w_down,
    bias_down,
    cotangent,
):
    seq_count, length = segment_ids.shape
    tokens = seq_count * length
    half = tokens // 2
    vocab_part = embed_table.shape[0]
    dp_size = lax.axis_size("dp")
    dp_index = lax.axis_index("dp")
    side = lax.axis_index("mp")
    fq, fk = lax.optimization_barrier(attention_masks(segment_ids[0]))
    level_step = jnp.log(time_high / time_low) / (TLEVELS - 1)
    level = time_low * jnp.exp(time_index.astype(F32) * level_step)
    scales = jnp.stack([lax.rsqrt(1.0 + level * level), level])
    rows = gather_rows(token_ids - side * vocab_part, embed_table)
    rows, *small_vectors = lax.optimization_barrier(
        (rows, norm1_gain, norm1_bias, norm2_gain, norm2_bias, bias_down)
    )
    vectors = jnp.stack(small_vectors).astype(F32)
    (
        queries, key_rows, value_rows, normed_one_t, stream_half, mixed_other, w_out_other, inputs_half, mixed_low, log_total, hidden_half, normed_two,
    ) = front(
        rows, noise_vec, scales, w_in, vectors, w_query, w_key, w_value, fq, fk, w_out, 3,
    )
    (
        every_id, layer_out, hidden_grad, norm_two_sums, w_out_grad, w_down_grad, w_up_grad, alone_grad,
        query_grad, key_grad, value_grad,
    ) = feed_forward(
        dp_size, 1, token_ids.reshape(-1, LANES), normed_two, cotangent, w_up, bias_up.astype(F32)[None, :], w_down,
        hidden_half, vectors, w_out, mixed_low, queries, key_rows, value_rows, log_total, fq, fk, mixed_other, w_out_other,
    )
    owned = vocab_part // dp_size
    mine = lax.dynamic_slice_in_dim(embed_table, dp_index * owned, owned, 0)
    qkv_grad, w_in_grad, sides_grad, noise_grad, table_grad, *_ = tail(
        vocab_part, dp_size, 2, query_grad, key_grad, value_grad, normed_one_t, w_query, w_key, w_value,
        stream_half, hidden_grad, vectors, w_in, inputs_half, scales, every_id, mine,
        norm_two_sums,
    )
    width = bias_down.shape[0] // dp_size
    (
        layer, noise, table, w_in_sum, query_sum, key_sum, value_sum, w_out_sum, w_up_sum, w_down_sum,
        gain_one_sum, bias_one_sum, gain_two_sum, bias_two_sum, bias_up_sum, bias_down_sum,
    ) = results(
        layer_out, noise_grad, table_grad, w_in_grad, qkv_grad, w_out_grad, w_up_grad, w_down_grad,
        sides_grad, alone_grad, width, bias_up.shape[0] // dp_size,
    )
    return (
        layer, noise, table, w_in_sum, gain_one_sum, bias_one_sum, query_sum, key_sum, value_sum, w_out_sum,
        gain_two_sum, bias_two_sum, w_up_sum, bias_up_sum, w_down_sum, bias_down_sum,
    )


def solution(mesh):
    placed = (
        P("dp"),
        P("dp", None),
        P("dp"),
        P("dp", None),
        P("mp", None),
        P(),
        P(),
        P(),
        P(None, "mp"),
        P(None, "mp"),
        P(None, "mp"),
        P("mp", None),
        P(),
        P(),
        P(None, "mp"),
        P("mp"),
        P("mp", None),
        P(),
        P("dp", None),
    )
    return jax.shard_map(
        on_device,
        mesh=mesh,
        in_specs=placed,
        out_specs=(
            P("dp", None),
            P("dp", None),
            P(("mp", "dp"), None),
            P("dp", None),
            P("dp"),
            P("dp"),
            P("dp", "mp"),
            P("dp", "mp"),
            P("dp", "mp"),
            P(("mp", "dp"), None),
            P("dp"),
            P("dp"),
            P("dp", "mp"),
            P(("mp", "dp")),
            P(("mp", "dp"), None),
            P("dp"),
        ),
        check_vma=False,
    )
```
